128 devices in a mesh: dp: 8 (over x, y_lo), tensor: 16 (over y_hi, z, core).
Axes of the slice: x: 4, y: 4 (y_hi: 2, y_lo: 2; y = y_hi * 2 + y_lo), z: 4, core: 2. Of those that a mesh axis runs over, the one named last changes fastest.
Arguments:
- token_ids: int32 [512, 2], P('dp'), may hold values from 0 to 65535
- embed_table: bfloat16 [65536, 4096], P(('dp', 'tensor')), may hold values from -77 to 77
- in_gain: float32 [4096], replicated, may hold values from 0.25 to 1.75
- in_weight: bfloat16 [4096, 12288], P(None, 'tensor'), may hold values from -0.09375 to 0.09375
- dt_weight: bfloat16 [4096, 32], P(None, 'tensor'), may hold values from -0.09375 to 0.09375
- dt_bias: float32 [32], P('tensor'), may hold values from -2.5 to 0.5
- a_log: float32 [32], P('tensor'), may hold values from -2 to 1.5
- d_skip: float32 [32], P('tensor'), may hold values from 0.5 to 2
- norm_gain: float32 [4096], P('tensor'), may hold values from 0.25 to 1.75
- out_weight: bfloat16 [4096, 4096], P('tensor'), may hold values from -0.125 to 0.125
- next_gain: float32 [4096], replicated, may hold values from 0.25 to 1.75
- ssm_state: float32 [512, 32, 128, 64], P('dp', 'tensor'), may hold values from -4 to 4
- trainer_weight: float32 [4096, 4096], P(('dp', 'tensor')), may hold values from -0.09375 to 0.09375
- head_map: int32 [32, 128], P('tensor'), may hold values from 0 to 127, each once within a row
Outputs:
- new_state: float32 [512, 32, 128, 64], P('dp', 'tensor')
- stream: bfloat16 [512, 2, 4096], P('dp', None, 'tensor')
- normed: bfloat16 [512, 2, 4096], P('dp')
- relaid: float32 [4096, 4096], P('tensor')
The draws below stay inside these ranges and needn't reach their ends.
Inputs may be any that keep to these rules, and one draw needn't show every extreme that they name: `token_ids`: token ids of the vocabulary of 65536 entries. `head_map`: each row is a permutation of the positions of a head.
All inputs are finite; a program needn't handle non-finite values.
Results may differ from the reference program's by a relative error of at most 0.0066.
Values may be sent and summed in bfloat16 or wider, within the bound.
A program may use at most 128 MiB of HBM per device.

```python
import math
import jax
import jax.numpy as jnp
import numpy as np
from jax import lax

D = 4096
HEADS = 32
HEAD = 128
STATE = 64
STEPS = 2
INNER = 4096
ROWS = 512
VOCAB = 65536


def draw_embed_table(key, part):
    key = jax.random.fold_in(key, 11)
    row_key, col_key, value_key = jax.random.split(key, 3)
    row_scale = jnp.exp(jax.random.uniform(row_key, (VOCAB, 1), jnp.float32, -1.2, 1.2))
    col_scale = jnp.exp(jax.random.uniform(col_key, (1, D), jnp.float32, -1.2, 1.2))
    position = jnp.arange(D, dtype=jnp.float32)[None, :] / float(max(D - 1, 1))
    ramp_up = jnp.sqrt(1.0 + 2.0 * position)
    values = jax.random.truncated_normal(value_key, -4.0, 4.0, (VOCAB, D), jnp.float32)
    return (values * row_scale * col_scale * ramp_up).astype(jnp.bfloat16)


def set_ends(drawn, own_key, least, top_value):
    shape = drawn.shape
    place = [jax.random.randint(jax.random.fold_in(own_key, axis), (), 0, shape[axis]) for axis in range(len(shape))]
    drawn = drawn.at[tuple(place)].set(least)
    longest = shape.index(max(shape))
    place[longest] = (place[longest] + 1) % shape[longest]
    return drawn.at[tuple(place)].set(top_value)


def with_spikes(values, stream_key, source, target, blocks, factor):
    def block_of(dim):
        return (jnp.arange(values.shape[dim]) // (values.shape[dim] // blocks)).reshape((-1,) + (1,) * (values.ndim - 1 - dim))

    first = jax.random.permutation(stream_key, blocks)[block_of(target)]
    far = (block_of(target) + blocks // 2) % blocks
    return jnp.where((block_of(source) == first) | (block_of(source) == far), factor * values, values)


def steps_of(own_key, shape, cuts, low, top_value):
    def one(dim, blocks):
        steps = jax.random.uniform(jax.random.fold_in(jax.random.fold_in(own_key, 6), dim), (blocks,), jnp.float32, low / len(cuts), top_value / len(cuts))
        return jnp.repeat(jnp.exp(steps), shape[dim] // blocks).reshape((-1,) + (1,) * (len(shape) - dim - 1))

    loudness = one(*cuts[0])
    for cut in cuts[1:]:
        loudness = loudness * one(*cut)
    return loudness


def rank_bounds(number_of, skew):
    portions = [(1 << 20) // math.isqrt(rank ** skew) + 1 for rank in range(1, number_of + 1)]
    width = 1 + sum(portions) // (1 << 30)
    return np.cumsum(np.array([max(1, weight // width) for weight in portions]))


def ranked_ids(stream_key, shape, amount, slope):
    grid = rank_bounds(amount, slope)
    pick = jax.random.randint(jax.random.fold_in(stream_key, 1), shape, 0, int(grid[amount - 1]))
    standing = jnp.searchsorted(jnp.asarray(grid, jnp.int32), pick, side="right")
    return jax.random.permutation(jax.random.fold_in(stream_key, 2), amount)[standing].astype(jnp.int32)


def bell_draw(rng, shape, spread, most, shards=(), kind=jnp.bfloat16):
    array = spread * jax.random.normal(rng, shape, jnp.float32)
    if shards:
        array = array * steps_of(rng, shape, shards, -0.22, 0.18)
    return jnp.clip(array, -most, most).astype(kind)


def noise_with(stream_key, extent, spread, most, shards, heavy, kind=jnp.bfloat16):
    result = spread * jax.random.normal(stream_key, extent, jnp.float32)
    if shards:
        result = result * steps_of(stream_key, extent, shards, -0.22, 0.18)
    return jnp.clip(with_spikes(result, jax.random.fold_in(stream_key, 3), *heavy), -most, most).astype(kind)


def setup_inputs(seed: int = 0) -> dict:
    arg_keys = jax.random.split(jax.random.key(seed), 15)
    token_ids = set_ends(ranked_ids(arg_keys[0], (ROWS, STEPS), VOCAB, 2), jax.random.fold_in(arg_keys[0], 3), 0, VOCAB - 1).astype(jnp.int32)
    embed_table = draw_embed_table(jax.random.fold_in(arg_keys[14], 71), 0)
    in_gain = jnp.clip(jax.random.uniform(arg_keys[2], (D,), jnp.float32, 0.25, 1.75), 0.25, 1.75)
    in_weight = bell_draw(arg_keys[3], (D, HEADS * (2 * HEAD + 2 * STATE)), D ** -0.5, 0.09375, ((1, 16),))
    dt_weight = bell_draw(arg_keys[4], (D, HEADS), D ** -0.5, 0.09375, ((1, 16),))
    dt_bias = jnp.clip(-2.5 + 3.0 * jax.random.uniform(arg_keys[5], (HEADS,), jnp.float32) ** steps_of(arg_keys[5], (HEADS,), ((0, 16),), -0.2, 0.2), -2.5, 0.5)
    a_log = jnp.clip(-2.0 + 3.5 * jax.random.uniform(arg_keys[6], (HEADS,), jnp.float32) ** steps_of(arg_keys[6], (HEADS,), ((0, 16),), -0.2, 0.2), -2.0, 1.5)
    d_skip = jnp.clip(0.5 + 1.5 * jax.random.uniform(arg_keys[7], (HEADS,), jnp.float32) ** steps_of(arg_keys[7], (HEADS,), ((0, 16),), -0.2, 0.2), 0.5, 2.0)
    norm_gain = jnp.clip(0.25 + 1.5 * jax.random.uniform(arg_keys[8], (INNER,), jnp.float32) ** steps_of(arg_keys[8], (INNER,), ((0, 16),), -0.2, 0.2), 0.25, 1.75)
    out_weight = noise_with(arg_keys[9], (INNER, D), INNER ** -0.5, 0.125, ((0, 16),), (0, 1, 16, 2.0))
    next_gain = jnp.clip(jax.random.uniform(arg_keys[10], (D,), jnp.float32, 0.25, 1.75), 0.25, 1.75)
    ssm_state = bell_draw(arg_keys[11], (ROWS, HEADS, HEAD, STATE), 0.5, 4.0, ((0, 8), (1, 16)), jnp.float32)
    trainer_weight = bell_draw(arg_keys[12], (D, INNER), INNER ** -0.5, 0.09375, ((0, 128),), jnp.float32)
    head_map = jax.vmap(lambda own: jax.random.permutation(own, HEAD))(jax.random.split(arg_keys[13], HEADS)).reshape((HEADS, HEAD)).astype(jnp.int32)
    return {"token_ids": token_ids, "embed_table": embed_table, "in_gain": in_gain, "in_weight": in_weight, "dt_weight": dt_weight, "dt_bias": dt_bias, "a_log": a_log, "d_skip": d_skip, "norm_gain": norm_gain, "out_weight": out_weight, "next_gain": next_gain, "ssm_state": ssm_state, "trainer_weight": trainer_weight, "head_map": head_map}


epsilon = 1e-05

def rms_scale(values, gain_row):
    mean_sq = lax.optimization_barrier(jnp.mean(values * values, axis=-1, keepdims=True))
    return values * lax.rsqrt(mean_sq + epsilon) * gain_row

def reference(token_ids, embed_table, in_gain, in_weight, dt_weight, dt_bias, a_log, d_skip, norm_gain, out_weight, next_gain, ssm_state, trainer_weight, head_map):
    embedded = jnp.take(embed_table, token_ids.reshape(-1).astype(jnp.int32), axis=0)
    embedded_wide = embedded.astype(jnp.float32)
    normed_in = rms_scale(embedded_wide, in_gain).astype(jnp.bfloat16)
    projected = jnp.dot(normed_in, in_weight, preferred_element_type=jnp.float32)
    projected = projected.reshape(ROWS, STEPS, HEADS, 2 * HEAD + 2 * STATE)
    head_input = projected[..., :HEAD]
    head_gate = projected[..., HEAD:2 * HEAD]
    write_key = projected[..., 2 * HEAD:2 * HEAD + STATE]
    read_query = projected[..., 2 * HEAD + STATE:]
    step_size = jax.nn.softplus(jnp.dot(normed_in, dt_weight, preferred_element_type=jnp.float32) + dt_bias)
    step_size = step_size.reshape(ROWS, STEPS, HEADS)
    decay_rate = jnp.exp(-step_size * jnp.exp(a_log))
    ssm_now = ssm_state
    outputs = []
    for step_idx in range(STEPS):
        scaled_input = step_size[:, step_idx, :, None] * head_input[:, step_idx]
        inject = scaled_input[..., None] * write_key[:, step_idx, :, None, :]
        ssm_now = decay_rate[:, step_idx, :, None, None] * ssm_now + inject
        readout = jnp.einsum('rhin,rhn->rhi', ssm_now, read_query[:, step_idx], precision=lax.Precision.HIGHEST)
        outputs.append(readout + d_skip[None, :, None] * head_input[:, step_idx])
    mixer_out = jnp.stack(outputs, axis=1)
    gated_out = mixer_out * jax.nn.silu(head_gate)
    mixed_out = rms_scale(gated_out, norm_gain.reshape(HEADS, HEAD)).astype(jnp.bfloat16)
    branch = jnp.dot(mixed_out.reshape(ROWS * STEPS, HEADS * HEAD), out_weight, preferred_element_type=jnp.float32)
    stream = (embedded_wide + branch).astype(jnp.bfloat16)
    normed = rms_scale(stream.astype(jnp.float32), next_gain).astype(jnp.bfloat16)
    row_index = (jnp.arange(HEADS, dtype=jnp.int32)[:, None] * HEAD + head_map.astype(jnp.int32)).reshape(-1)
    relaid = jnp.take(trainer_weight.T, row_index, axis=0)
    return (ssm_now, stream.reshape(ROWS, STEPS, D), normed.reshape(ROWS, STEPS, D), relaid)
```

```python
import functools
import jax
import jax.numpy as jnp
from jax import lax
from jax.experimental import pallas as pl
from jax.experimental.pallas import tpu as pltpu
from jax.sharding import PartitionSpec as P

epsilon = 1e-05
MESH = pl.DeviceIdType.MESH
SLOTS = 8
Z = 4
X = 4


def remote(src, dst, send_sem, recv_sem, **place):
    return pltpu.make_async_remote_copy(
        src_ref=src,
        dst_ref=dst,
        send_sem=send_sem,
        recv_sem=recv_sem,
        device_id=place,
        device_id_type=MESH,
    )


def greet(places):
    barrier = pltpu.get_barrier_semaphore()
    for place in places:
        pl.semaphore_signal(barrier, inc=1, device_id=place, device_id_type=MESH)
    pl.semaphore_wait(barrier, len(places))


def tensor_near(t):
    y, z, c = t // (2 * Z), lax.rem(t // 2, Z), lax.rem(t, 2)
    ahead = [lax.rem(z + o, Z) for o in range(1, Z)]
    behind = [lax.rem(z + Z - o, Z) for o in range(1, Z)]
    place = lambda yy, zz, cc: yy * (2 * Z) + zz * 2 + cc
    return y, z, c, ahead, behind, place


def gather_blocks(buf, t, send, recv):
    y, z, c, ahead, behind, place = tensor_near(t)
    other, across = place(y, z, 1 - c), place(1 - y, z, c)

    def go(block, role, to):
        copy = remote(buf.at[block], buf.at[block], send.at[role], recv.at[role], tensor=to)
        copy.start()
        return copy

    to_across = go(t, 1, across)
    to_z = [go(t, 2 + o, place(y, ahead[o], c)) for o in range(Z - 1)]
    to_core = [go(t, 0, other)]
    to_across.wait_recv()
    passed = [go(across, 5 + o, place(y, ahead[o], c)) for o in range(Z - 1)]
    to_core.append(go(across, 8, other))
    for o in range(Z - 1):
        to_z[o].wait_recv()
        to_core.append(go(place(y, behind[o], c), 9 + o, other))
    for o in range(Z - 1):
        passed[o].wait_recv()
        to_core.append(go(place(1 - y, behind[o], c), 12 + o, other))
    for copy in to_core:
        copy.wait_recv()
    for copy in [to_across] + to_z + passed + to_core:
        copy.wait_send()


def lookup_kernel(first, *refs):
    if first:
        (ids_ref, table_hbm, trainer_hbm, emb, need_ref, swapped, *rest) = refs
        (trainer, swap_out, swap_send, swap_recv, *rest) = rest
    else:
        (ids_ref, start_ref, table_hbm, emb, *rest) = refs
    (table, all_ids, out_d, in_d, out_t, in_t, local, ids_send, ids_recv, d_send, d_recv, t_send, t_recv,
     g_send, g_recv) = rest
    groups, holders = in_d.shape[0], in_t.shape[0]
    rows, vocab, width = ids_ref.shape[1], table.shape[0], table.shape[1]
    block = width // holders
    half = width // 2
    g, t = lax.axis_index("dp"), lax.axis_index("tensor")
    load = pltpu.make_async_copy(table_hbm, table, local.at[0])
    load.start()
    if first:
        load_trainer = pltpu.make_async_copy(trainer_hbm, trainer, local.at[1])
        load_trainer.start()
    all_ids[g] = jnp.broadcast_to(ids_ref[...], (8, rows))
    others_d = [lax.rem(g + o, groups) for o in range(1, groups)]
    others_t = [lax.rem(t + o, holders) for o in range(1, holders)]
    greet([{"dp": d} for d in others_d] + [{"tensor": d} for d in others_t])
    moves = []
    for o, d in enumerate(others_d):
        moves.append(remote(all_ids.at[g], all_ids.at[g], ids_send.at[o], ids_recv.at[o], dp=d))
        moves[-1].start()

    swaps = []
    if first:
        load_trainer.wait()
        for o in range(holders):
            swap_out[o] = trainer[:, o * block : (o + 1) * block].astype(jnp.bfloat16)
        for o, d in enumerate(others_t):
            swaps.append(remote(swap_out.at[d], swapped.at[t], swap_send.at[o], swap_recv.at[o], tensor=d))
            swaps[-1].start()
        swapped[t] = swap_out[t]

    start = 0 if first else start_ref[0:1, 0:1]
    row = ids_ref[...]
    column = jnp.broadcast_to(row, (8, rows)).astype(jnp.float32).T.astype(jnp.int32)[:, 0:1]
    at0 = lax.broadcasted_iota(jnp.int32, (rows, rows), 0)
    at1 = lax.broadcasted_iota(jnp.int32, (rows, rows), 1)

    def order(row, column):
        again = jnp.where((column == row) & (at0 < at1), 1.0, 0.0)
        once = 1.0 - jnp.max(again, axis=0, keepdims=True)
        floor = column - lax.rem(column, vocab)
        before = jnp.where((row >= floor) & (row < column), once, 0.0)
        return jnp.sum(before, axis=1, keepdims=True).astype(jnp.int32)

    slot = order(row, column) - start
    holder = column // vocab
    from_t, from_g = lax.rem(holder, holders), holder // holders
    want = jnp.where((slot >= 0) & (slot < SLOTS), (from_t * groups + from_g) * SLOTS + slot, -1)
    candidates = holders * groups * SLOTS

    for copy in moves:
        copy.wait()

    ids_all = all_ids[0]
    at_g = lax.broadcasted_iota(jnp.int32, (8, rows), 0)
    for gg in range(1, groups):
        ids_all = jnp.where(at_g == gg, all_ids[gg], ids_all)
    columns = ids_all.astype(jnp.float32).T.astype(jnp.int32)
    base = (g * holders + t) * vocab
    at_v = lax.broadcasted_iota(jnp.int32, (rows, vocab), 1)
    pick_g = lax.broadcasted_iota(jnp.int32, (16, vocab), 0)
    held = jnp.zeros((16, vocab), jnp.float32)
    for gg in range(groups):
        asked = jnp.where(columns[:, gg : gg + 1] - base == at_v, 1.0, 0.0)
        held = jnp.where(pick_g == gg, jnp.max(asked, axis=0, keepdims=True), held)
    lower = jnp.where(
        lax.broadcasted_iota(jnp.int32, (vocab, vocab), 0) < lax.broadcasted_iota(jnp.int32, (vocab, vocab), 1),
        1.0,
        0.0,
    ).astype(jnp.bfloat16)
    rank = jnp.dot(held.astype(jnp.bfloat16), lower, preferred_element_type=jnp.float32).astype(jnp.int32) - start
    at_c = lax.broadcasted_iota(jnp.int32, (SLOTS, vocab), 0)
    chosen = jnp.concatenate(
        [
            jnp.where((rank[gg : gg + 1] == at_c) & (held[gg : gg + 1] > 0.5), 1.0, 0.0)
            for gg in range(groups)
        ],
        axis=0,
    ).astype(jnp.bfloat16)
    load.wait()
    step = 512
    for at in range(0, half, step):
        low = jnp.dot(chosen, table[:, at : at + step], preferred_element_type=jnp.float32)
        high = jnp.dot(chosen, table[:, half + at : half + at + step], preferred_element_type=jnp.float32)
        both = jnp.concatenate(
            [low.reshape(groups, SLOTS, step), high.reshape(groups, SLOTS, step)], axis=1
        )
        out_d[:, :, at : at + step] = both.astype(jnp.bfloat16)
    sent = []
    for o, d in enumerate(others_d):
        sent.append(remote(out_d.at[d], in_d.at[g], d_send.at[o], d_recv.at[o], dp=d))
        sent[-1].start()
    in_d[g] = out_d[g]
    if first:
        most = jnp.zeros((1, 1), jnp.int32)
        for gg in range(groups):
            most = jnp.maximum(
                most, jnp.max(order(all_ids[gg][0:1], columns[:, gg : gg + 1]), axis=0, keepdims=True)
            )
        need_ref[...] = jnp.broadcast_to(most + 1, need_ref.shape)
    select = jnp.where(
        want == lax.broadcasted_iota(jnp.int32, (rows, candidates), 1), 1.0, 0.0
    ).astype(jnp.bfloat16)
    for copy in sent:
        copy.wait()
    for o in range(holders):
        part, at = o // (holders // 2), (o % (holders // 2)) * block
        piece = in_d[:, :, at : at + block].astype(jnp.float32)[:, part * SLOTS : (part + 1) * SLOTS]
        out_t[o] = piece.reshape(groups * SLOTS, block).astype(jnp.bfloat16)
    sent = []
    for o, d in enumerate(others_t):
        sent.append(remote(out_t.at[d], in_t.at[t], t_send.at[o], t_recv.at[o], tensor=d))
        sent[-1].start()
    in_t[t] = out_t[t]
    for copy in sent:
        copy.wait()
    found = jnp.dot(select, in_t[...].reshape(candidates, block), preferred_element_type=jnp.float32)
    emb[t] = found.astype(jnp.bfloat16)
    gather_blocks(emb, t, g_send, g_recv)
    for copy in swaps:
        copy.wait()


def lookup(ids, table, groups, holders, trainer=None, start=None):
    first = start is None
    rows = ids.shape[1]
    vocab, width = table.shape
    block = width // holders
    bf16, dma = jnp.bfloat16, pltpu.SemaphoreType.DMA
    vmem, anywhere = pl.BlockSpec(memory_space=pltpu.VMEM), pl.BlockSpec(memory_space=pl.ANY)
    emb_shape = jax.ShapeDtypeStruct((holders, rows, block), bf16)
    scratch = [
        pltpu.VMEM((vocab, width), bf16),
        pltpu.VMEM((groups, 8, rows), jnp.int32),
        pltpu.VMEM((groups, 2 * SLOTS, width // 2), bf16),
        pltpu.VMEM((groups, 2 * SLOTS, width // 2), bf16),
        pltpu.VMEM((holders, groups * SLOTS, block), bf16),
        pltpu.VMEM((holders, groups * SLOTS, block), bf16),
        dma((2,)),
        dma((groups - 1,)),
        dma((groups - 1,)),
        dma((groups - 1,)),
        dma((groups - 1,)),
        dma((holders - 1,)),
        dma((holders - 1,)),
        dma((holders - 1,)),
        dma((holders - 1,)),
    ]
    if first:
        trows = trainer.shape[0]
        args, in_specs = (ids, table, trainer), [vmem, anywhere, anywhere]
        out_shape = (
            emb_shape,
            jax.ShapeDtypeStruct((8, 128), jnp.int32),
            jax.ShapeDtypeStruct((holders, trows, block), bf16),
        )
        scratch = [
            pltpu.VMEM(trainer.shape, jnp.float32),
            pltpu.VMEM((holders, trows, block), bf16),
            dma((holders - 1,)),
            dma((holders - 1,)),
        ] + scratch
    else:
        args, in_specs = (ids, start, table), [vmem, vmem, anywhere]
        out_shape = (emb_shape,)
    return pl.pallas_call(
        functools.partial(lookup_kernel, first),
        out_shape=out_shape,
        in_specs=in_specs,
        out_specs=tuple(vmem for _ in out_shape),
        scratch_shapes=scratch,
        compiler_params=pltpu.CompilerParams(
            collective_id=0 if first else 1, has_side_effects=True, vmem_limit_bytes=40 * 2**20
        ),
        name="lookup_first" if first else "lookup_more",
    )(*args)


def project_kernel(mixed, weight_hbm, emb, swapped_hbm, stream, whole, gathered, weight, out_c, in_c, kept, out_z, in_z,
                   slab, out_y, in_y, local, c_send, c_recv, z_send, z_recv, y_send, y_recv, g_send, g_recv, x_send,
                   x_recv):
    g, t = lax.axis_index("dp"), lax.axis_index("tensor")
    block = whole.shape[2]
    load = pltpu.make_async_copy(weight_hbm, weight, local.at[0])
    load.start()
    own = pltpu.make_async_copy(swapped_hbm, gathered.at[g], local.at[1])
    own.start()
    y, z, c, ahead, behind, place = tensor_near(t)
    x, low = g // 2, lax.rem(g, 2)
    beside = x * 2 + 1 - low
    x_ahead = [lax.rem(x + o, X) * 2 + low for o in range(1, X)]
    other, across = place(y, z, 1 - c), place(1 - y, z, c)
    greet(
        [{"tensor": other}, {"tensor": across}, {"dp": beside}]
        + [{"tensor": place(y, zz, c)} for zz in ahead]
        + [{"dp": d} for d in x_ahead]
    )

    def share(block, role, to):
        copy = remote(gathered.at[block], gathered.at[block], x_send.at[role], x_recv.at[role], dp=to)
        copy.start()
        return copy

    load.wait()
    rows_in = mixed[...]

    def partial_of(k, cc):
        at = place(k % 2, k // 2, cc) * block
        return jnp.dot(rows_in, weight[:, pl.ds(pl.multiple_of(at, block), block)], preferred_element_type=jnp.float32)

    to_core = []
    for k in range(2 * Z):
        out_c[k] = partial_of(k, 1 - c).astype(jnp.bfloat16)
        to_core.append(remote(out_c.at[k], in_c.at[k], c_send.at[k], c_recv.at[k], tensor=other))
        to_core[-1].start()
    own.wait()
    to_beside = share(g, 0, beside)
    to_x = [share(g, 1 + o, x_ahead[o]) for o in range(X - 1)]
    for k in range(2 * Z):
        kept[k // 2, k % 2] = partial_of(k, c)
    for k in range(2 * Z):
        to_core[k].wait_recv()
        total = kept[k // 2, k % 2] + in_c[k].astype(jnp.float32)
        kept[k // 2, k % 2] = total
        out_z[k // 2, k % 2] = total.astype(jnp.bfloat16)
    to_z = []
    for o in range(Z - 1):
        to_z.append(
            remote(out_z.at[ahead[o]], in_z.at[o], z_send.at[o], z_recv.at[o], tensor=place(y, ahead[o], c))
        )
        to_z[-1].start()
    to_beside.wait_recv()
    passed = [share(beside, X + o, x_ahead[o]) for o in range(X - 1)]
    total = kept[z]
    for o in range(Z - 1):
        to_z[o].wait_recv()
        total = total + in_z[o].astype(jnp.float32)
    slab[...] = total
    out_y[...] = slab[1 - y].astype(jnp.bfloat16)
    to_y = remote(out_y, in_y, y_send.at[0], y_recv.at[0], tensor=across)
    to_y.start()
    to_y.wait_recv()
    branch = slab[y] + in_y[...].astype(jnp.float32)
    mine = (emb[t].astype(jnp.float32) + branch).astype(jnp.bfloat16)
    stream[...] = mine
    whole[t] = mine
    gather_blocks(whole, t, g_send, g_recv)
    for copy in to_x + passed:
        copy.wait_recv()
    for copy in to_core + to_z + [to_y, to_beside] + to_x + passed:
        copy.wait_send()


def project(mixed, weight, emb, swapped, groups):
    holders, rows, block = emb.shape
    bf16, f32, dma = jnp.bfloat16, jnp.float32, pltpu.SemaphoreType.DMA
    vmem, anywhere = pl.BlockSpec(memory_space=pltpu.VMEM), pl.BlockSpec(memory_space=pl.ANY)
    return pl.pallas_call(
        project_kernel,
        out_shape=(
            jax.ShapeDtypeStruct((rows, block), bf16),
            jax.ShapeDtypeStruct((holders, rows, block), bf16),
            jax.ShapeDtypeStruct((groups,) + swapped.shape, bf16),
        ),
        in_specs=[vmem, anywhere, vmem, anywhere],
        out_specs=(vmem, vmem, vmem),
        scratch_shapes=[
            pltpu.VMEM(weight.shape, bf16),
            pltpu.VMEM((2 * Z, rows, block), bf16),
            pltpu.VMEM((2 * Z, rows, block), bf16),
            pltpu.VMEM((Z, 2, rows, block), f32),
            pltpu.VMEM((Z, 2, rows, block), bf16),
            pltpu.VMEM((Z - 1, 2, rows, block), bf16),
            pltpu.VMEM((2, rows, block), f32),
            pltpu.VMEM((rows, block), bf16),
            pltpu.VMEM((rows, block), bf16),
            dma((2,)),
            dma((2 * Z,)),
            dma((2 * Z,)),
            dma((Z - 1,)),
            dma((Z - 1,)),
            dma((1,)),
            dma((1,)),
            dma((holders - 1,)),
            dma((holders - 1,)),
            dma((2 * X - 1,)),
            dma((2 * X - 1,)),
        ],
        compiler_params=pltpu.CompilerParams(
            collective_id=2, has_side_effects=True, vmem_limit_bytes=40 * 2**20
        ),
        name="project",
    )(mixed, weight, emb, swapped)


def per_device(
    token_ids,
    embed_table,
    in_gain,
    in_weight,
    dt_weight,
    dt_bias,
    a_log,
    d_skip,
    norm_gain,
    out_weight,
    next_gain,
    ssm_state,
    trainer_weight,
    head_map,
):
    row_count, step_count = token_ids.shape
    model_width = embed_table.shape[1]
    heads_local = dt_weight.shape[1]
    head_size, state_size = ssm_state.shape[2], ssm_state.shape[3]
    holders = lax.axis_size("tensor")
    groups = lax.axis_size("dp")
    rows = row_count * step_count

    ids = token_ids.T.reshape(1, rows)
    emb, need, swapped = lookup(ids, embed_table, groups, holders, trainer=trainer_weight)

    def more(carry):
        done, held = carry
        start = jnp.full((8, 128), done, jnp.int32)
        (found,) = lookup(ids, embed_table, groups, holders, start=start)
        return done + SLOTS, held + found

    _, emb = lax.while_loop(lambda carry: carry[0] < need[0, 0], more, (jnp.int32(SLOTS), emb))

    embedded_wide = emb.transpose(1, 0, 2).reshape(rows, model_width).astype(jnp.float32)
    mean_sq = jnp.mean(embedded_wide * embedded_wide, axis=-1, keepdims=True)
    normed_in = (embedded_wide * lax.rsqrt(mean_sq + epsilon) * in_gain).astype(jnp.bfloat16)
    projected = jnp.dot(normed_in, in_weight, preferred_element_type=jnp.float32)
    projected = projected.reshape(step_count, row_count, heads_local, 2 * head_size + 2 * state_size)
    head_input = projected[..., :head_size]
    head_gate = projected[..., head_size : 2 * head_size]
    write_key = projected[..., 2 * head_size : 2 * head_size + state_size]
    read_query = projected[..., 2 * head_size + state_size :]
    step_size = jax.nn.softplus(jnp.dot(normed_in, dt_weight, preferred_element_type=jnp.float32) + dt_bias)
    step_size = step_size.reshape(step_count, row_count, heads_local)
    decay_rate = jnp.exp(-step_size * jnp.exp(a_log))
    ssm_now = ssm_state
    outputs = []
    for step_idx in range(step_count):
        scaled_input = step_size[step_idx, :, :, None] * head_input[step_idx]
        inject = scaled_input[..., None] * write_key[step_idx, :, :, None, :]
        ssm_now = decay_rate[step_idx, :, :, None, None] * ssm_now + inject
        readout = jnp.sum(ssm_now * read_query[step_idx, :, :, None, :], axis=-1)
        outputs.append(readout + d_skip[None, :, None] * head_input[step_idx])
    gated_out = jnp.stack(outputs, axis=0) * jax.nn.silu(head_gate)
    mean_sq = jnp.mean(gated_out * gated_out, axis=-1, keepdims=True)
    mixed_out = gated_out * lax.rsqrt(mean_sq + epsilon) * norm_gain.reshape(heads_local, head_size)
    mixed_out = mixed_out.astype(jnp.bfloat16).reshape(rows, heads_local * head_size)

    stream, whole, gathered = project(mixed_out, out_weight, emb, swapped, groups)
    wide = whole.astype(jnp.float32)
    mean_sq = jnp.sum(wide * wide, axis=(0, 2), keepdims=True) / model_width
    normed = wide * lax.rsqrt(mean_sq + epsilon) * next_gain.reshape(holders, 1, -1)
    normed = normed.astype(jnp.bfloat16).reshape(holders, step_count, row_count, -1)
    normed = normed.transpose(2, 1, 0, 3).reshape(row_count, step_count, model_width)
    stream = stream.reshape(step_count, row_count, -1).transpose(1, 0, 2)

    units = heads_local * head_size
    row_index = (lax.broadcasted_iota(jnp.int32, head_map.shape, 0) * head_size + head_map).reshape(-1)
    swap = (row_index[:, None] == lax.broadcasted_iota(jnp.int32, (1, units), 1)).astype(jnp.bfloat16)
    relaid = lax.dot_general(
        swap, gathered.reshape(model_width, units), (((1,), (1,)), ((), ())), preferred_element_type=jnp.float32
    )
    return ssm_now, stream, normed, relaid


def solution(mesh):
    placed = (
        P("dp", None),
        P(("dp", "tensor"), None),
        P(),
        P(None, "tensor"),
        P(None, "tensor"),
        P("tensor"),
        P("tensor"),
        P("tensor"),
        P("tensor"),
        P("tensor", None),
        P(),
        P("dp", "tensor", None, None),
        P(("dp", "tensor"), None),
        P("tensor", None),
    )
    return jax.shard_map(
        per_device,
        mesh=mesh,
        in_specs=placed,
        out_specs=(
            P("dp", "tensor", None, None),
            P("dp", None, "tensor"),
            P("dp", None, None),
            P("tensor", None),
        ),
        check_vma=False,
    )
```

```python
import functools
import jax
import jax.numpy as jnp
from jax import lax
from jax.experimental import pallas as pl
from jax.experimental.pallas import tpu as pltpu
from jax.sharding import PartitionSpec as P

epsilon = 1e-05
MESH = pl.DeviceIdType.MESH
SLOTS = 8
Z = 4
X = 4


def remote(src, dst, send_sem, recv_sem, **place):
    return pltpu.make_async_remote_copy(
        src_ref=src,
        dst_ref=dst,
        send_sem=send_sem,
        recv_sem=recv_sem,
        device_id=place,
        device_id_type=MESH,
    )


def greet(places):
    barrier = pltpu.get_barrier_semaphore()
    for place in places:
        pl.semaphore_signal(barrier, inc=1, device_id=place, device_id_type=MESH)
    pl.semaphore_wait(barrier, len(places))


def tensor_near(t):
    y, z, c = t // (2 * Z), lax.rem(t // 2, Z), lax.rem(t, 2)
    ahead = [lax.rem(z + o, Z) for o in range(1, Z)]
    behind = [lax.rem(z + Z - o, Z) for o in range(1, Z)]
    place = lambda yy, zz, cc: yy * (2 * Z) + zz * 2 + cc
    return y, z, c, ahead, behind, place


def gather_blocks(buf, t, send, recv):
    y, z, c, ahead, behind, place = tensor_near(t)
    other, across = place(y, z, 1 - c), place(1 - y, z, c)

    def go(block, role, to):
        copy = remote(buf.at[block], buf.at[block], send.at[role], recv.at[role], tensor=to)
        copy.start()
        return copy

    to_across = go(t, 1, across)
    to_z = [go(t, 2 + o, place(y, ahead[o], c)) for o in range(Z - 1)]
    to_core = [go(t, 0, other)]
    to_across.wait_recv()
    passed = [go(across, 5 + o, place(y, ahead[o], c)) for o in range(Z - 1)]
    to_core.append(go(across, 8, other))
    for o in range(Z - 1):
        to_z[o].wait_recv()
        to_core.append(go(place(y, behind[o], c), 9 + o, other))
    for o in range(Z - 1):
        passed[o].wait_recv()
        to_core.append(go(place(1 - y, behind[o], c), 12 + o, other))
    for copy in to_core:
        copy.wait_recv()
    for copy in [to_across] + to_z + passed + to_core:
        copy.wait_send()


def lookup_kernel(first, *refs):
    if first:
        (ids_ref, table_hbm, trainer_hbm, emb, need_ref, swapped, *rest) = refs
        (trainer, swap_out, swap_send, swap_recv, *rest) = rest
    else:
        (ids_ref, start_ref, table_hbm, emb, *rest) = refs
    (table, all_ids, out_d, in_d, out_t, in_t, local, ids_send, ids_recv, d_send, d_recv, t_send, t_recv,
     g_send, g_recv) = rest
    groups, holders = in_d.shape[0], in_t.shape[0]
    rows, vocab, width = ids_ref.shape[1], table.shape[0], table.shape[1]
    block = width // holders
    half = width // 2
    g, t = lax.axis_index("dp"), lax.axis_index("tensor")
    load = pltpu.make_async_copy(table_hbm, table, local.at[0])
    load.start()
    if first:
        load_trainer = pltpu.make_async_copy(trainer_hbm, trainer, local.at[1])
        load_trainer.start()
    all_ids[g] = jnp.broadcast_to(ids_ref[...], (8, rows))
    others_d = [lax.rem(g + o, groups) for o in range(1, groups)]
    others_t = [lax.rem(t + o, holders) for o in range(1, holders)]
    greet([{"dp": d} for d in others_d] + [{"tensor": d} for d in others_t])
    moves = []
    for o, d in enumerate(others_d):
        moves.append(remote(all_ids.at[g], all_ids.at[g], ids_send.at[o], ids_recv.at[o], dp=d))
        moves[-1].start()

    swaps = []
    if first:
        load_trainer.wait()
        for o in range(holders):
            swap_out[o] = trainer[:, o * block : (o + 1) * block].astype(jnp.bfloat16)
        for o, d in enumerate(others_t):
            swaps.append(remote(swap_out.at[d], swapped.at[t], swap_send.at[o], swap_recv.at[o], tensor=d))
            swaps[-1].start()
        swapped[t] = swap_out[t]

    start = 0 if first else start_ref[0:1, 0:1]
    row = ids_ref[...]
    column = jnp.broadcast_to(row, (8, rows)).astype(jnp.float32).T.astype(jnp.int32)[:, 0:1]
    at0 = lax.broadcasted_iota(jnp.int32, (rows, rows), 0)
    at1 = lax.broadcasted_iota(jnp.int32, (rows, rows), 1)

    def order(row, column):
        again = jnp.where((column == row) & (at0 < at1), 1.0, 0.0)
        once = 1.0 - jnp.max(again, axis=0, keepdims=True)
        floor = column - lax.rem(column, vocab)
        before = jnp.where((row >= floor) & (row < column), once, 0.0)
        return jnp.sum(before, axis=1, keepdims=True).astype(jnp.int32)

    slot = order(row, column) - start
    holder = column // vocab
    from_t, from_g = lax.rem(holder, holders), holder // holders
    want = jnp.where((slot >= 0) & (slot < SLOTS), (from_t * groups + from_g) * SLOTS + slot, -1)
    candidates = holders * groups * SLOTS

    for copy in moves:
        copy.wait()

    ids_all = all_ids[0]
    at_g = lax.broadcasted_iota(jnp.int32, (8, rows), 0)
    for gg in range(1, groups):
        ids_all = jnp.where(at_g == gg, all_ids[gg], ids_all)
    columns = ids_all.astype(jnp.float32).T.astype(jnp.int32)
    base = (g * holders + t) * vocab
    at_v = lax.broadcasted_iota(jnp.int32, (rows, vocab), 1)
    pick_g = lax.broadcasted_iota(jnp.int32, (16, vocab), 0)
    held = jnp.zeros((16, vocab), jnp.float32)
    for gg in range(groups):
        asked = jnp.where(columns[:, gg : gg + 1] - base == at_v, 1.0, 0.0)
        held = jnp.where(pick_g == gg, jnp.max(asked, axis=0, keepdims=True), held)
    lower = jnp.where(
        lax.broadcasted_iota(jnp.int32, (vocab, vocab), 0) < lax.broadcasted_iota(jnp.int32, (vocab, vocab), 1),
        1.0,
        0.0,
    ).astype(jnp.bfloat16)
    rank = jnp.dot(held.astype(jnp.bfloat16), lower, preferred_element_type=jnp.float32).astype(jnp.int32) - start
    at_c = lax.broadcasted_iota(jnp.int32, (SLOTS, vocab), 0)
    chosen = jnp.concatenate(
        [
            jnp.where((rank[gg : gg + 1] == at_c) & (held[gg : gg + 1] > 0.5), 1.0, 0.0)
            for gg in range(groups)
        ],
        axis=0,
    ).astype(jnp.bfloat16)
    load.wait()
    step = 512
    for at in range(0, half, step):
        low = jnp.dot(chosen, table[:, at : at + step], preferred_element_type=jnp.float32)
        high = jnp.dot(chosen, table[:, half + at : half + at + step], preferred_element_type=jnp.float32)
        both = jnp.concatenate(
            [low.reshape(groups, SLOTS, step), high.reshape(groups, SLOTS, step)], axis=1
        )
        out_d[:, :, at : at + step] = both.astype(jnp.bfloat16)
    sent = []
    for o, d in enumerate(others_d):
        sent.append(remote(out_d.at[d], in_d.at[g], d_send.at[o], d_recv.at[o], dp=d))
        sent[-1].start()
    in_d[g] = out_d[g]
    if first:
        most = jnp.zeros((1, 1), jnp.int32)
        for gg in range(groups):
            most = jnp.maximum(
                most, jnp.max(order(all_ids[gg][0:1], columns[:, gg : gg + 1]), axis=0, keepdims=True)
            )
        need_ref[...] = jnp.broadcast_to(most + 1, need_ref.shape)
    select = jnp.where(
        want == lax.broadcasted_iota(jnp.int32, (rows, candidates), 1), 1.0, 0.0
    ).astype(jnp.bfloat16)
    for copy in sent:
        copy.wait()
    for o in range(holders):
        part, at = o // (holders // 2), (o % (holders // 2)) * block
        piece = in_d[:, :, at : at + block].astype(jnp.float32)[:, part * SLOTS : (part + 1) * SLOTS]
        out_t[o] = piece.reshape(groups * SLOTS, block).astype(jnp.bfloat16)
    sent = []
    for o, d in enumerate(others_t):
        sent.append(remote(out_t.at[d], in_t.at[t], t_send.at[o], t_recv.at[o], tensor=d))
        sent[-1].start()
    in_t[t] = out_t[t]
    for copy in sent:
        copy.wait()
    found = jnp.dot(select, in_t[...].reshape(candidates, block), preferred_element_type=jnp.float32)
    emb[t] = found.astype(jnp.bfloat16)
    gather_blocks(emb, t, g_send, g_recv)
    for copy in swaps:
        copy.wait()


def lookup(ids, table, groups, holders, trainer=None, start=None):
    first = start is None
    rows = ids.shape[1]
    vocab, width = table.shape
    block = width // holders
    bf16, dma = jnp.bfloat16, pltpu.SemaphoreType.DMA
    vmem, anywhere = pl.BlockSpec(memory_space=pltpu.VMEM), pl.BlockSpec(memory_space=pl.ANY)
    emb_shape = jax.ShapeDtypeStruct((holders, rows, block), bf16)
    scratch = [
        pltpu.VMEM((vocab, width), bf16),
        pltpu.VMEM((groups, 8, rows), jnp.int32),
        pltpu.VMEM((groups, 2 * SLOTS, width // 2), bf16),
        pltpu.VMEM((groups, 2 * SLOTS, width // 2), bf16),
        pltpu.VMEM((holders, groups * SLOTS, block), bf16),
        pltpu.VMEM((holders, groups * SLOTS, block), bf16),
        dma((2,)),
        dma((groups - 1,)),
        dma((groups - 1,)),
        dma((groups - 1,)),
        dma((groups - 1,)),
        dma((holders - 1,)),
        dma((holders - 1,)),
        dma((holders - 1,)),
        dma((holders - 1,)),
    ]
    if first:
        trows = trainer.shape[0]
        args, in_specs = (ids, table, trainer), [vmem, anywhere, anywhere]
        out_shape = (
            emb_shape,
            jax.ShapeDtypeStruct((8, 128), jnp.int32),
            jax.ShapeDtypeStruct((holders, trows, block), bf16),
        )
        scratch = [
            pltpu.VMEM(trainer.shape, jnp.float32),
            pltpu.VMEM((holders, trows, block), bf16),
            dma((holders - 1,)),
            dma((holders - 1,)),
        ] + scratch
    else:
        args, in_specs = (ids, start, table), [vmem, vmem, anywhere]
        out_shape = (emb_shape,)
    return pl.pallas_call(
        functools.partial(lookup_kernel, first),
        out_shape=out_shape,
        in_specs=in_specs,
        out_specs=tuple(vmem for _ in out_shape),
        scratch_shapes=scratch,
        compiler_params=pltpu.CompilerParams(
            collective_id=0 if first else 1, has_side_effects=True, vmem_limit_bytes=40 * 2**20
        ),
        name="lookup_first" if first else "lookup_more",
    )(*args)


def project_kernel(mixed, weight_hbm, emb, swapped_hbm, stream, whole, gathered, weight, out_c, in_c, kept, out_z, in_z,
                   slab, out_y, in_y, local, c_send, c_recv, z_send, z_recv, y_send, y_recv, g_send, g_recv, x_send,
                   x_recv):
    g, t = lax.axis_index("dp"), lax.axis_index("tensor")
    block = whole.shape[2]
    load = pltpu.make_async_copy(weight_hbm, weight, local.at[0])
    load.start()
    own = pltpu.make_async_copy(swapped_hbm, gathered.at[g], local.at[1])
    own.start()
    y, z, c, ahead, behind, place = tensor_near(t)
    x, low = g // 2, lax.rem(g, 2)
    beside = x * 2 + 1 - low
    x_ahead = [lax.rem(x + o, X) * 2 + low for o in range(1, X)]
    other, across = place(y, z, 1 - c), place(1 - y, z, c)
    greet(
        [{"tensor": other}, {"tensor": across}, {"dp": beside}]
        + [{"tensor": place(y, zz, c)} for zz in ahead]
        + [{"dp": d} for d in x_ahead]
    )

    def share(block, role, to):
        copy = remote(gathered.at[block], gathered.at[block], x_send.at[role], x_recv.at[role], dp=to)
        copy.start()
        return copy

    load.wait()
    rows_in = mixed[...]

    def partial_of(k, cc):
        at = place(k % 2, k // 2, cc) * block
        return jnp.dot(rows_in, weight[:, pl.ds(pl.multiple_of(at, block), block)], preferred_element_type=jnp.float32)

    to_core = []
    for k in range(2 * Z):
        out_c[k] = partial_of(k, 1 - c).astype(jnp.bfloat16)
        to_core.append(remote(out_c.at[k], in_c.at[k], c_send.at[k], c_recv.at[k], tensor=other))
        to_core[-1].start()
    own.wait()
    to_beside = share(g, 0, beside)
    to_x = [share(g, 1 + o, x_ahead[o]) for o in range(X - 1)]
    for k in range(2 * Z):
        kept[k // 2, k % 2] = partial_of(k, c)
    for k in range(2 * Z):
        to_core[k].wait_recv()
        total = kept[k // 2, k % 2] + in_c[k].astype(jnp.float32)
        kept[k // 2, k % 2] = total
        out_z[k // 2, k % 2] = total.astype(jnp.bfloat16)
    to_z = []
    for o in range(Z - 1):
        to_z.append(
            remote(out_z.at[ahead[o]], in_z.at[o], z_send.at[o], z_recv.at[o], tensor=place(y, ahead[o], c))
        )
        to_z[-1].start()
    to_beside.wait_recv()
    passed = [share(beside, X + o, x_ahead[o]) for o in range(X - 1)]
    total = kept[z]
    for o in range(Z - 1):
        to_z[o].wait_recv()
        total = total + in_z[o].astype(jnp.float32)
    slab[...] = total
    out_y[...] = slab[1 - y].astype(jnp.bfloat16)
    to_y = remote(out_y, in_y, y_send.at[0], y_recv.at[0], tensor=across)
    to_y.start()
    to_y.wait_recv()
    branch = slab[y] + in_y[...].astype(jnp.float32)
    mine = (emb[t].astype(jnp.float32) + branch).astype(jnp.bfloat16)
    stream[...] = mine
    whole[t] = mine
    gather_blocks(whole, t, g_send, g_recv)
    for copy in to_x + passed:
        copy.wait_recv()
    for copy in to_core + to_z + [to_y, to_beside] + to_x + passed:
        copy.wait_send()


def project(mixed, weight, emb, swapped, groups):
    holders, rows, block = emb.shape
    bf16, f32, dma = jnp.bfloat16, jnp.float32, pltpu.SemaphoreType.DMA
    vmem, anywhere = pl.BlockSpec(memory_space=pltpu.VMEM), pl.BlockSpec(memory_space=pl.ANY)
    return pl.pallas_call(
        project_kernel,
        out_shape=(
            jax.ShapeDtypeStruct((rows, block), bf16),
            jax.ShapeDtypeStruct((holders, rows, block), bf16),
            jax.ShapeDtypeStruct((groups,) + swapped.shape, bf16),
        ),
        in_specs=[vmem, anywhere, vmem, anywhere],
        out_specs=(vmem, vmem, vmem),
        scratch_shapes=[
            pltpu.VMEM(weight.shape, bf16),
            pltpu.VMEM((2 * Z, rows, block), bf16),
            pltpu.VMEM((2 * Z, rows, block), bf16),
            pltpu.VMEM((Z, 2, rows, block), f32),
            pltpu.VMEM((Z, 2, rows, block), bf16),
            pltpu.VMEM((Z - 1, 2, rows, block), bf16),
            pltpu.VMEM((2, rows, block), f32),
            pltpu.VMEM((rows, block), bf16),
            pltpu.VMEM((rows, block), bf16),
            dma((2,)),
            dma((2 * Z,)),
            dma((2 * Z,)),
            dma((Z - 1,)),
            dma((Z - 1,)),
            dma((1,)),
            dma((1,)),
            dma((holders - 1,)),
            dma((holders - 1,)),
            dma((2 * X - 1,)),
            dma((2 * X - 1,)),
        ],
        compiler_params=pltpu.CompilerParams(
            collective_id=2, has_side_effects=True, vmem_limit_bytes=40 * 2**20
        ),
        name="project",
    )(mixed, weight, emb, swapped)


def mixer_kernel(heads, emb, gain, weight_hbm, dtw, scalars, ngain, state_hbm, new_hbm, mixed, weight, state, nrm, proj,
                 kq, xin, xrow, decay, read, w_sem, s_sem, n_sem):
    holders, rows, block = emb.shape
    row_count, _, state_size, head_size = state.shape
    columns = weight.shape[1] // heads
    steps = rows // row_count
    parts = w_sem.shape[0]
    depth = weight.shape[0] // parts
    chunks = s_sem.shape[0]
    per = row_count // chunks
    loads = []
    for p in range(parts):
        at = pl.ds(p * depth, depth)
        loads.append(pltpu.make_async_copy(weight_hbm.at[at], weight.at[at], w_sem.at[p]))
        loads[-1].start()
    for p in range(chunks):
        at = pl.ds(p * per, per)
        pltpu.make_async_copy(state_hbm.at[at], state.at[at], s_sem.at[p]).start()

    squares = jnp.zeros((rows, block), jnp.float32)
    for k in range(holders):
        wide = emb[k].astype(jnp.float32)
        squares = squares + wide * wide
    scale = lax.rsqrt(jnp.sum(squares, axis=1, keepdims=True) / (holders * block) + epsilon)
    for k in range(holders):
        nrm[:, k * block : (k + 1) * block] = (emb[k].astype(jnp.float32) * scale * gain[k : k + 1]).astype(jnp.bfloat16)
    narrow = dtw[...].astype(jnp.float32)
    narrow = jnp.concatenate([narrow, jnp.zeros((16 - heads, narrow.shape[1]), jnp.float32)], axis=0).astype(jnp.bfloat16)
    steps_raw = lax.dot_general(nrm[...], narrow, (((1,), (1,)), ((), ())), preferred_element_type=jnp.float32)
    for p in range(parts):
        loads[p].wait()
        part = jnp.dot(nrm[:, p * depth : (p + 1) * depth], weight[p * depth : (p + 1) * depth],
                       preferred_element_type=jnp.float32)
        proj[...] = part if p == 0 else proj[...] + part

    for h in range(heads):
        at = h * columns
        raw = steps_raw[:, h : h + 1] + scalars[0, h]
        size = jnp.maximum(raw, 0.0) + jnp.log1p(jnp.exp(-jnp.abs(raw)))
        rate = jnp.exp(-size * jnp.exp(jnp.full((rows, 1), scalars[1, h], jnp.float32)))
        xin[h] = proj[:, at : at + head_size]
        xrow[h] = size * proj[:, at : at + head_size]
        decay[h] = jnp.broadcast_to(rate, (rows, head_size))
        kq[h] = proj[:, at + 2 * head_size : at + 2 * head_size + 2 * state_size].T

    def chunk(p, carry):
        at = pl.ds(p * per, per)
        pltpu.make_async_copy(state_hbm.at[at], state.at[at], s_sem.at[p]).wait()
        for h in range(heads):
            turned = pltpu.roll(kq[h], lax.rem(rows - p * per, rows), 1)
            outs = [[] for _ in range(steps)]
            for i in range(per):
                now = state[p * per + i, h]
                for s in range(steps):
                    lane = s * row_count + i
                    r = s * row_count + p * per + i
                    key = turned[:state_size, lane : lane + 1]
                    query = turned[state_size:, lane : lane + 1]
                    now = decay[h, pl.ds(r, 1)] * now + xrow[h, pl.ds(r, 1)] * key
                    outs[s].append(jnp.sum(now * query, axis=0, keepdims=True))
                state[p * per + i, h] = now
            for s in range(steps):
                read[h, pl.ds(pl.multiple_of(s * row_count + p * per, per), per)] = jnp.concatenate(outs[s], axis=0)
        pltpu.make_async_copy(state.at[at], new_hbm.at[at], n_sem.at[p]).start()
        return carry

    lax.fori_loop(0, chunks, chunk, 0)
    for h in range(heads):
        at = h * columns
        out = read[h] + scalars[2, h] * xin[h]
        gate = proj[:, at + head_size : at + 2 * head_size]
        out = out * (gate / (1.0 + jnp.exp(-gate)))
        out = out * lax.rsqrt(jnp.mean(out * out, axis=1, keepdims=True) + epsilon)
        out = out * ngain[:, h * head_size : (h + 1) * head_size]
        mixed[:, h * head_size : (h + 1) * head_size] = out.astype(jnp.bfloat16)
    for p in range(chunks):
        at = pl.ds(p * per, per)
        pltpu.make_async_copy(state.at[at], new_hbm.at[at], n_sem.at[p]).wait()


def mixer(emb, gain, weight, dtw, scalars, ngain, state):
    holders, rows, block = emb.shape
    row_count, heads, state_size, head_size = state.shape
    bf16, f32, dma = jnp.bfloat16, jnp.float32, pltpu.SemaphoreType.DMA
    vmem, anywhere = pl.BlockSpec(memory_space=pltpu.VMEM), pl.BlockSpec(memory_space=pl.ANY)
    smem = pl.BlockSpec(memory_space=pltpu.SMEM)
    return pl.pallas_call(
        functools.partial(mixer_kernel, heads),
        out_shape=(
            jax.ShapeDtypeStruct(state.shape, f32),
            jax.ShapeDtypeStruct((rows, heads * head_size), bf16),
        ),
        in_specs=[vmem, vmem, anywhere, vmem, smem, vmem, anywhere],
        out_specs=(anywhere, vmem),
        scratch_shapes=[
            pltpu.VMEM(weight.shape, bf16),
            pltpu.VMEM(state.shape, f32),
            pltpu.VMEM((rows, holders * block), bf16),
            pltpu.VMEM((rows, weight.shape[1]), f32),
            pltpu.VMEM((heads, 2 * state_size, rows), f32),
            pltpu.VMEM((heads, rows, head_size), f32),
            pltpu.VMEM((heads, rows, head_size), f32),
            pltpu.VMEM((heads, rows, head_size), f32),
            pltpu.VMEM((heads, rows, head_size), f32),
            dma((4,)),
            dma((8,)),
            dma((8,)),
        ],
        compiler_params=pltpu.CompilerParams(vmem_limit_bytes=40 * 2**20),
        name="mixer",
    )(emb, gain, weight, dtw, scalars, ngain, state)


def per_device(
    token_ids,
    embed_table,
    in_gain,
    in_weight,
    dt_weight,
    dt_bias,
    a_log,
    d_skip,
    norm_gain,
    out_weight,
    next_gain,
    ssm_state,
    trainer_weight,
    head_map,
):
    row_count, step_count = token_ids.shape
    model_width = embed_table.shape[1]
    heads_local = dt_weight.shape[1]
    head_size, state_size = ssm_state.shape[2], ssm_state.shape[3]
    holders = lax.axis_size("tensor")
    groups = lax.axis_size("dp")
    rows = row_count * step_count

    ids = token_ids.T.reshape(1, rows)
    emb, need, swapped = lookup(ids, embed_table, groups, holders, trainer=trainer_weight)

    def more(carry):
        done, held = carry
        start = jnp.full((8, 128), done, jnp.int32)
        (found,) = lookup(ids, embed_table, groups, holders, start=start)
        return done + SLOTS, held + found

    _, emb = lax.while_loop(lambda carry: carry[0] < need[0, 0], more, (jnp.int32(SLOTS), emb))

    now, mixed_out = mixer(
        emb,
        in_gain.reshape(holders, -1),
        in_weight,
        dt_weight.T,
        jnp.stack([dt_bias, a_log, d_skip]),
        norm_gain.reshape(1, -1),
        ssm_state.swapaxes(2, 3),
    )

    stream, whole, gathered = project(mixed_out, out_weight, emb, swapped, groups)
    wide = whole.astype(jnp.float32)
    mean_sq = jnp.sum(wide * wide, axis=(0, 2), keepdims=True) / model_width
    normed = wide * lax.rsqrt(mean_sq + epsilon) * next_gain.reshape(holders, 1, -1)
    normed = normed.astype(jnp.bfloat16).reshape(holders, step_count, row_count, -1)
    normed = normed.transpose(2, 1, 0, 3).reshape(row_count, step_count, model_width)
    stream = stream.reshape(step_count, row_count, -1).transpose(1, 0, 2)

    units = heads_local * head_size
    row_index = (lax.broadcasted_iota(jnp.int32, head_map.shape, 0) * head_size + head_map).reshape(-1)
    swap = (row_index[:, None] == lax.broadcasted_iota(jnp.int32, (1, units), 1)).astype(jnp.bfloat16)
    relaid = lax.dot_general(
        swap, gathered.reshape(model_width, units), (((1,), (1,)), ((), ())), preferred_element_type=jnp.float32
    )
    return now.swapaxes(2, 3), stream, normed, relaid


def solution(mesh):
    placed = (
        P("dp", None),
        P(("dp", "tensor"), None),
        P(),
        P(None, "tensor"),
        P(None, "tensor"),
        P("tensor"),
        P("tensor"),
        P("tensor"),
        P("tensor"),
        P("tensor", None),
        P(),
        P("dp", "tensor", None, None),
        P(("dp", "tensor"), None),
        P("tensor", None),
    )
    return jax.shard_map(
        per_device,
        mesh=mesh,
        in_specs=placed,
        out_specs=(
            P("dp", "tensor", None, None),
            P("dp", None, "tensor"),
            P("dp", None, None),
            P("tensor", None),
        ),
        check_vma=False,
    )
```

```python
import functools
import jax
import jax.numpy as jnp
from jax import lax
from jax.experimental import pallas as pl
from jax.experimental.pallas import tpu as pltpu
from jax.sharding import PartitionSpec as P

epsilon = 1e-05
MESH = pl.DeviceIdType.MESH
SLOTS = 8
WIDE = 32
Z = 4
X = 4


def remote(src, dst, send_sem, recv_sem, **place):
    return pltpu.make_async_remote_copy(
        src_ref=src,
        dst_ref=dst,
        send_sem=send_sem,
        recv_sem=recv_sem,
        device_id=place,
        device_id_type=MESH,
    )


def greet(places):
    barrier = pltpu.get_barrier_semaphore()
    for place in places:
        pl.semaphore_signal(barrier, inc=1, device_id=place, device_id_type=MESH)
    pl.semaphore_wait(barrier, len(places))


def tensor_near(t):
    y, z, c = t // (2 * Z), lax.rem(t // 2, Z), lax.rem(t, 2)
    ahead = [lax.rem(z + o, Z) for o in range(1, Z)]
    behind = [lax.rem(z + Z - o, Z) for o in range(1, Z)]
    place = lambda yy, zz, cc: yy * (2 * Z) + zz * 2 + cc
    return y, z, c, ahead, behind, place


def gather_blocks(buf, t, send, recv, use=lambda block: None):
    y, z, c, ahead, behind, place = tensor_near(t)
    other, across = place(y, z, 1 - c), place(1 - y, z, c)
    started, to_core = [], []

    def go(block, role, to):
        copy = remote(buf.at[block], buf.at[block], send.at[role], recv.at[role], tensor=to)
        copy.start()
        started.append(copy)
        return copy

    def core(block, role):
        to_core.append((go(block, role, other), role))

    to_across = go(t, 1, across)
    to_z = {o: go(t, 2 + o, place(y, ahead[o], c)) for o in (1, 0, 2)}
    core(t, 0)
    use(t)
    for o in (0, 2):
        to_z[o].wait_recv()
        core(place(y, behind[o], c), 9 + o)
    to_across.wait_recv()
    passed = {o: go(across, 5 + o // 2, place(y, ahead[o], c)) for o in (0, 2)}
    core(across, 8)
    to_z[1].wait_recv()
    far = go(place(y, behind[1], c), 7, across)
    core(place(y, behind[1], c), 10)
    use(place(y, behind[0], c))
    use(place(y, behind[2], c))
    use(across)
    use(place(y, behind[1], c))
    for o in (0, 2):
        passed[o].wait_recv()
        core(place(1 - y, behind[o], c), 12 + o // 2)
        use(place(1 - y, behind[o], c))
    to_core[0][0].wait_recv()
    use(other)
    far.wait_recv()
    core(place(1 - y, behind[1], c), 14)
    use(place(1 - y, behind[1], c))
    sources = [
        place(y, behind[0], 1 - c),
        place(y, behind[2], 1 - c),
        place(1 - y, z, 1 - c),
        place(y, behind[1], 1 - c),
        place(1 - y, behind[0], 1 - c),
        place(1 - y, behind[2], 1 - c),
        place(1 - y, behind[1], 1 - c),
    ]
    for (copy, _), block in zip(to_core[1:], sources):
        copy.wait_recv()
        use(block)
    for copy in started:
        copy.wait_send()


def order(row, column, at0, at1, vocab):
    again = jnp.where((column == row) & (at0 < at1), 1.0, 0.0)
    once = 1.0 - jnp.max(again, axis=0, keepdims=True)
    floor = column - lax.rem(column, vocab)
    before = jnp.where((row >= floor) & (row < column), once, 0.0)
    return once, jnp.sum(before, axis=1, keepdims=True).astype(jnp.int32)


def lookup_kernel(ids_ref, start_ref, table_hbm, emb, table, all_ids, out_d, in_d, out_t, in_t, local, ids_send, ids_recv,
                  d_send, d_recv, t_send, t_recv, g_send, g_recv):
    groups, holders = in_d.shape[0], in_t.shape[0]
    steps, row_count = ids_ref.shape
    rows, vocab, width = steps * row_count, table.shape[0], table.shape[1]
    block = width // holders
    half = width // 2
    g, t = lax.axis_index("dp"), lax.axis_index("tensor")
    load = pltpu.make_async_copy(table_hbm, table, local.at[0])
    load.start()
    row = jnp.concatenate([ids_ref[s : s + 1] for s in range(steps)], axis=1)
    all_ids[g] = jnp.broadcast_to(row, (8, rows))
    others_d = [lax.rem(g + o, groups) for o in range(1, groups)]
    others_t = [lax.rem(t + o, holders) for o in range(1, holders)]
    greet([{"dp": d} for d in others_d] + [{"tensor": d} for d in others_t])
    moves = []
    for o, d in enumerate(others_d):
        moves.append(remote(all_ids.at[g], all_ids.at[g], ids_send.at[o], ids_recv.at[o], dp=d))
        moves[-1].start()

    start = start_ref[0:1, 0:1]
    column = jnp.broadcast_to(row, (8, rows)).astype(jnp.float32).T.astype(jnp.int32)[:, 0:1]
    at0 = lax.broadcasted_iota(jnp.int32, (rows, rows), 0)
    at1 = lax.broadcasted_iota(jnp.int32, (rows, rows), 1)

    slot = order(row, column, at0, at1, vocab)[1] - start
    holder = column // vocab
    from_t, from_g = lax.rem(holder, holders), holder // holders
    want = jnp.where((slot >= 0) & (slot < SLOTS), (from_t * groups + from_g) * SLOTS + slot, -1)
    candidates = holders * groups * SLOTS

    for copy in moves:
        copy.wait()

    ids_all = all_ids[0]
    at_g = lax.broadcasted_iota(jnp.int32, (8, rows), 0)
    for gg in range(1, groups):
        ids_all = jnp.where(at_g == gg, all_ids[gg], ids_all)
    columns = ids_all.astype(jnp.float32).T.astype(jnp.int32)
    base = (g * holders + t) * vocab
    at_v = lax.broadcasted_iota(jnp.int32, (rows, vocab), 1)
    pick_g = lax.broadcasted_iota(jnp.int32, (16, vocab), 0)
    held = jnp.zeros((16, vocab), jnp.float32)
    for gg in range(groups):
        asked = jnp.where(columns[:, gg : gg + 1] - base == at_v, 1.0, 0.0)
        held = jnp.where(pick_g == gg, jnp.max(asked, axis=0, keepdims=True), held)
    lower = jnp.where(
        lax.broadcasted_iota(jnp.int32, (vocab, vocab), 0) < lax.broadcasted_iota(jnp.int32, (vocab, vocab), 1),
        1.0,
        0.0,
    ).astype(jnp.bfloat16)
    rank = jnp.dot(held.astype(jnp.bfloat16), lower, preferred_element_type=jnp.float32).astype(jnp.int32) - start
    at_c = lax.broadcasted_iota(jnp.int32, (SLOTS, vocab), 0)
    chosen = jnp.concatenate(
        [
            jnp.where((rank[gg : gg + 1] == at_c) & (held[gg : gg + 1] > 0.5), 1.0, 0.0)
            for gg in range(groups)
        ],
        axis=0,
    ).astype(jnp.bfloat16)
    load.wait()
    step = 512
    for at in range(0, half, step):
        low = jnp.dot(chosen, table[:, at : at + step], preferred_element_type=jnp.float32)
        high = jnp.dot(chosen, table[:, half + at : half + at + step], preferred_element_type=jnp.float32)
        both = jnp.concatenate(
            [low.reshape(groups, SLOTS, step), high.reshape(groups, SLOTS, step)], axis=1
        )
        out_d[:, :, at : at + step] = both.astype(jnp.bfloat16)
    sent = []
    for o, d in enumerate(others_d):
        sent.append(remote(out_d.at[d], in_d.at[g], d_send.at[o], d_recv.at[o], dp=d))
        sent[-1].start()
    in_d[g] = out_d[g]
    select = jnp.where(
        want == lax.broadcasted_iota(jnp.int32, (rows, candidates), 1), 1.0, 0.0
    ).astype(jnp.bfloat16)
    permute = jnp.where(at1 == lax.rem(at0, steps) * row_count + at0 // steps, 1.0, 0.0).astype(jnp.bfloat16)
    select = jnp.dot(permute, select, preferred_element_type=jnp.float32).astype(jnp.bfloat16)
    for copy in sent:
        copy.wait()
    for o in range(holders):
        part, at = o // (holders // 2), (o % (holders // 2)) * block
        piece = in_d[:, :, at : at + block].astype(jnp.float32)[:, part * SLOTS : (part + 1) * SLOTS]
        out_t[o] = piece.reshape(groups * SLOTS, block).astype(jnp.bfloat16)
    sent = []
    for o, d in enumerate(others_t):
        sent.append(remote(out_t.at[d], in_t.at[t], t_send.at[o], t_recv.at[o], tensor=d))
        sent[-1].start()
    in_t[t] = out_t[t]
    for copy in sent:
        copy.wait()
    found = jnp.dot(select, in_t[...].reshape(candidates, block), preferred_element_type=jnp.float32)
    emb[t] = found.astype(jnp.bfloat16)
    gather_blocks(emb, t, g_send, g_recv)


def lookup(ids, table, groups, holders, start):
    rows = ids.shape[0] * ids.shape[1]
    vocab, width = table.shape
    block = width // holders
    bf16, dma = jnp.bfloat16, pltpu.SemaphoreType.DMA
    vmem, anywhere = pl.BlockSpec(memory_space=pltpu.VMEM), pl.BlockSpec(memory_space=pl.ANY)
    return pl.pallas_call(
        lookup_kernel,
        out_shape=jax.ShapeDtypeStruct((holders, rows, block), bf16),
        in_specs=[vmem, vmem, anywhere],
        out_specs=vmem,
        scratch_shapes=[
            pltpu.VMEM((vocab, width), bf16),
            pltpu.VMEM((groups, 8, rows), jnp.int32),
            pltpu.VMEM((groups, 2 * SLOTS, width // 2), bf16),
            pltpu.VMEM((groups, 2 * SLOTS, width // 2), bf16),
            pltpu.VMEM((holders, groups * SLOTS, block), bf16),
            pltpu.VMEM((holders, groups * SLOTS, block), bf16),
            dma((1,)),
            dma((groups - 1,)),
            dma((groups - 1,)),
            dma((groups - 1,)),
            dma((groups - 1,)),
            dma((holders - 1,)),
            dma((holders - 1,)),
            dma((holders - 1,)),
            dma((holders - 1,)),
        ],
        compiler_params=pltpu.CompilerParams(collective_id=1, has_side_effects=True, vmem_limit_bytes=40 * 2**20),
        name="lookup_round",
    )(ids, start, table)


def normalize(whole, gain, out):
    holders, rows, block = whole.shape
    squares = jnp.zeros((rows, block), jnp.float32)
    for k in range(holders):
        wide = whole[k].astype(jnp.float32)
        squares = squares + wide * wide
    scale = lax.rsqrt(jnp.sum(squares, axis=1, keepdims=True) / (holders * block) + epsilon)
    for k in range(holders):
        at = slice(k * block, (k + 1) * block)
        out[:, at] = (whole[k].astype(jnp.float32) * scale * gain[:, at]).astype(jnp.bfloat16)


def project_kernel(mixed, weight_hbm, emb, next_gain, stream, normed, whole, weight, out_c, in_c, kept, out_z, in_z, slab, out_y, in_y, local,
                   c_send, c_recv, z_send, z_recv, y_send, y_recv, g_send, g_recv):
    t = lax.axis_index("tensor")
    block = whole.shape[2]
    load = pltpu.make_async_copy(weight_hbm, weight, local.at[0])
    load.start()
    y, z, c, ahead, behind, place = tensor_near(t)
    other, across = place(y, z, 1 - c), place(1 - y, z, c)
    greet([{"tensor": other}, {"tensor": across}] + [{"tensor": place(y, zz, c)} for zz in ahead])

    load.wait()
    rows_in = mixed[...]

    def partial_of(k, cc):
        at = place(k % 2, k // 2, cc) * block
        return jnp.dot(rows_in, weight[:, pl.ds(pl.multiple_of(at, block), block)], preferred_element_type=jnp.float32)

    to_core = []
    for k in range(2 * Z):
        out_c[k] = partial_of(k, 1 - c).astype(jnp.bfloat16)
        to_core.append(remote(out_c.at[k], in_c.at[k], c_send.at[k], c_recv.at[k], tensor=other))
        to_core[-1].start()
    for k in range(2 * Z):
        kept[k // 2, k % 2] = partial_of(k, c)
    for k in range(2 * Z):
        to_core[k].wait_recv()
        total = kept[k // 2, k % 2] + in_c[k].astype(jnp.float32)
        kept[k // 2, k % 2] = total
        out_z[k // 2, k % 2] = total.astype(jnp.bfloat16)
    to_z = []
    for o in range(Z - 1):
        to_z.append(
            remote(out_z.at[ahead[o]], in_z.at[o], z_send.at[o], z_recv.at[o], tensor=place(y, ahead[o], c))
        )
        to_z[-1].start()
    total = kept[z]
    for o in range(Z - 1):
        to_z[o].wait_recv()
        total = total + in_z[o].astype(jnp.float32)
    slab[...] = total
    out_y[...] = slab[1 - y].astype(jnp.bfloat16)
    to_y = remote(out_y, in_y, y_send.at[0], y_recv.at[0], tensor=across)
    to_y.start()
    to_y.wait_recv()
    branch = slab[y] + in_y[...].astype(jnp.float32)
    mine = (emb[t].astype(jnp.float32) + branch).astype(jnp.bfloat16)
    stream[...] = mine
    whole[t] = mine
    gather_blocks(whole, t, g_send, g_recv)
    normalize(whole, next_gain, normed)
    for copy in to_core + to_z + [to_y]:
        copy.wait_send()


def project(mixed, weight, emb, next_gain):
    holders, rows, block = emb.shape
    bf16, f32, dma = jnp.bfloat16, jnp.float32, pltpu.SemaphoreType.DMA
    vmem, anywhere = pl.BlockSpec(memory_space=pltpu.VMEM), pl.BlockSpec(memory_space=pl.ANY)
    return pl.pallas_call(
        project_kernel,
        out_shape=(
            jax.ShapeDtypeStruct((rows, block), bf16),
            jax.ShapeDtypeStruct((rows, holders * block), bf16),
        ),
        in_specs=[vmem, anywhere, vmem, vmem],
        out_specs=(vmem, vmem),
        scratch_shapes=[
            pltpu.VMEM((holders, rows, block), bf16),
            pltpu.VMEM(weight.shape, bf16),
            pltpu.VMEM((2 * Z, rows, block), bf16),
            pltpu.VMEM((2 * Z, rows, block), bf16),
            pltpu.VMEM((Z, 2, rows, block), f32),
            pltpu.VMEM((Z, 2, rows, block), bf16),
            pltpu.VMEM((Z - 1, 2, rows, block), bf16),
            pltpu.VMEM((2, rows, block), f32),
            pltpu.VMEM((rows, block), bf16),
            pltpu.VMEM((rows, block), bf16),
            dma((1,)),
            dma((2 * Z,)),
            dma((2 * Z,)),
            dma((Z - 1,)),
            dma((Z - 1,)),
            dma((1,)),
            dma((1,)),
            dma((holders - 1,)),
            dma((holders - 1,)),
        ],
        compiler_params=pltpu.CompilerParams(
            collective_id=2, has_side_effects=True, vmem_limit_bytes=40 * 2**20
        ),
        name="project",
    )(mixed, weight, emb, next_gain)


def readout(p, per, heads, steps, query, state, read):
    rows = read.shape[1]
    base = pl.multiple_of(p * (per * steps), per * steps)
    for h in range(heads):
        turned = pltpu.roll(query[h], lax.rem(rows - base, rows), 1)
        outs = []
        for i in range(per):
            old = state[p * per + i, h]
            for s in range(steps):
                lane = i * steps + s
                outs.append(jnp.sum(old * turned[:, lane : lane + 1], axis=0, keepdims=True))
        read[h, pl.ds(base, per * steps)] = jnp.concatenate(outs, axis=0)


def update(p, per, heads, steps, key, state, decay, xrow):
    rows = xrow.shape[1]
    base = pl.multiple_of(p * (per * steps), per * steps)
    for h in range(heads):
        turned = pltpu.roll(key[h], lax.rem(rows - base, rows), 1)
        for i in range(per):
            now = state[p * per + i, h]
            for s in range(steps):
                lane = i * steps + s
                now = decay[h, pl.ds(base + lane, 1)] * now + xrow[h, pl.ds(base + lane, 1)] * turned[:, lane : lane + 1]
            state[p * per + i, h] = now


def mix(h, proj, raw, bias, log_rate, columns, head_size, state_size, key, query, xin, xrow, decay):
    rows, at = proj.shape[0], h * columns
    value = raw[:, h : h + 1] + bias[h]
    size = jnp.maximum(value, 0.0) + jnp.log1p(jnp.exp(-jnp.abs(value)))
    rate = jnp.exp(-size * jnp.exp(jnp.full((rows, 1), log_rate[h], jnp.float32)))
    entry = proj[:, at : at + head_size]
    xin[h] = entry
    xrow[h] = size * entry
    decay[h] = jnp.broadcast_to(rate, (rows, head_size))
    at += 2 * head_size
    turned = proj[:, at : at + 2 * state_size].T
    key[h] = turned[:state_size]
    query[h] = turned[state_size:]


def close(h, steps, proj, skip, ngain, columns, head_size, state_size, xin, xrow, decay, read, mixed):
    at = h * columns
    rows = proj.shape[0]
    both = proj[:, at + 2 * head_size : at + 2 * head_size + 2 * state_size]
    queries = both[:, state_size:]
    step = lax.rem(lax.broadcasted_iota(jnp.int32, (rows, 1), 0), steps)
    rates, entry = decay[h], xrow[h]
    reach = rates
    out = jnp.sum(both[:, :state_size] * queries, axis=1, keepdims=True) * entry
    for back in range(1, steps):
        keys = pltpu.roll(both, back, 0)[:, :state_size]
        old = jnp.sum(keys * queries, axis=1, keepdims=True) * pltpu.roll(entry, back, 0)
        out = jnp.where(step >= back, out + reach * old, out)
        reach = jnp.where(step >= back, reach * pltpu.roll(rates, back, 0), reach)
    out = out + reach * read[h]
    out = out + skip[h] * xin[h]
    gate = proj[:, at + head_size : at + 2 * head_size]
    out = out * (gate / (1.0 + jnp.exp(-gate)))
    out = out * lax.rsqrt(jnp.mean(out * out, axis=1, keepdims=True) + epsilon)
    out = out * ngain[:, h * head_size : (h + 1) * head_size]
    mixed[:, h * head_size : (h + 1) * head_size] = out.astype(jnp.bfloat16)


def mixer_kernel(heads, emb, gain, weight_hbm, dtw, bias, log_rate, skip, ngain, state_hbm, new_hbm, mixed, weight, state, nrm, proj,
                 key, query, xin, xrow, decay, read, w_sem, s_sem, n_sem):
    holders, rows, block = emb.shape
    row_count, _, state_size, head_size = state.shape
    columns = weight.shape[1] // heads
    steps = rows // row_count
    parts = w_sem.shape[0]
    depth = weight.shape[0] // parts
    chunks = s_sem.shape[0]
    per = row_count // chunks
    loads = []
    for p in range(parts):
        at = pl.ds(p * depth, depth)
        loads.append(pltpu.make_async_copy(weight_hbm.at[at], weight.at[at], w_sem.at[p]))
        loads[-1].start()
    for p in range(chunks):
        at = pl.ds(p * per, per)
        pltpu.make_async_copy(state_hbm.at[at], state.at[at], s_sem.at[p]).start()

    squares = jnp.zeros((rows, block), jnp.float32)
    for k in range(holders):
        wide = emb[k].astype(jnp.float32)
        squares = squares + wide * wide
    scale = lax.rsqrt(jnp.sum(squares, axis=1, keepdims=True) / (holders * block) + epsilon)
    for k in range(holders):
        nrm[:, k * block : (k + 1) * block] = (emb[k].astype(jnp.float32) * scale * gain[:, k * block : (k + 1) * block]).astype(jnp.bfloat16)
    narrow = dtw[...].astype(jnp.float32)
    narrow = jnp.concatenate([narrow, jnp.zeros((16 - heads, narrow.shape[1]), jnp.float32)], axis=0).astype(jnp.bfloat16)
    steps_raw = lax.dot_general(nrm[...], narrow, (((1,), (1,)), ((), ())), preferred_element_type=jnp.float32)
    for p in range(parts):
        loads[p].wait()
        part = jnp.dot(nrm[:, p * depth : (p + 1) * depth], weight[p * depth : (p + 1) * depth],
                       preferred_element_type=jnp.float32)
        proj[...] = part if p == 0 else proj[...] + part

    sizes = (columns, head_size, state_size)
    for h in range(heads):
        mix(h, proj, steps_raw, bias, log_rate, *sizes, key, query, xin, xrow, decay)

    def chunk(p, carry):
        at = pl.ds(p * per, per)
        pltpu.make_async_copy(state_hbm.at[at], state.at[at], s_sem.at[p]).wait()
        readout(p, per, heads, steps, query, state, read)
        update(p, per, heads, steps, key, state, decay, xrow)
        pltpu.make_async_copy(state.at[at], new_hbm.at[at], n_sem.at[p]).start()
        return carry

    lax.fori_loop(0, chunks, chunk, 0)
    for h in range(heads):
        close(h, steps, proj, skip, ngain, *sizes, xin, xrow, decay, read, mixed)
    for p in range(chunks):
        at = pl.ds(p * per, per)
        pltpu.make_async_copy(state.at[at], new_hbm.at[at], n_sem.at[p]).wait()


def mixer(emb, gain, weight, dtw, bias, log_rate, skip, ngain, state):
    holders, rows, block = emb.shape
    row_count, heads, state_size, head_size = state.shape
    bf16, f32, dma = jnp.bfloat16, jnp.float32, pltpu.SemaphoreType.DMA
    vmem, anywhere = pl.BlockSpec(memory_space=pltpu.VMEM), pl.BlockSpec(memory_space=pl.ANY)
    smem = pl.BlockSpec(memory_space=pltpu.SMEM)
    return pl.pallas_call(
        functools.partial(mixer_kernel, heads),
        out_shape=(
            jax.ShapeDtypeStruct(state.shape, f32),
            jax.ShapeDtypeStruct((rows, heads * head_size), bf16),
        ),
        in_specs=[vmem, vmem, anywhere, vmem, smem, smem, smem, vmem, anywhere],
        out_specs=(anywhere, vmem),
        scratch_shapes=[
            pltpu.VMEM(weight.shape, bf16),
            pltpu.VMEM(state.shape, f32),
            pltpu.VMEM((rows, holders * block), bf16),
            pltpu.VMEM((rows, weight.shape[1]), f32),
            pltpu.VMEM((heads, state_size, rows), f32),
            pltpu.VMEM((heads, state_size, rows), f32),
            pltpu.VMEM((heads, rows, head_size), f32),
            pltpu.VMEM((heads, rows, head_size), f32),
            pltpu.VMEM((heads, rows, head_size), f32),
            pltpu.VMEM((heads, rows, head_size), f32),
            dma((4,)),
            dma((8,)),
            dma((8,)),
        ],
        compiler_params=pltpu.CompilerParams(vmem_limit_bytes=40 * 2**20),
        name="mixer",
    )(emb, gain, weight, dtw, bias, log_rate, skip, ngain, state)


def fused_kernel(heads, ids_in, table_hbm, trainer_hbm, gain, weight_hbm, dtw, bias, log_rate, skip, ngain,
                 state_hbm, oweight_hbm, next_gain, head_map, new_hbm, stream, normed, gathered, swap, need, table,
                 trainer, weight, state, oweight, all_ids, out_d, in_d, out_t, in_t, out_r, in_r, emb, whole,
                 swap_out, proj, narrow, raw, key, query, xin, xrow, decay, read, mixed, out_c, in_c, kept, out_z,
                 in_z, slab, out_y, in_y, l_sem, w_sem, s_sem, n_sem, i_send, i_recv, d_send, d_recv, t_send,
                 t_recv, r_send, r_recv, e_send, e_recv, a_send, a_recv, x_send, x_recv, c_send, c_recv, z_send,
                 z_recv, y_send, y_recv, g_send, g_recv):
    bf16, f32 = jnp.bfloat16, jnp.float32
    groups, holders = in_d.shape[0], in_t.shape[0]
    vocab, width = table.shape
    rows, block = emb.shape[1], emb.shape[2]
    half = width // 2
    row_count, _, state_size, head_size = state.shape
    steps = rows // row_count
    trows = trainer.shape[0]
    g, t = lax.axis_index("dp"), lax.axis_index("tensor")
    y, z, c, ahead, behind, place = tensor_near(t)
    other, across = place(y, z, 1 - c), place(1 - y, z, c)
    x, low = g // 2, lax.rem(g, 2)
    beside = x * 2 + 1 - low
    x_ahead = [lax.rem(x + o, X) * 2 + low for o in range(1, X)]
    x_behind = [lax.rem(x + X - o, X) * 2 + low for o in range(1, X)]

    load_table = pltpu.make_async_copy(table_hbm, table, l_sem.at[0])
    load_table.start()
    load_trainer = pltpu.make_async_copy(trainer_hbm, trainer, l_sem.at[1])
    load_trainer.start()
    ids2 = ids_in[...]
    row = jnp.concatenate([ids2[s : s + 1] for s in range(steps)], axis=1)
    all_ids[g] = jnp.broadcast_to(row, (8, rows))
    others_d = [lax.rem(g + o, groups) for o in range(1, groups)]
    others_t = [lax.rem(t + o, holders) for o in range(1, holders)]
    greet([{"dp": d} for d in others_d] + [{"tensor": d} for d in others_t])
    moves = []
    for o, d in enumerate(others_d):
        moves.append(remote(all_ids.at[g], all_ids.at[g], i_send.at[o], i_recv.at[o], dp=d))
        moves[-1].start()

    load_oweight = pltpu.make_async_copy(oweight_hbm, oweight, l_sem.at[2])
    loads_w = [
        pltpu.make_async_copy(weight_hbm.at[pl.ds(k * block, block)], weight.at[k], w_sem.at[k])
        for k in range(holders)
    ]
    chunks = s_sem.shape[0]
    per = row_count // chunks

    def old_state(p):
        at = pl.ds(p * per, per)
        return pltpu.make_async_copy(state_hbm.at[at], state.at[at], s_sem.at[p])

    def fresh_state(p):
        at = pl.ds(p * per, per)
        return pltpu.make_async_copy(state.at[at], new_hbm.at[at], n_sem.at[p])

    load_trainer.wait()
    for o in range(holders):
        swap_out[o] = trainer[:, o * block : (o + 1) * block].astype(bf16)
    swaps = []
    for o, d in enumerate(others_t):
        swaps.append(remote(swap_out.at[d], gathered.at[g, t], a_send.at[o], a_recv.at[o], tensor=d))
        swaps[-1].start()
    gathered[g, t] = swap_out[t]
    for copy in loads_w + [load_oweight]:
        copy.start()
    for p in range(chunks):
        old_state(p).start()

    at0 = lax.broadcasted_iota(jnp.int32, (rows, rows), 0)
    at1 = lax.broadcasted_iota(jnp.int32, (rows, rows), 1)

    def turn(column):
        return jnp.broadcast_to(column.astype(f32), (rows, rows)).T[0:1].astype(jnp.int32)

    def places(row, column):
        once, slot = order(row, column, at0, at1, vocab)
        fits = jnp.where(turn(slot) < SLOTS, once, 0.0)
        column_t, row_t = lax.rem(column // vocab, holders), lax.rem(row // vocab, holders)
        before = jnp.where((row_t == column_t) & (row < column), fits, 0.0)
        return once, slot, jnp.sum(before, axis=1, keepdims=True).astype(jnp.int32)

    column = jnp.broadcast_to(row, (8, rows)).astype(f32).T.astype(jnp.int32)[:, 0:1]
    once, slot, index = places(row, column)
    from_t, from_g = lax.rem(column // vocab, holders), column // (vocab * holders)
    comes = (slot < SLOTS) & (index < WIDE)
    want = jnp.where(comes, from_t * WIDE + index, -1)
    select = jnp.where(want == lax.broadcasted_iota(jnp.int32, (rows, holders * WIDE), 1), 1.0, 0.0).astype(bf16)
    permute = jnp.where(at1 == lax.rem(at0, steps) * row_count + at0 // steps, 1.0, 0.0).astype(bf16)
    select = jnp.dot(permute, select, preferred_element_type=f32).astype(bf16)
    index_row = turn(jnp.where((from_t == t) & comes, index, -1))
    lift = jnp.where(
        (lax.broadcasted_iota(jnp.int32, (WIDE, rows), 0) == index_row) & (once > 0.5), 1.0, 0.0
    ).astype(bf16)
    spot = jnp.where(slot < SLOTS, from_g * (2 * SLOTS) + slot, -2 * SLOTS * groups)
    take_low = jnp.dot(lift, jnp.where(spot == at1, 1.0, 0.0).astype(bf16), preferred_element_type=f32).astype(bf16)
    take_high = jnp.dot(
        lift, jnp.where(spot + SLOTS == at1, 1.0, 0.0).astype(bf16), preferred_element_type=f32
    ).astype(bf16)
    lower = jnp.where(
        lax.broadcasted_iota(jnp.int32, (vocab, vocab), 0) < lax.broadcasted_iota(jnp.int32, (vocab, vocab), 1),
        1.0,
        0.0,
    ).astype(bf16)

    for copy in moves:
        copy.wait()
    ids_all = all_ids[0]
    at_g = lax.broadcasted_iota(jnp.int32, (8, rows), 0)
    for gg in range(1, groups):
        ids_all = jnp.where(at_g == gg, all_ids[gg], ids_all)
    columns = ids_all.astype(f32).T.astype(jnp.int32)
    base = (g * holders + t) * vocab
    at_v = lax.broadcasted_iota(jnp.int32, (rows, vocab), 1)
    pick_g = lax.broadcasted_iota(jnp.int32, (16, vocab), 0)
    held = jnp.zeros((16, vocab), f32)
    for gg in range(groups):
        asked = jnp.where(columns[:, gg : gg + 1] - base == at_v, 1.0, 0.0)
        held = jnp.where(pick_g == gg, jnp.max(asked, axis=0, keepdims=True), held)
    rank = jnp.dot(held.astype(bf16), lower, preferred_element_type=f32).astype(jnp.int32)
    at_c = lax.broadcasted_iota(jnp.int32, (SLOTS, vocab), 0)
    chosen = jnp.concatenate(
        [
            jnp.where((rank[gg : gg + 1] == at_c) & (held[gg : gg + 1] > 0.5), 1.0, 0.0)
            for gg in range(groups)
        ],
        axis=0,
    ).astype(bf16)
    load_table.wait()
    step = 512
    for at in range(0, half, step):
        left = jnp.dot(chosen, table[:, at : at + step], preferred_element_type=f32)
        right = jnp.dot(chosen, table[:, half + at : half + at + step], preferred_element_type=f32)
        both = jnp.concatenate(
            [left.reshape(groups, SLOTS, step), right.reshape(groups, SLOTS, step)], axis=1
        )
        out_d[:, :, at : at + step] = both.astype(bf16)
    sent = []
    for o, d in enumerate(others_d):
        sent.append(remote(out_d.at[d], in_d.at[g], d_send.at[o], d_recv.at[o], dp=d))
        sent[-1].start()
    in_d[g] = out_d[g]

    most = jnp.zeros((1, 1), jnp.int32)
    over = jnp.zeros((1, 1), jnp.int32)
    for gg in range(groups):
        _, slots, indices = places(all_ids[gg][0:1], columns[:, gg : gg + 1])
        most = jnp.maximum(most, jnp.max(slots, axis=0, keepdims=True))
        over = jnp.maximum(over, jnp.max(indices, axis=0, keepdims=True))
    todo = jnp.where((most >= SLOTS) | (over >= WIDE), most + 1, 0)
    need[0, 0] = todo[0, 0]
    units = heads * head_size
    maps = jnp.concatenate(
        [head_map[...].astype(f32), jnp.zeros((8 - heads, head_size), f32)], axis=0
    ).T.astype(jnp.int32)
    at_u = lax.broadcasted_iota(jnp.int32, (head_size, units), 1)
    for h in range(heads):
        swap[h * head_size : (h + 1) * head_size] = jnp.where(
            maps[:, h : h + 1] + h * head_size == at_u, 1.0, 0.0
        ).astype(bf16)
    for k in range(holders):
        thin = dtw[:, k * block : (k + 1) * block].astype(f32)
        narrow[k] = jnp.concatenate([thin, jnp.zeros((16 - heads, block), f32)], axis=0).astype(bf16)
    proj[...] = jnp.zeros_like(proj)
    raw[...] = jnp.zeros_like(raw)

    for copy in sent:
        copy.wait()
    arrived = in_d[...].reshape(groups * 2 * SLOTS, half)
    total = jnp.zeros((WIDE, block), f32)
    for part, take in enumerate((take_low, take_high)):
        for k in range(holders // 2):
            piece = jnp.dot(take, arrived[:, k * block : (k + 1) * block], preferred_element_type=f32)
            out_r[part * (holders // 2) + k] = piece.astype(bf16)
            total = total + piece * piece
    scale = lax.rsqrt(jnp.sum(total, axis=1, keepdims=True) / width + epsilon)
    for k in range(holders):
        scaled = out_r[k].astype(f32) * scale * gain[:, k * block : (k + 1) * block]
        out_t[k] = scaled.astype(bf16)
    sent = []
    for o, d in enumerate(others_t):
        sent.append(remote(out_t.at[d], in_t.at[t], t_send.at[o], t_recv.at[o], tensor=d))
        sent[-1].start()
    in_t[t] = out_t[t]

    shared = []

    def share(block_at, role, to):
        copy = remote(gathered.at[block_at], gathered.at[block_at], x_send.at[role], x_recv.at[role], dp=to)
        copy.start()
        shared.append(copy)
        return copy

    for copy in swaps:
        copy.wait()
    to_x = [share(g, 1 + o, x_ahead[o]) for o in range(X - 1)]

    for copy in sent:
        copy.wait()
    found = jnp.dot(select, in_t[...].reshape(holders * WIDE, block), preferred_element_type=f32)
    emb[t] = found.astype(bf16)

    def project_in(k):
        proj[...] += jnp.dot(emb[k], weight[k], preferred_element_type=f32)
        raw[...] += lax.dot_general(emb[k], narrow[k], (((1,), (1,)), ((), ())), preferred_element_type=f32)

    for copy in loads_w:
        copy.wait()
    gather_blocks(emb, t, e_send, e_recv, project_in)
    residual = []
    for o, d in enumerate(others_t):
        residual.append(remote(out_r.at[d], in_r.at[t], r_send.at[o], r_recv.at[o], tensor=d))
        residual[-1].start()
    in_r[t] = out_r[t]
    to_beside = share(g, 0, beside)
    sizes = (weight.shape[2] // heads, head_size, state_size)
    for h in range(heads):
        mix(h, proj, raw, bias, log_rate, *sizes, key, query, xin, xrow, decay)

    def look(p, carry):
        old_state(p).wait()
        readout(p, per, heads, steps, query, state, read)
        return carry

    lax.fori_loop(0, chunks, look, 0)
    for h in range(heads):
        close(h, steps, proj, skip, ngain, *sizes, xin, xrow, decay, read, mixed)

    load_oweight.wait()
    rows_in = mixed[...]

    def partial_of(k, cc):
        at = place(k % 2, k // 2, cc) * block
        return jnp.dot(rows_in, oweight[:, pl.ds(pl.multiple_of(at, block), block)], preferred_element_type=f32)

    to_core = []
    for k in range(2 * Z):
        out_c[k] = partial_of(k, 1 - c).astype(bf16)
        to_core.append(remote(out_c.at[k], in_c.at[k], c_send.at[k], c_recv.at[k], tensor=other))
        to_core[-1].start()
    for k in range(2 * Z):
        kept[k // 2, k % 2] = partial_of(k, c)
    for k in range(2 * Z):
        to_core[k].wait_recv()
        total = kept[k // 2, k % 2] + in_c[k].astype(f32)
        kept[k // 2, k % 2] = total
        out_z[k // 2, k % 2] = total.astype(bf16)
    to_z = []
    for o in range(Z - 1):
        to_z.append(
            remote(out_z.at[ahead[o]], in_z.at[o], z_send.at[o], z_recv.at[o], tensor=place(y, ahead[o], c))
        )
        to_z[-1].start()

    def move_on(p, carry):
        update(p, per, heads, steps, key, state, decay, xrow)
        fresh_state(p).start()
        return carry

    lax.fori_loop(0, chunks // 2, move_on, 0)
    to_beside.wait_recv()
    passed = [share(beside, X + o, x_ahead[o]) for o in range(X - 1)]
    lax.fori_loop(chunks // 2, chunks, move_on, 0)
    for copy in residual:
        copy.wait()
    embedded = jnp.dot(select, in_r[...].reshape(holders * WIDE, block), preferred_element_type=f32)
    total = kept[z]
    for o in range(Z - 1):
        to_z[o].wait_recv()
        total = total + in_z[o].astype(f32)
    slab[...] = total
    out_y[...] = slab[1 - y].astype(bf16)
    to_y = remote(out_y, in_y, y_send.at[0], y_recv.at[0], tensor=across)
    to_y.start()
    to_y.wait_recv()
    branch = slab[y] + in_y[...].astype(f32)
    mine = (embedded + branch).astype(bf16)
    stream[...] = mine
    whole[t] = mine

    gather_blocks(whole, t, g_send, g_recv)
    normalize(whole, next_gain, normed)
    for copy in to_x + passed:
        copy.wait_recv()
    for copy in to_core + to_z + [to_y] + shared:
        copy.wait_send()
    for p in range(chunks):
        fresh_state(p).wait()


def fused(ids, table, trainer, gain, weight, dtw, bias, log_rate, skip, ngain, state, oweight, next_gain, head_map,
          groups, holders):
    row_count, heads, state_size, head_size = state.shape
    rows = ids.shape[0] * ids.shape[1]
    vocab, width = table.shape
    block = width // holders
    trows = trainer.shape[0]
    units = heads * head_size
    columns = weight.shape[1]
    bf16, f32, dma = jnp.bfloat16, jnp.float32, pltpu.SemaphoreType.DMA
    vmem, anywhere = pl.BlockSpec(memory_space=pltpu.VMEM), pl.BlockSpec(memory_space=pl.ANY)
    smem = pl.BlockSpec(memory_space=pltpu.SMEM)
    buffers = [
        ((vocab, width), bf16),
        (trainer.shape, f32),
        ((holders, block, columns), bf16),
        (state.shape, f32),
        (oweight.shape, bf16),
        ((groups, 8, rows), jnp.int32),
        ((groups, 2 * SLOTS, width // 2), bf16),
        ((groups, 2 * SLOTS, width // 2), bf16),
        ((holders, WIDE, block), bf16),
        ((holders, WIDE, block), bf16),
        ((holders, WIDE, block), bf16),
        ((holders, WIDE, block), bf16),
        ((holders, rows, block), bf16),
        ((holders, rows, block), bf16),
        ((holders, trows, block), bf16),
        ((rows, columns), f32),
        ((holders, 16, block), bf16),
        ((rows, 16), f32),
        ((heads, state_size, rows), f32),
        ((heads, state_size, rows), f32),
        ((heads, rows, head_size), f32),
        ((heads, rows, head_size), f32),
        ((heads, rows, head_size), f32),
        ((heads, rows, head_size), f32),
        ((rows, units), bf16),
        ((2 * Z, rows, block), bf16),
        ((2 * Z, rows, block), bf16),
        ((Z, 2, rows, block), f32),
        ((Z, 2, rows, block), bf16),
        ((Z - 1, 2, rows, block), bf16),
        ((2, rows, block), f32),
        ((rows, block), bf16),
        ((rows, block), bf16),
    ]
    semaphores = [3, holders, 8, 8]
    for count in (groups - 1, groups - 1, holders - 1, holders - 1, holders - 1, holders - 1, 2 * X - 1, 2 * Z, Z - 1, 1):
        semaphores += [count, count]
    semaphores += [holders - 1, holders - 1]
    return pl.pallas_call(
        functools.partial(fused_kernel, heads),
        out_shape=(
            jax.ShapeDtypeStruct(state.shape, f32),
            jax.ShapeDtypeStruct((rows, block), bf16),
            jax.ShapeDtypeStruct((rows, width), bf16),
            jax.ShapeDtypeStruct((groups, holders, trows, block), bf16),
            jax.ShapeDtypeStruct((units, units), bf16),
            jax.ShapeDtypeStruct((1, 1), jnp.int32),
        ),
        in_specs=[vmem, anywhere, anywhere, vmem, anywhere, vmem, smem, smem, smem, vmem, anywhere, anywhere, vmem, vmem],
        out_specs=(anywhere, vmem, vmem, vmem, vmem, smem),
        scratch_shapes=[pltpu.VMEM(*buffer) for buffer in buffers] + [dma((count,)) for count in semaphores],
        compiler_params=pltpu.CompilerParams(
            collective_id=0, has_side_effects=True, vmem_limit_bytes=60 * 2**20
        ),
        name="fused",
    )(ids, table, trainer, gain, weight, dtw, bias, log_rate, skip, ngain, state, oweight, next_gain, head_map)


def per_device(
    token_ids,
    embed_table,
    in_gain,
    in_weight,
    dt_weight,
    dt_bias,
    a_log,
    d_skip,
    norm_gain,
    out_weight,
    next_gain,
    ssm_state,
    trainer_weight,
    head_map,
):
    row_count, step_count = token_ids.shape
    width = embed_table.shape[1]
    holders = lax.axis_size("tensor")
    groups = lax.axis_size("dp")
    rows = row_count * step_count
    state = ssm_state.swapaxes(2, 3)
    gain, ngain, ngain_next = in_gain.reshape(1, -1), norm_gain.reshape(1, -1), next_gain.reshape(1, -1)
    mix = (in_weight, dt_weight.T, dt_bias, a_log, d_skip, ngain, state)
    now, stream, normed, gathered, swap, need = fused(
        token_ids.T, embed_table, trainer_weight, gain, *mix, out_weight, ngain_next, head_map, groups, holders
    )

    def again(carry):
        todo = carry[0]

        def more(inner):
            done, held = inner
            return done + SLOTS, held + lookup(token_ids.T, embed_table, groups, holders, jnp.full((8, 128), done, jnp.int32))

        empty = jnp.zeros((holders, rows, width // holders), jnp.bfloat16)
        _, emb = lax.while_loop(lambda inner: inner[0] < todo, more, (jnp.int32(0), empty))
        now, mixed = mixer(emb, gain, *mix)
        stream, normed = project(mixed, out_weight, emb, ngain_next)
        return jnp.int32(0), now, stream, normed

    _, now, stream, normed = lax.while_loop(
        lambda carry: carry[0] > 0, again, (need.reshape(()), now, stream, normed)
    )
    relaid = lax.dot_general(
        swap,
        gathered.reshape(width, swap.shape[1]),
        (((1,), (1,)), ((), ())),
        preferred_element_type=jnp.float32,
    )
    return (
        now.swapaxes(2, 3),
        stream.reshape(row_count, step_count, -1),
        normed.reshape(row_count, step_count, width),
        relaid,
    )


def solution(mesh):
    placed = (
        P("dp", None),
        P(("dp", "tensor"), None),
        P(),
        P(None, "tensor"),
        P(None, "tensor"),
        P("tensor"),
        P("tensor"),
        P("tensor"),
        P("tensor"),
        P("tensor", None),
        P(),
        P("dp", "tensor", None, None),
        P(("dp", "tensor"), None),
        P("tensor", None),
    )
    return jax.shard_map(
        per_device,
        mesh=mesh,
        in_specs=placed,
        out_specs=(
            P("dp", "tensor", None, None),
            P("dp", None, "tensor"),
            P("dp", None, None),
            P("tensor", None),
        ),
        check_vma=False,
    )
```

```python
import functools
import jax
import jax.numpy as jnp
from jax import lax
from jax.experimental import pallas as pl
from jax.experimental.pallas import tpu as pltpu
from jax.sharding import PartitionSpec as P

epsilon = 1e-05
MESH = pl.DeviceIdType.MESH
SLOTS = 8
WIDE = 32
Z = 4
X = 4


def remote(src, dst, send_sem, recv_sem, **place):
    return pltpu.make_async_remote_copy(
        src_ref=src,
        dst_ref=dst,
        send_sem=send_sem,
        recv_sem=recv_sem,
        device_id=place,
        device_id_type=MESH,
    )


def greet(places):
    barrier = pltpu.get_barrier_semaphore()
    for place in places:
        pl.semaphore_signal(barrier, inc=1, device_id=place, device_id_type=MESH)
    pl.semaphore_wait(barrier, len(places))


def tensor_near(t):
    y, z, c = t // (2 * Z), lax.rem(t // 2, Z), lax.rem(t, 2)
    ahead = [lax.rem(z + o, Z) for o in range(1, Z)]
    behind = [lax.rem(z + Z - o, Z) for o in range(1, Z)]
    place = lambda yy, zz, cc: yy * (2 * Z) + zz * 2 + cc
    return y, z, c, ahead, behind, place


def spot(t):
    return lax.rem(t, 2) * (2 * Z) + t // 2 if not isinstance(t, int) else t % 2 * (2 * Z) + t // 2


def farthest_first(t):
    y, z, c, ahead, _, place = tensor_near(t)
    chips = [(1 - y, ahead[1]), (1 - y, ahead[0]), (1 - y, ahead[2]), (1 - y, z)]
    chips += [(y, ahead[1]), (y, ahead[0]), (y, ahead[2])]
    return [place(yy, zz, cc) for yy, zz in chips for cc in (c, 1 - c)] + [place(y, z, 1 - c)]


def gather_blocks(buf, t, send, recv, use=lambda at, position: None):
    y, z, c, ahead, behind, place = tensor_near(t)
    other = place(y, z, 1 - c)
    to = [(1 - y, ahead[1]), (1 - y, ahead[0]), (1 - y, ahead[2]), (1 - y, z), (y, ahead[1]), (y, ahead[0]), (y, ahead[2])]
    own = spot(t)
    sent = []
    for role, (yy, zz) in enumerate(to):
        sent.append(remote(buf.at[own], buf.at[own], send.at[role], recv.at[role], tensor=place(yy, zz, c)))
        sent[-1].start()

    def core(yy, role):
        at = pl.ds((c * 2 + yy) * Z, Z)
        copy = remote(buf.at[at], buf.at[at], send.at[role], recv.at[role], tensor=other)
        copy.start()
        return copy

    def used(yy, zz, cc):
        position = place(yy, zz, cc)
        use(spot(position), position)

    used(y, z, c)
    for role in (5, 6, 4):
        sent[role].wait_recv()
    near = core(y, 7)
    for zz in behind:
        used(y, zz, c)
    for role in (3, 1, 2, 0):
        sent[role].wait_recv()
    far = core(1 - y, 8)
    for zz in [z] + behind:
        used(1 - y, zz, c)
    near.wait_recv()
    for zz in [z] + behind:
        used(y, zz, 1 - c)
    far.wait_recv()
    for zz in [z] + behind:
        used(1 - y, zz, 1 - c)
    for copy in sent + [near, far]:
        copy.wait_send()


def order(row, column, at0, at1, vocab):
    again = jnp.where((column == row) & (at0 < at1), 1.0, 0.0)
    once = 1.0 - jnp.max(again, axis=0, keepdims=True)
    floor = column - lax.rem(column, vocab)
    before = jnp.where((row >= floor) & (row < column), once, 0.0)
    return once, jnp.sum(before, axis=1, keepdims=True).astype(jnp.int32)


def lookup_kernel(ids_ref, start_ref, table_hbm, emb, table, all_ids, out_d, in_d, out_t, in_t, local, ids_send, ids_recv,
                  d_send, d_recv, t_send, t_recv, g_send, g_recv):
    groups, holders = in_d.shape[0], in_t.shape[0]
    steps, row_count = ids_ref.shape
    rows, vocab, width = steps * row_count, table.shape[0], table.shape[1]
    block = width // holders
    half = width // 2
    g, t = lax.axis_index("dp"), lax.axis_index("tensor")
    load = pltpu.make_async_copy(table_hbm, table, local.at[0])
    load.start()
    row = jnp.concatenate([ids_ref[s : s + 1] for s in range(steps)], axis=1)
    all_ids[g] = jnp.broadcast_to(row, (8, rows))
    others_d = [lax.rem(g + o, groups) for o in range(1, groups)]
    others_t = [lax.rem(t + o, holders) for o in range(1, holders)]
    greet([{"dp": d} for d in others_d] + [{"tensor": d} for d in others_t])
    moves = []
    for o, d in enumerate(others_d):
        moves.append(remote(all_ids.at[g], all_ids.at[g], ids_send.at[o], ids_recv.at[o], dp=d))
        moves[-1].start()

    start = start_ref[0:1, 0:1]
    column = jnp.broadcast_to(row, (8, rows)).astype(jnp.float32).T.astype(jnp.int32)[:, 0:1]
    at0 = lax.broadcasted_iota(jnp.int32, (rows, rows), 0)
    at1 = lax.broadcasted_iota(jnp.int32, (rows, rows), 1)

    slot = order(row, column, at0, at1, vocab)[1] - start
    holder = column // vocab
    from_t, from_g = lax.rem(holder, holders), holder // holders
    want = jnp.where((slot >= 0) & (slot < SLOTS), (from_t * groups + from_g) * SLOTS + slot, -1)
    candidates = holders * groups * SLOTS

    for copy in moves:
        copy.wait()

    ids_all = all_ids[0]
    at_g = lax.broadcasted_iota(jnp.int32, (8, rows), 0)
    for gg in range(1, groups):
        ids_all = jnp.where(at_g == gg, all_ids[gg], ids_all)
    columns = ids_all.astype(jnp.float32).T.astype(jnp.int32)
    base = (g * holders + t) * vocab
    at_v = lax.broadcasted_iota(jnp.int32, (rows, vocab), 1)
    pick_g = lax.broadcasted_iota(jnp.int32, (16, vocab), 0)
    held = jnp.zeros((16, vocab), jnp.float32)
    for gg in range(groups):
        asked = jnp.where(columns[:, gg : gg + 1] - base == at_v, 1.0, 0.0)
        held = jnp.where(pick_g == gg, jnp.max(asked, axis=0, keepdims=True), held)
    lower = jnp.where(
        lax.broadcasted_iota(jnp.int32, (vocab, vocab), 0) < lax.broadcasted_iota(jnp.int32, (vocab, vocab), 1),
        1.0,
        0.0,
    ).astype(jnp.bfloat16)
    rank = jnp.dot(held.astype(jnp.bfloat16), lower, preferred_element_type=jnp.float32).astype(jnp.int32) - start
    at_c = lax.broadcasted_iota(jnp.int32, (SLOTS, vocab), 0)
    chosen = jnp.concatenate(
        [
            jnp.where((rank[gg : gg + 1] == at_c) & (held[gg : gg + 1] > 0.5), 1.0, 0.0)
            for gg in range(groups)
        ],
        axis=0,
    ).astype(jnp.bfloat16)
    load.wait()
    step = 512
    for at in range(0, half, step):
        low = jnp.dot(chosen, table[:, at : at + step], preferred_element_type=jnp.float32)
        high = jnp.dot(chosen, table[:, half + at : half + at + step], preferred_element_type=jnp.float32)
        both = jnp.concatenate(
            [low.reshape(groups, SLOTS, step), high.reshape(groups, SLOTS, step)], axis=1
        )
        out_d[:, :, at : at + step] = both.astype(jnp.bfloat16)
    sent = []
    for o, d in enumerate(others_d):
        sent.append(remote(out_d.at[d], in_d.at[g], d_send.at[o], d_recv.at[o], dp=d))
        sent[-1].start()
    in_d[g] = out_d[g]
    select = jnp.where(
        want == lax.broadcasted_iota(jnp.int32, (rows, candidates), 1), 1.0, 0.0
    ).astype(jnp.bfloat16)
    permute = jnp.where(at1 == lax.rem(at0, steps) * row_count + at0 // steps, 1.0, 0.0).astype(jnp.bfloat16)
    select = jnp.dot(permute, select, preferred_element_type=jnp.float32).astype(jnp.bfloat16)
    for copy in sent:
        copy.wait()
    for o in range(holders):
        part, at = o // (holders // 2), (o % (holders // 2)) * block
        piece = in_d[:, :, at : at + block].astype(jnp.float32)[:, part * SLOTS : (part + 1) * SLOTS]
        out_t[o] = piece.reshape(groups * SLOTS, block).astype(jnp.bfloat16)
    sent = []
    for o, d in enumerate(others_t):
        sent.append(remote(out_t.at[d], in_t.at[t], t_send.at[o], t_recv.at[o], tensor=d))
        sent[-1].start()
    in_t[t] = out_t[t]
    for copy in sent:
        copy.wait()
    found = jnp.dot(select, in_t[...].reshape(candidates, block), preferred_element_type=jnp.float32)
    emb[spot(t)] = found.astype(jnp.bfloat16)
    gather_blocks(emb, t, g_send, g_recv)


def lookup(ids, table, groups, holders, start):
    rows = ids.shape[0] * ids.shape[1]
    vocab, width = table.shape
    block = width // holders
    bf16, dma = jnp.bfloat16, pltpu.SemaphoreType.DMA
    vmem, anywhere = pl.BlockSpec(memory_space=pltpu.VMEM), pl.BlockSpec(memory_space=pl.ANY)
    return pl.pallas_call(
        lookup_kernel,
        out_shape=jax.ShapeDtypeStruct((holders, rows, block), bf16),
        in_specs=[vmem, vmem, anywhere],
        out_specs=vmem,
        scratch_shapes=[
            pltpu.VMEM((vocab, width), bf16),
            pltpu.VMEM((groups, 8, rows), jnp.int32),
            pltpu.VMEM((groups, 2 * SLOTS, width // 2), bf16),
            pltpu.VMEM((groups, 2 * SLOTS, width // 2), bf16),
            pltpu.VMEM((holders, groups * SLOTS, block), bf16),
            pltpu.VMEM((holders, groups * SLOTS, block), bf16),
            dma((1,)),
            dma((groups - 1,)),
            dma((groups - 1,)),
            dma((groups - 1,)),
            dma((groups - 1,)),
            dma((holders - 1,)),
            dma((holders - 1,)),
            dma((holders - 1,)),
            dma((holders - 1,)),
        ],
        compiler_params=pltpu.CompilerParams(collective_id=1, has_side_effects=True, vmem_limit_bytes=40 * 2**20),
        name="lookup_round",
    )(ids, start, table)


def normalize(whole, gain, out):
    holders, rows, block = whole.shape
    squares = jnp.zeros((rows, block), jnp.float32)
    for k in range(holders):
        wide = whole[k].astype(jnp.float32)
        squares = squares + wide * wide
    scale = lax.rsqrt(jnp.sum(squares, axis=1, keepdims=True) / (holders * block) + epsilon)
    for k in range(holders):
        at = slice(k * block, (k + 1) * block)
        scaled = whole[spot(k)].astype(jnp.float32) * scale * gain[:, at]
        out[:, :, at] = scaled.reshape(out.shape[0], out.shape[1], block).astype(jnp.bfloat16)


def project_kernel(mixed, weight_hbm, emb, next_gain, stream, normed, whole, weight, out_c, in_c, kept, out_z, in_z, slab, out_y, in_y, local,
                   c_send, c_recv, z_send, z_recv, y_send, y_recv, g_send, g_recv):
    t = lax.axis_index("tensor")
    block = whole.shape[2]
    load = pltpu.make_async_copy(weight_hbm, weight, local.at[0])
    load.start()
    y, z, c, ahead, behind, place = tensor_near(t)
    other, across = place(y, z, 1 - c), place(1 - y, z, c)
    greet([{"tensor": other}, {"tensor": across}] + [{"tensor": place(y, zz, c)} for zz in ahead])

    load.wait()
    rows_in = mixed[...]

    def partial_of(k, cc):
        at = place(k % 2, k // 2, cc) * block
        return jnp.dot(rows_in, weight[:, pl.ds(pl.multiple_of(at, block), block)], preferred_element_type=jnp.float32)

    to_core = []
    for k in range(2 * Z):
        out_c[k] = partial_of(k, 1 - c).astype(jnp.bfloat16)
        to_core.append(remote(out_c.at[k], in_c.at[k], c_send.at[k], c_recv.at[k], tensor=other))
        to_core[-1].start()
    for k in range(2 * Z):
        kept[k // 2, k % 2] = partial_of(k, c)
    for k in range(2 * Z):
        to_core[k].wait_recv()
        total = kept[k // 2, k % 2] + in_c[k].astype(jnp.float32)
        kept[k // 2, k % 2] = total
        out_z[k // 2, k % 2] = total.astype(jnp.bfloat16)
    to_z = []
    for o in range(Z - 1):
        to_z.append(
            remote(out_z.at[ahead[o]], in_z.at[o], z_send.at[o], z_recv.at[o], tensor=place(y, ahead[o], c))
        )
        to_z[-1].start()
    total = kept[z]
    for o in range(Z - 1):
        to_z[o].wait_recv()
        total = total + in_z[o].astype(jnp.float32)
    slab[...] = total
    out_y[...] = slab[1 - y].astype(jnp.bfloat16)
    to_y = remote(out_y, in_y, y_send.at[0], y_recv.at[0], tensor=across)
    to_y.start()
    to_y.wait_recv()
    branch = slab[y] + in_y[...].astype(jnp.float32)
    mine = (emb[spot(t)].astype(jnp.float32) + branch).astype(jnp.bfloat16)
    stream[...] = mine.astype(jnp.float32).reshape(stream.shape).astype(jnp.bfloat16)
    whole[spot(t)] = mine
    gather_blocks(whole, t, g_send, g_recv)
    normalize(whole, next_gain, normed)
    for copy in to_core + to_z + [to_y]:
        copy.wait_send()


def project(mixed, weight, emb, next_gain, steps):
    holders, rows, block = emb.shape
    bf16, f32, dma = jnp.bfloat16, jnp.float32, pltpu.SemaphoreType.DMA
    vmem, anywhere = pl.BlockSpec(memory_space=pltpu.VMEM), pl.BlockSpec(memory_space=pl.ANY)
    return pl.pallas_call(
        project_kernel,
        out_shape=(
            jax.ShapeDtypeStruct((rows // steps, steps, block), bf16),
            jax.ShapeDtypeStruct((rows // steps, steps, holders * block), bf16),
        ),
        in_specs=[vmem, anywhere, vmem, vmem],
        out_specs=(vmem, vmem),
        scratch_shapes=[
            pltpu.VMEM((holders, rows, block), bf16),
            pltpu.VMEM(weight.shape, bf16),
            pltpu.VMEM((2 * Z, rows, block), bf16),
            pltpu.VMEM((2 * Z, rows, block), bf16),
            pltpu.VMEM((Z, 2, rows, block), f32),
            pltpu.VMEM((Z, 2, rows, block), bf16),
            pltpu.VMEM((Z - 1, 2, rows, block), bf16),
            pltpu.VMEM((2, rows, block), f32),
            pltpu.VMEM((rows, block), bf16),
            pltpu.VMEM((rows, block), bf16),
            dma((1,)),
            dma((2 * Z,)),
            dma((2 * Z,)),
            dma((Z - 1,)),
            dma((Z - 1,)),
            dma((1,)),
            dma((1,)),
            dma((holders - 1,)),
            dma((holders - 1,)),
        ],
        compiler_params=pltpu.CompilerParams(
            collective_id=2, has_side_effects=True, vmem_limit_bytes=40 * 2**20
        ),
        name="project",
    )(mixed, weight, emb, next_gain)


def readout(p, per, heads, steps, query, state, read):
    rows = read.shape[1]
    base = pl.multiple_of(p * (per * steps), per * steps)
    for h in range(heads):
        turned = pltpu.roll(query[h], lax.rem(rows - base, rows), 1)
        outs = []
        for i in range(per):
            old = state[p * per + i, h]
            for s in range(steps):
                lane = i * steps + s
                outs.append(jnp.sum(old * turned[:, lane : lane + 1], axis=0, keepdims=True))
        read[h, pl.ds(base, per * steps)] = jnp.concatenate(outs, axis=0)


def update(p, per, heads, steps, key, state, decay, xrow):
    rows = xrow.shape[1]
    base = pl.multiple_of(p * (per * steps), per * steps)
    for h in range(heads):
        turned = pltpu.roll(key[h], lax.rem(rows - base, rows), 1)
        for i in range(per):
            now = state[p * per + i, h]
            for s in range(steps):
                lane = i * steps + s
                now = decay[h, pl.ds(base + lane, 1)] * now + xrow[h, pl.ds(base + lane, 1)] * turned[:, lane : lane + 1]
            state[p * per + i, h] = now


def mix(h, proj, raw, bias, log_rate, columns, head_size, state_size, key, query, xin, xrow, decay):
    rows, at = proj.shape[0], h * columns
    value = raw[:, h : h + 1] + bias[h]
    size = jnp.maximum(value, 0.0) + jnp.log1p(jnp.exp(-jnp.abs(value)))
    rate = jnp.exp(-size * jnp.exp(jnp.full((rows, 1), log_rate[h], jnp.float32)))
    entry = proj[:, at : at + head_size]
    xin[h] = entry
    xrow[h] = size * entry
    decay[h] = jnp.broadcast_to(rate, (rows, head_size))
    at += 2 * head_size
    turned = proj[:, at : at + 2 * state_size].T
    key[h] = turned[:state_size]
    query[h] = turned[state_size:]


def close(h, steps, proj, skip, ngain, columns, head_size, state_size, xin, xrow, decay, read, mixed):
    at = h * columns
    rows = proj.shape[0]
    both = proj[:, at + 2 * head_size : at + 2 * head_size + 2 * state_size]
    queries = both[:, state_size:]
    step = lax.rem(lax.broadcasted_iota(jnp.int32, (rows, 1), 0), steps)
    rates, entry = decay[h], xrow[h]
    reach = rates
    out = jnp.sum(both[:, :state_size] * queries, axis=1, keepdims=True) * entry
    for back in range(1, steps):
        keys = pltpu.roll(both, back, 0)[:, :state_size]
        old = jnp.sum(keys * queries, axis=1, keepdims=True) * pltpu.roll(entry, back, 0)
        out = jnp.where(step >= back, out + reach * old, out)
        reach = jnp.where(step >= back, reach * pltpu.roll(rates, back, 0), reach)
    out = out + reach * read[h]
    out = out + skip[h] * xin[h]
    gate = proj[:, at + head_size : at + 2 * head_size]
    out = out * (gate / (1.0 + jnp.exp(-gate)))
    out = out * lax.rsqrt(jnp.mean(out * out, axis=1, keepdims=True) + epsilon)
    out = out * ngain[:, h * head_size : (h + 1) * head_size]
    mixed[:, h * head_size : (h + 1) * head_size] = out.astype(jnp.bfloat16)


def mixer_kernel(heads, emb, gain, weight_hbm, dtw, bias, log_rate, skip, ngain, state_hbm, new_hbm, mixed, weight, state, nrm, proj,
                 key, query, xin, xrow, decay, read, w_sem, s_sem, n_sem):
    holders, rows, block = emb.shape
    row_count, _, state_size, head_size = state.shape
    columns = weight.shape[1] // heads
    steps = rows // row_count
    parts = w_sem.shape[0]
    depth = weight.shape[0] // parts
    chunks = s_sem.shape[0]
    per = row_count // chunks
    loads = []
    for p in range(parts):
        at = pl.ds(p * depth, depth)
        loads.append(pltpu.make_async_copy(weight_hbm.at[at], weight.at[at], w_sem.at[p]))
        loads[-1].start()
    for p in range(chunks):
        at = pl.ds(p * per, per)
        pltpu.make_async_copy(state_hbm.at[at], state.at[at], s_sem.at[p]).start()

    squares = jnp.zeros((rows, block), jnp.float32)
    for k in range(holders):
        wide = emb[spot(k)].astype(jnp.float32)
        squares = squares + wide * wide
    scale = lax.rsqrt(jnp.sum(squares, axis=1, keepdims=True) / (holders * block) + epsilon)
    for k in range(holders):
        nrm[:, k * block : (k + 1) * block] = (emb[spot(k)].astype(jnp.float32) * scale * gain[:, k * block : (k + 1) * block]).astype(jnp.bfloat16)
    narrow = dtw[...].astype(jnp.float32)
    narrow = jnp.concatenate([narrow, jnp.zeros((16 - heads, narrow.shape[1]), jnp.float32)], axis=0).astype(jnp.bfloat16)
    steps_raw = lax.dot_general(nrm[...], narrow, (((1,), (1,)), ((), ())), preferred_element_type=jnp.float32)
    for p in range(parts):
        loads[p].wait()
        part = jnp.dot(nrm[:, p * depth : (p + 1) * depth], weight[p * depth : (p + 1) * depth],
                       preferred_element_type=jnp.float32)
        proj[...] = part if p == 0 else proj[...] + part

    sizes = (columns, head_size, state_size)
    for h in range(heads):
        mix(h, proj, steps_raw, bias, log_rate, *sizes, key, query, xin, xrow, decay)

    def chunk(p, carry):
        at = pl.ds(p * per, per)
        pltpu.make_async_copy(state_hbm.at[at], state.at[at], s_sem.at[p]).wait()
        readout(p, per, heads, steps, query, state, read)
        update(p, per, heads, steps, key, state, decay, xrow)
        pltpu.make_async_copy(state.at[at], new_hbm.at[at], n_sem.at[p]).start()
        return carry

    lax.fori_loop(0, chunks, chunk, 0)
    for h in range(heads):
        close(h, steps, proj, skip, ngain, *sizes, xin, xrow, decay, read, mixed)
    for p in range(chunks):
        at = pl.ds(p * per, per)
        pltpu.make_async_copy(state.at[at], new_hbm.at[at], n_sem.at[p]).wait()


def mixer(emb, gain, weight, dtw, bias, log_rate, skip, ngain, state):
    holders, rows, block = emb.shape
    row_count, heads, state_size, head_size = state.shape
    bf16, f32, dma = jnp.bfloat16, jnp.float32, pltpu.SemaphoreType.DMA
    vmem, anywhere = pl.BlockSpec(memory_space=pltpu.VMEM), pl.BlockSpec(memory_space=pl.ANY)
    smem = pl.BlockSpec(memory_space=pltpu.SMEM)
    return pl.pallas_call(
        functools.partial(mixer_kernel, heads),
        out_shape=(
            jax.ShapeDtypeStruct(state.shape, f32),
            jax.ShapeDtypeStruct((rows, heads * head_size), bf16),
        ),
        in_specs=[vmem, vmem, anywhere, vmem, smem, smem, smem, vmem, anywhere],
        out_specs=(anywhere, vmem),
        scratch_shapes=[
            pltpu.VMEM(weight.shape, bf16),
            pltpu.VMEM(state.shape, f32),
            pltpu.VMEM((rows, holders * block), bf16),
            pltpu.VMEM((rows, weight.shape[1]), f32),
            pltpu.VMEM((heads, state_size, rows), f32),
            pltpu.VMEM((heads, state_size, rows), f32),
            pltpu.VMEM((heads, rows, head_size), f32),
            pltpu.VMEM((heads, rows, head_size), f32),
            pltpu.VMEM((heads, rows, head_size), f32),
            pltpu.VMEM((heads, rows, head_size), f32),
            dma((4,)),
            dma((8,)),
            dma((8,)),
        ],
        compiler_params=pltpu.CompilerParams(vmem_limit_bytes=40 * 2**20),
        name="mixer",
    )(emb, gain, weight, dtw, bias, log_rate, skip, ngain, state)


def fused_kernel(heads, ids_in, table_hbm, trainer_hbm, gain, weight_hbm, dtw, bias, log_rate, skip, ngain,
                 state_hbm, oweight_hbm, next_gain, head_map, new_hbm, stream, normed, relaid, need, table,
                 gathered, swap, relaid_v, trainer, weight, state, oweight, all_ids, out_d, in_d, out_t, in_t,
                 out_r, in_r, emb, whole, swap_out, proj, narrow, raw, key, query, xin, xrow, decay, read, mixed,
                 out_c, in_c, kept, out_z, in_z, slab, slab_b, out_y, in_y, out_yb, in_yb, out_zb, in_zb, l_sem,
                 w_sem, s_sem, n_sem, m_sem, i_send, i_recv, d_send, d_recv, t_send, t_recv, r_send, r_recv, e_send,
                 e_recv, a_send, a_recv, x_send, x_recv, c_send, c_recv, z_send, z_recv, y_send, y_recv, g_send,
                 g_recv):
    bf16, f32 = jnp.bfloat16, jnp.float32
    groups, holders = in_d.shape[0], in_t.shape[0]
    vocab, width = table.shape
    rows, block = emb.shape[1], emb.shape[2]
    half = width // 2
    row_count, _, state_size, head_size = state.shape
    steps = rows // row_count
    trows = trainer.shape[0]
    g, t = lax.axis_index("dp"), lax.axis_index("tensor")
    y, z, c, ahead, behind, place = tensor_near(t)
    other, across = place(y, z, 1 - c), place(1 - y, z, c)
    x, low = g // 2, lax.rem(g, 2)
    beside = x * 2 + 1 - low
    x_ahead = [lax.rem(x + o, X) * 2 + low for o in range(1, X)]
    x_behind = [lax.rem(x + X - o, X) * 2 + low for o in range(1, X)]

    load_table = pltpu.make_async_copy(table_hbm, table, l_sem.at[0])
    load_table.start()
    load_trainer = pltpu.make_async_copy(trainer_hbm, trainer, l_sem.at[1])
    load_trainer.start()
    ids2 = ids_in[...]
    row = jnp.concatenate([ids2[s : s + 1] for s in range(steps)], axis=1)
    all_ids[g] = jnp.broadcast_to(row, (8, rows))
    others_d = [xx * 2 + 1 - low for xx in (lax.rem(x + 2, X), lax.rem(x + 1, X), lax.rem(x + 3, X))]
    others_d += [x_ahead[1], x_ahead[0], x_ahead[2], beside]
    others_t = farthest_first(t)
    greet([{"dp": d} for d in others_d] + [{"tensor": d} for d in others_t])
    moves = []
    for o, d in enumerate(others_d):
        moves.append(remote(all_ids.at[g], all_ids.at[g], i_send.at[o], i_recv.at[o], dp=d))
        moves[-1].start()

    load_oweight = pltpu.make_async_copy(oweight_hbm, oweight, l_sem.at[2])
    loads_w = [
        pltpu.make_async_copy(weight_hbm.at[pl.ds(k * block, block)], weight.at[k], w_sem.at[k])
        for k in range(holders)
    ]
    chunks = s_sem.shape[0]
    per = row_count // chunks

    def old_state(p):
        at = pl.ds(p * per, per)
        return pltpu.make_async_copy(state_hbm.at[at], state.at[at], s_sem.at[p])

    def fresh_state(p):
        at = pl.ds(p * per, per)
        return pltpu.make_async_copy(state.at[at], new_hbm.at[at], n_sem.at[p])

    load_trainer.wait()
    for o in range(holders):
        swap_out[o] = trainer[:, o * block : (o + 1) * block].astype(bf16)
    swaps = []
    for o, d in enumerate(others_t):
        swaps.append(remote(swap_out.at[d], gathered.at[g, t], a_send.at[o], a_recv.at[o], tensor=d))
        swaps[-1].start()
    gathered[g, t] = swap_out[t]
    for copy in loads_w + [load_oweight]:
        copy.start()
    for p in range(chunks):
        old_state(p).start()

    at0 = lax.broadcasted_iota(jnp.int32, (rows, rows), 0)
    at1 = lax.broadcasted_iota(jnp.int32, (rows, rows), 1)

    def turn(column):
        return jnp.broadcast_to(column.astype(f32), (rows, rows)).T[0:1].astype(jnp.int32)

    def places(row, column):
        once, slot = order(row, column, at0, at1, vocab)
        fits = jnp.where(turn(slot) < SLOTS, once, 0.0)
        column_t, row_t = lax.rem(column // vocab, holders), lax.rem(row // vocab, holders)
        before = jnp.where((row_t == column_t) & (row < column), fits, 0.0)
        return once, slot, jnp.sum(before, axis=1, keepdims=True).astype(jnp.int32)

    column = jnp.broadcast_to(row, (8, rows)).astype(f32).T.astype(jnp.int32)[:, 0:1]
    once, slot, index = places(row, column)
    from_t, from_g = lax.rem(column // vocab, holders), column // (vocab * holders)
    comes = (slot < SLOTS) & (index < WIDE)
    want = jnp.where(comes, from_t * WIDE + index, -1)
    select = jnp.where(want == lax.broadcasted_iota(jnp.int32, (rows, holders * WIDE), 1), 1.0, 0.0).astype(bf16)
    permute = jnp.where(at1 == lax.rem(at0, steps) * row_count + at0 // steps, 1.0, 0.0).astype(bf16)
    select = jnp.dot(permute, select, preferred_element_type=f32).astype(bf16)
    index_row = turn(jnp.where((from_t == t) & comes, index, -1))
    lift = jnp.where(
        (lax.broadcasted_iota(jnp.int32, (WIDE, rows), 0) == index_row) & (once > 0.5), 1.0, 0.0
    ).astype(bf16)
    lie = jnp.where(slot < SLOTS, from_g * (2 * SLOTS) + slot, -2 * SLOTS * groups)
    take_low = jnp.dot(lift, jnp.where(lie == at1, 1.0, 0.0).astype(bf16), preferred_element_type=f32).astype(bf16)
    take_high = jnp.dot(
        lift, jnp.where(lie + SLOTS == at1, 1.0, 0.0).astype(bf16), preferred_element_type=f32
    ).astype(bf16)
    lower = jnp.where(
        lax.broadcasted_iota(jnp.int32, (vocab, vocab), 0) < lax.broadcasted_iota(jnp.int32, (vocab, vocab), 1),
        1.0,
        0.0,
    ).astype(bf16)

    for copy in moves:
        copy.wait()
    ids_all = all_ids[0]
    at_g = lax.broadcasted_iota(jnp.int32, (8, rows), 0)
    for gg in range(1, groups):
        ids_all = jnp.where(at_g == gg, all_ids[gg], ids_all)
    columns = ids_all.astype(f32).T.astype(jnp.int32)
    base = (g * holders + t) * vocab
    at_v = lax.broadcasted_iota(jnp.int32, (rows, vocab), 1)
    pick_g = lax.broadcasted_iota(jnp.int32, (16, vocab), 0)
    held = jnp.zeros((16, vocab), f32)
    for gg in range(groups):
        asked = jnp.where(columns[:, gg : gg + 1] - base == at_v, 1.0, 0.0)
        held = jnp.where(pick_g == gg, jnp.max(asked, axis=0, keepdims=True), held)
    rank = jnp.dot(held.astype(bf16), lower, preferred_element_type=f32).astype(jnp.int32)
    at_c = lax.broadcasted_iota(jnp.int32, (SLOTS, vocab), 0)
    chosen = jnp.concatenate(
        [
            jnp.where((rank[gg : gg + 1] == at_c) & (held[gg : gg + 1] > 0.5), 1.0, 0.0)
            for gg in range(groups)
        ],
        axis=0,
    ).astype(bf16)
    load_table.wait()
    step = 512
    for at in range(0, half, step):
        left = jnp.dot(chosen, table[:, at : at + step], preferred_element_type=f32)
        right = jnp.dot(chosen, table[:, half + at : half + at + step], preferred_element_type=f32)
        both = jnp.concatenate(
            [left.reshape(groups, SLOTS, step), right.reshape(groups, SLOTS, step)], axis=1
        )
        out_d[:, :, at : at + step] = both.astype(bf16)
    sent = []
    for o, d in enumerate(others_d):
        sent.append(remote(out_d.at[d], in_d.at[g], d_send.at[o], d_recv.at[o], dp=d))
        sent[-1].start()
    in_d[g] = out_d[g]

    most = jnp.zeros((1, 1), jnp.int32)
    over = jnp.zeros((1, 1), jnp.int32)
    for gg in range(groups):
        _, slots, indices = places(all_ids[gg][0:1], columns[:, gg : gg + 1])
        most = jnp.maximum(most, jnp.max(slots, axis=0, keepdims=True))
        over = jnp.maximum(over, jnp.max(indices, axis=0, keepdims=True))
    todo = jnp.where((most >= SLOTS) | (over >= WIDE), most + 1, 0)
    need[0, 0] = todo[0, 0]
    units = heads * head_size
    maps = jnp.concatenate(
        [head_map[...].astype(f32), jnp.zeros((8 - heads, head_size), f32)], axis=0
    ).T.astype(jnp.int32)
    at_u = lax.broadcasted_iota(jnp.int32, (head_size, units), 1)
    for h in range(heads):
        swap[h * head_size : (h + 1) * head_size] = jnp.where(
            maps[:, h : h + 1] + h * head_size == at_u, 1.0, 0.0
        ).astype(bf16)
    for k in range(holders):
        thin = dtw[:, k * block : (k + 1) * block].astype(f32)
        narrow[k] = jnp.concatenate([thin, jnp.zeros((16 - heads, block), f32)], axis=0).astype(bf16)
    proj[...] = jnp.zeros_like(proj)
    raw[...] = jnp.zeros_like(raw)

    for copy in sent:
        copy.wait()
    arrived = in_d[...].reshape(groups * 2 * SLOTS, half)
    total = jnp.zeros((WIDE, block), f32)
    for part, take in enumerate((take_low, take_high)):
        for k in range(holders // 2):
            piece = jnp.dot(take, arrived[:, k * block : (k + 1) * block], preferred_element_type=f32)
            out_r[part * (holders // 2) + k] = piece.astype(bf16)
            total = total + piece * piece
    scale = lax.rsqrt(jnp.sum(total, axis=1, keepdims=True) / width + epsilon)
    for k in range(holders):
        scaled = out_r[k].astype(f32) * scale * gain[:, k * block : (k + 1) * block]
        out_t[k] = scaled.astype(bf16)
    sent = []
    for o, d in enumerate(others_t):
        sent.append(remote(out_t.at[d], in_t.at[t], t_send.at[o], t_recv.at[o], tensor=d))
        sent[-1].start()
    in_t[t] = out_t[t]

    shared = []

    def share(block_at, role, to):
        copy = remote(gathered.at[block_at], gathered.at[block_at], x_send.at[role], x_recv.at[role], dp=to)
        copy.start()
        shared.append(copy)
        return copy

    for copy in swaps:
        copy.wait()
    to_x = [share(g, 1 + o, x_ahead[o]) for o in range(X - 1)]

    def relay(at):
        piece = gathered[at].reshape(holders * trows, block)
        relaid_v[at] = lax.dot_general(swap[...], piece, (((1,), (1,)), ((), ())), preferred_element_type=f32)
        relaid_out(at).start()

    def relaid_out(at):
        wide = holders * trows
        columns = pl.ds(pl.multiple_of(at * wide, wide), wide)
        return pltpu.make_async_copy(relaid_v.at[at], relaid.at[:, columns], m_sem.at[at])


    for copy in sent:
        copy.wait()
    found = jnp.dot(select, in_t[...].reshape(holders * WIDE, block), preferred_element_type=f32)
    emb[spot(t)] = found.astype(bf16)

    def project_in(at, k):
        proj[...] += jnp.dot(emb[at], weight[k], preferred_element_type=f32)
        raw[...] += lax.dot_general(emb[at], narrow[k], (((1,), (1,)), ((), ())), preferred_element_type=f32)

    for copy in loads_w:
        copy.wait()
    gather_blocks(emb, t, e_send, e_recv, project_in)
    residual = []
    for o, d in enumerate(others_t):
        residual.append(remote(out_r.at[d], in_r.at[t], r_send.at[o], r_recv.at[o], tensor=d))
        residual[-1].start()
    in_r[t] = out_r[t]
    to_beside = share(g, 0, beside)
    sizes = (weight.shape[2] // heads, head_size, state_size)
    for h in range(heads):
        mix(h, proj, raw, bias, log_rate, *sizes, key, query, xin, xrow, decay)

    def look(p, carry):
        old_state(p).wait()
        readout(p, per, heads, steps, query, state, read)
        return carry

    lax.fori_loop(0, chunks, look, 0)
    for h in range(heads):
        close(h, steps, proj, skip, ngain, *sizes, xin, xrow, decay, read, mixed)

    load_oweight.wait()
    rows_in = mixed[...]

    def partial_of(yy, zz, cc):
        at = place(yy, zz, cc) * block
        return jnp.dot(rows_in, oweight[:, pl.ds(pl.multiple_of(at, block), block)], preferred_element_type=f32)

    to_core = []
    for n in range(2):
        for zz in range(Z // 2):
            for yy in range(2):
                out_c[n, zz, yy] = partial_of(yy, n * (Z // 2) + zz, 1 - c).astype(bf16)
        to_core.append(remote(out_c.at[n], in_c.at[n], c_send.at[n], c_recv.at[n], tensor=other))
        to_core[-1].start()
    for zz in range(Z):
        for yy in range(2):
            kept[zz, yy] = partial_of(yy, zz, c)
    cut = rows // 2
    for n in range(2):
        to_core[n].wait_recv()
        for zz in range(n * (Z // 2), (n + 1) * (Z // 2)):
            for yy in range(2):
                total = kept[zz, yy] + in_c[n, zz % (Z // 2), yy].astype(f32)
                kept[zz, yy] = total
                out_z[zz, yy] = total[:cut].astype(bf16)
                out_yb[yy, zz] = total[cut:].astype(bf16)
    to_yb = remote(out_yb.at[1 - y], in_yb, y_send.at[0], y_recv.at[0], tensor=across)
    to_yb.start()
    to_z = {}
    for o in (1, 0, 2):
        to_z[o] = remote(out_z.at[ahead[o]], in_z.at[o], z_send.at[o], z_recv.at[o], tensor=place(y, ahead[o], c))
        to_z[o].start()

    def move_on(p, carry):
        update(p, per, heads, steps, key, state, decay, xrow)
        fresh_state(p).start()
        return carry

    lax.fori_loop(0, chunks // 2, move_on, 0)
    to_beside.wait_recv()
    passed = [share(beside, X + o, x_ahead[o]) for o in range(X - 1)]
    relay(g)
    to_yb.wait_recv()
    for zz in range(Z):
        total = kept[zz, y, cut:] + in_yb[zz].astype(f32)
        slab_b[zz] = total
        out_zb[zz] = total.astype(bf16)
    to_zb = {}
    for o in (1, 0, 2):
        to_zb[o] = remote(
            out_zb.at[ahead[o]], in_zb.at[o], z_send.at[3 + o], z_recv.at[3 + o], tensor=place(y, ahead[o], c)
        )
        to_zb[o].start()
    total = kept[z, :, :cut]
    for o in (0, 2, 1):
        to_z[o].wait_recv()
        total = total + in_z[o].astype(f32)
    slab[...] = total
    out_y[...] = slab[1 - y].astype(bf16)
    to_y = remote(out_y, in_y, y_send.at[1], y_recv.at[1], tensor=across)
    to_y.start()
    lax.fori_loop(chunks // 2, chunks, move_on, 0)
    relay(beside)
    for o in range(X - 1):
        to_x[o].wait_recv()
        relay(x_behind[o])
    for copy in residual:
        copy.wait()
    embedded = jnp.dot(select, in_r[...].reshape(holders * WIDE, block), preferred_element_type=f32)
    total = slab_b[z]
    for o in (0, 2, 1):
        to_zb[o].wait_recv()
        total = total + in_zb[o].astype(f32)
    here = spot(t)
    whole[here, cut:] = (embedded[cut:] + total).astype(bf16)
    to_y.wait_recv()
    whole[here, :cut] = (embedded[:cut] + (slab[y] + in_y[...].astype(f32))).astype(bf16)
    stream[...] = whole[here].astype(f32).reshape(stream.shape).astype(bf16)
    gather_blocks(whole, t, g_send, g_recv)
    for o in range(X - 1):
        passed[o].wait_recv()
        relay(x_behind[o] + 1 - 2 * low)
    normalize(whole, next_gain, normed)
    for copy in to_core + list(to_z.values()) + list(to_zb.values()) + [to_yb, to_y] + shared:
        copy.wait_send()
    for at in range(groups):
        relaid_out(at).wait()
    for p in range(chunks):
        fresh_state(p).wait()


def fused(ids, table, trainer, gain, weight, dtw, bias, log_rate, skip, ngain, state, oweight, next_gain, head_map,
          groups, holders):
    row_count, heads, state_size, head_size = state.shape
    steps = ids.shape[0]
    rows = steps * ids.shape[1]
    vocab, width = table.shape
    block = width // holders
    trows = trainer.shape[0]
    units = heads * head_size
    cut = rows // 2
    columns = weight.shape[1]
    bf16, f32, dma = jnp.bfloat16, jnp.float32, pltpu.SemaphoreType.DMA
    vmem, anywhere = pl.BlockSpec(memory_space=pltpu.VMEM), pl.BlockSpec(memory_space=pl.ANY)
    smem = pl.BlockSpec(memory_space=pltpu.SMEM)
    buffers = [
        ((vocab, width), bf16),
        ((groups, holders, trows, block), bf16),
        ((units, units), bf16),
        ((groups, units, holders * trows), f32),
        (trainer.shape, f32),
        ((holders, block, columns), bf16),
        (state.shape, f32),
        (oweight.shape, bf16),
        ((groups, 8, rows), jnp.int32),
        ((groups, 2 * SLOTS, width // 2), bf16),
        ((groups, 2 * SLOTS, width // 2), bf16),
        ((holders, WIDE, block), bf16),
        ((holders, WIDE, block), bf16),
        ((holders, WIDE, block), bf16),
        ((holders, WIDE, block), bf16),
        ((holders, rows, block), bf16),
        ((holders, rows, block), bf16),
        ((holders, trows, block), bf16),
        ((rows, columns), f32),
        ((holders, 16, block), bf16),
        ((rows, 16), f32),
        ((heads, state_size, rows), f32),
        ((heads, state_size, rows), f32),
        ((heads, rows, head_size), f32),
        ((heads, rows, head_size), f32),
        ((heads, rows, head_size), f32),
        ((heads, rows, head_size), f32),
        ((rows, units), bf16),
        ((2, Z // 2, 2, rows, block), bf16),
        ((2, Z // 2, 2, rows, block), bf16),
        ((Z, 2, rows, block), f32),
        ((Z, 2, cut, block), bf16),
        ((Z - 1, 2, cut, block), bf16),
        ((2, cut, block), f32),
        ((Z, cut, block), f32),
        ((cut, block), bf16),
        ((cut, block), bf16),
        ((2, Z, cut, block), bf16),
        ((Z, cut, block), bf16),
        ((Z, cut, block), bf16),
        ((Z - 1, cut, block), bf16),
    ]
    semaphores = [3, holders, 8, 8, groups]
    for count in (groups - 1, groups - 1, holders - 1, holders - 1, holders - 1, holders - 1, 2 * X - 1):
        semaphores += [count, count]
    for count in (2, 2 * (Z - 1), 2, holders - 1):
        semaphores += [count, count]
    return pl.pallas_call(
        functools.partial(fused_kernel, heads),
        out_shape=(
            jax.ShapeDtypeStruct(state.shape, f32),
            jax.ShapeDtypeStruct((row_count, steps, block), bf16),
            jax.ShapeDtypeStruct((row_count, steps, width), bf16),
            jax.ShapeDtypeStruct((units, width), f32),
            jax.ShapeDtypeStruct((1, 1), jnp.int32),
        ),
        in_specs=[vmem, anywhere, anywhere, vmem, anywhere, vmem, smem, smem, smem, vmem, anywhere, anywhere, vmem, vmem],
        out_specs=(anywhere, vmem, vmem, anywhere, smem),
        scratch_shapes=[pltpu.VMEM(*buffer) for buffer in buffers] + [dma((count,)) for count in semaphores],
        compiler_params=pltpu.CompilerParams(
            collective_id=0, has_side_effects=True, vmem_limit_bytes=60 * 2**20
        ),
        name="fused",
    )(ids, table, trainer, gain, weight, dtw, bias, log_rate, skip, ngain, state, oweight, next_gain, head_map)


def per_device(
    token_ids,
    embed_table,
    in_gain,
    in_weight,
    dt_weight,
    dt_bias,
    a_log,
    d_skip,
    norm_gain,
    out_weight,
    next_gain,
    ssm_state,
    trainer_weight,
    head_map,
):
    row_count, step_count = token_ids.shape
    width = embed_table.shape[1]
    holders = lax.axis_size("tensor")
    groups = lax.axis_size("dp")
    rows = row_count * step_count
    state = ssm_state.swapaxes(2, 3)
    gain, ngain, ngain_next = in_gain.reshape(1, -1), norm_gain.reshape(1, -1), next_gain.reshape(1, -1)
    mix = (in_weight, dt_weight.T, dt_bias, a_log, d_skip, ngain, state)
    now, stream, normed, relaid, need = fused(
        token_ids.T, embed_table, trainer_weight, gain, *mix, out_weight, ngain_next, head_map, groups, holders
    )

    def again(carry):
        todo = carry[0]

        def more(inner):
            done, held = inner
            return done + SLOTS, held + lookup(token_ids.T, embed_table, groups, holders, jnp.full((8, 128), done, jnp.int32))

        empty = jnp.zeros((holders, rows, width // holders), jnp.bfloat16)
        _, emb = lax.while_loop(lambda inner: inner[0] < todo, more, (jnp.int32(0), empty))
        now, mixed = mixer(emb, gain, *mix)
        stream, normed = project(mixed, out_weight, emb, ngain_next, step_count)
        return jnp.int32(0), now, stream, normed

    _, now, stream, normed = lax.while_loop(
        lambda carry: carry[0] > 0, again, (need.reshape(()), now, stream, normed)
    )
    return (
        now.swapaxes(2, 3),
        stream,
        normed,
        relaid,
    )


def solution(mesh):
    placed = (
        P("dp", None),
        P(("dp", "tensor"), None),
        P(),
        P(None, "tensor"),
        P(None, "tensor"),
        P("tensor"),
        P("tensor"),
        P("tensor"),
        P("tensor"),
        P("tensor", None),
        P(),
        P("dp", "tensor", None, None),
        P(("dp", "tensor"), None),
        P("tensor", None),
    )
    return jax.shard_map(
        per_device,
        mesh=mesh,
        in_specs=placed,
        out_specs=(
            P("dp", "tensor", None, None),
            P("dp", None, "tensor"),
            P("dp", None, None),
            P("tensor", None),
        ),
        check_vma=False,
    )
```

```python
import functools
import jax
import jax.numpy as jnp
from jax import lax
from jax.experimental import pallas as pl
from jax.experimental.pallas import tpu as pltpu
from jax.sharding import PartitionSpec as P

epsilon = 1e-05
MESH = pl.DeviceIdType.MESH
SLOTS = 8
WIDE = 32
Z = 4
X = 4


def remote(src, dst, send_sem, recv_sem, **place):
    return pltpu.make_async_remote_copy(
        src_ref=src,
        dst_ref=dst,
        send_sem=send_sem,
        recv_sem=recv_sem,
        device_id=place,
        device_id_type=MESH,
    )


def greet(places):
    barrier = pltpu.get_barrier_semaphore()
    for place in places:
        pl.semaphore_signal(barrier, inc=1, device_id=place, device_id_type=MESH)
    pl.semaphore_wait(barrier, len(places))


def tensor_near(t):
    y, z, c = t // (2 * Z), lax.rem(t // 2, Z), lax.rem(t, 2)
    ahead = [lax.rem(z + o, Z) for o in range(1, Z)]
    behind = [lax.rem(z + Z - o, Z) for o in range(1, Z)]
    place = lambda yy, zz, cc: yy * (2 * Z) + zz * 2 + cc
    return y, z, c, ahead, behind, place


def spot(t):
    return lax.rem(t, 2) * (2 * Z) + t // 2 if not isinstance(t, int) else t % 2 * (2 * Z) + t // 2


def farthest_first(t):
    y, z, c, ahead, _, place = tensor_near(t)
    chips = [(1 - y, ahead[1]), (1 - y, ahead[0]), (1 - y, ahead[2]), (1 - y, z)]
    chips += [(y, ahead[1]), (y, ahead[0]), (y, ahead[2])]
    return [place(yy, zz, cc) for yy, zz in chips for cc in (c, 1 - c)] + [place(y, z, 1 - c)]


def gather_blocks(buf, t, send, recv, use=lambda at, position: None, meanwhile=lambda: None):
    y, z, c, ahead, behind, place = tensor_near(t)
    other = place(y, z, 1 - c)
    to = [(1 - y, ahead[1]), (1 - y, ahead[0]), (1 - y, ahead[2]), (1 - y, z), (y, ahead[1]), (y, ahead[0]), (y, ahead[2])]
    own = spot(t)
    sent = []
    for role, (yy, zz) in enumerate(to):
        sent.append(remote(buf.at[own], buf.at[own], send.at[role], recv.at[role], tensor=place(yy, zz, c)))
        sent[-1].start()

    def core(yy, role):
        at = pl.ds((c * 2 + yy) * Z, Z)
        copy = remote(buf.at[at], buf.at[at], send.at[role], recv.at[role], tensor=other)
        copy.start()
        return copy

    def used(yy, zz, cc):
        position = place(yy, zz, cc)
        use(spot(position), position)

    meanwhile()
    used(y, z, c)
    for role in (5, 6, 4):
        sent[role].wait_recv()
    near = core(y, 7)
    for zz in behind:
        used(y, zz, c)
    for role in (3, 1, 2, 0):
        sent[role].wait_recv()
    far = core(1 - y, 8)
    for zz in [z] + behind:
        used(1 - y, zz, c)
    near.wait_recv()
    for zz in [z] + behind:
        used(y, zz, 1 - c)
    far.wait_recv()
    for zz in [z] + behind:
        used(1 - y, zz, 1 - c)
    return sent + [near, far]


def order(row, column, at0, at1, vocab):
    again = jnp.where((column == row) & (at0 < at1), 1.0, 0.0)
    once = 1.0 - jnp.max(again, axis=0, keepdims=True)
    floor = column - lax.rem(column, vocab)
    before = jnp.where((row >= floor) & (row < column), once, 0.0)
    return once, jnp.sum(before, axis=1, keepdims=True).astype(jnp.int32)


def lookup_kernel(ids_ref, start_ref, table_hbm, emb, table, all_ids, out_d, in_d, out_t, in_t, local, ids_send, ids_recv,
                  d_send, d_recv, t_send, t_recv, g_send, g_recv):
    groups, holders = in_d.shape[0], in_t.shape[0]
    steps, row_count = ids_ref.shape
    rows, vocab, width = steps * row_count, table.shape[0], table.shape[1]
    block = width // holders
    half = width // 2
    g, t = lax.axis_index("dp"), lax.axis_index("tensor")
    load = pltpu.make_async_copy(table_hbm, table, local.at[0])
    load.start()
    row = jnp.concatenate([ids_ref[s : s + 1] for s in range(steps)], axis=1)
    all_ids[g] = jnp.broadcast_to(row, (8, rows))
    others_d = [lax.rem(g + o, groups) for o in range(1, groups)]
    others_t = [lax.rem(t + o, holders) for o in range(1, holders)]
    greet([{"dp": d} for d in others_d] + [{"tensor": d} for d in others_t])
    moves = []
    for o, d in enumerate(others_d):
        moves.append(remote(all_ids.at[g], all_ids.at[g], ids_send.at[o], ids_recv.at[o], dp=d))
        moves[-1].start()

    start = start_ref[0:1, 0:1]
    column = jnp.broadcast_to(row, (8, rows)).astype(jnp.float32).T.astype(jnp.int32)[:, 0:1]
    at0 = lax.broadcasted_iota(jnp.int32, (rows, rows), 0)
    at1 = lax.broadcasted_iota(jnp.int32, (rows, rows), 1)

    slot = order(row, column, at0, at1, vocab)[1] - start
    holder = column // vocab
    from_t, from_g = lax.rem(holder, holders), holder // holders
    want = jnp.where((slot >= 0) & (slot < SLOTS), (from_t * groups + from_g) * SLOTS + slot, -1)
    candidates = holders * groups * SLOTS

    for copy in moves:
        copy.wait()

    ids_all = all_ids[0]
    at_g = lax.broadcasted_iota(jnp.int32, (8, rows), 0)
    for gg in range(1, groups):
        ids_all = jnp.where(at_g == gg, all_ids[gg], ids_all)
    columns = ids_all.astype(jnp.float32).T.astype(jnp.int32)
    base = (g * holders + t) * vocab
    at_v = lax.broadcasted_iota(jnp.int32, (rows, vocab), 1)
    pick_g = lax.broadcasted_iota(jnp.int32, (16, vocab), 0)
    held = jnp.zeros((16, vocab), jnp.float32)
    for gg in range(groups):
        asked = jnp.where(columns[:, gg : gg + 1] - base == at_v, 1.0, 0.0)
        held = jnp.where(pick_g == gg, jnp.max(asked, axis=0, keepdims=True), held)
    lower = jnp.where(
        lax.broadcasted_iota(jnp.int32, (vocab, vocab), 0) < lax.broadcasted_iota(jnp.int32, (vocab, vocab), 1),
        1.0,
        0.0,
    ).astype(jnp.bfloat16)
    rank = jnp.dot(held.astype(jnp.bfloat16), lower, preferred_element_type=jnp.float32).astype(jnp.int32) - start
    at_c = lax.broadcasted_iota(jnp.int32, (SLOTS, vocab), 0)
    chosen = jnp.concatenate(
        [
            jnp.where((rank[gg : gg + 1] == at_c) & (held[gg : gg + 1] > 0.5), 1.0, 0.0)
            for gg in range(groups)
        ],
        axis=0,
    ).astype(jnp.bfloat16)
    load.wait()
    step = 512
    for at in range(0, half, step):
        low = jnp.dot(chosen, table[:, at : at + step], preferred_element_type=jnp.float32)
        high = jnp.dot(chosen, table[:, half + at : half + at + step], preferred_element_type=jnp.float32)
        both = jnp.concatenate(
            [low.reshape(groups, SLOTS, step), high.reshape(groups, SLOTS, step)], axis=1
        )
        out_d[:, :, at : at + step] = both.astype(jnp.bfloat16)
    sent = []
    for o, d in enumerate(others_d):
        sent.append(remote(out_d.at[d], in_d.at[g], d_send.at[o], d_recv.at[o], dp=d))
        sent[-1].start()
    in_d[g] = out_d[g]
    select = jnp.where(
        want == lax.broadcasted_iota(jnp.int32, (rows, candidates), 1), 1.0, 0.0
    ).astype(jnp.bfloat16)
    permute = jnp.where(at1 == lax.rem(at0, steps) * row_count + at0 // steps, 1.0, 0.0).astype(jnp.bfloat16)
    select = jnp.dot(permute, select, preferred_element_type=jnp.float32).astype(jnp.bfloat16)
    for copy in sent:
        copy.wait()
    for o in range(holders):
        part, at = o // (holders // 2), (o % (holders // 2)) * block
        piece = in_d[:, :, at : at + block].astype(jnp.float32)[:, part * SLOTS : (part + 1) * SLOTS]
        out_t[o] = piece.reshape(groups * SLOTS, block).astype(jnp.bfloat16)
    sent = []
    for o, d in enumerate(others_t):
        sent.append(remote(out_t.at[d], in_t.at[t], t_send.at[o], t_recv.at[o], tensor=d))
        sent[-1].start()
    in_t[t] = out_t[t]
    for copy in sent:
        copy.wait()
    found = jnp.dot(select, in_t[...].reshape(candidates, block), preferred_element_type=jnp.float32)
    emb[spot(t)] = found.astype(jnp.bfloat16)
    for copy in gather_blocks(emb, t, g_send, g_recv):
        copy.wait_send()


def lookup(ids, table, groups, holders, start):
    rows = ids.shape[0] * ids.shape[1]
    vocab, width = table.shape
    block = width // holders
    bf16, dma = jnp.bfloat16, pltpu.SemaphoreType.DMA
    vmem, anywhere = pl.BlockSpec(memory_space=pltpu.VMEM), pl.BlockSpec(memory_space=pl.ANY)
    return pl.pallas_call(
        lookup_kernel,
        out_shape=jax.ShapeDtypeStruct((holders, rows, block), bf16),
        in_specs=[vmem, vmem, anywhere],
        out_specs=vmem,
        scratch_shapes=[
            pltpu.VMEM((vocab, width), bf16),
            pltpu.VMEM((groups, 8, rows), jnp.int32),
            pltpu.VMEM((groups, 2 * SLOTS, width // 2), bf16),
            pltpu.VMEM((groups, 2 * SLOTS, width // 2), bf16),
            pltpu.VMEM((holders, groups * SLOTS, block), bf16),
            pltpu.VMEM((holders, groups * SLOTS, block), bf16),
            dma((1,)),
            dma((groups - 1,)),
            dma((groups - 1,)),
            dma((groups - 1,)),
            dma((groups - 1,)),
            dma((holders - 1,)),
            dma((holders - 1,)),
            dma((holders - 1,)),
            dma((holders - 1,)),
        ],
        compiler_params=pltpu.CompilerParams(collective_id=1, has_side_effects=True, vmem_limit_bytes=40 * 2**20),
        name="lookup_round",
    )(ids, start, table)


def normalize(whole, gain, out):
    holders, rows, block = whole.shape
    squares = jnp.zeros((rows, block), jnp.float32)
    for k in range(holders):
        wide = whole[k].astype(jnp.float32)
        squares = squares + wide * wide
    scale = lax.rsqrt(jnp.sum(squares, axis=1, keepdims=True) / (holders * block) + epsilon)
    for k in range(holders):
        at = slice(k * block, (k + 1) * block)
        scaled = whole[spot(k)].astype(jnp.float32) * scale * gain[:, at]
        out[:, :, at] = scaled.reshape(out.shape[0], out.shape[1], block).astype(jnp.bfloat16)


def project_kernel(mixed, weight_hbm, emb, next_gain, stream, normed, whole, weight, out_c, in_c, kept, out_z, in_z, slab, out_y, in_y, local,
                   c_send, c_recv, z_send, z_recv, y_send, y_recv, g_send, g_recv):
    t = lax.axis_index("tensor")
    block = whole.shape[2]
    load = pltpu.make_async_copy(weight_hbm, weight, local.at[0])
    load.start()
    y, z, c, ahead, behind, place = tensor_near(t)
    other, across = place(y, z, 1 - c), place(1 - y, z, c)
    greet([{"tensor": other}, {"tensor": across}] + [{"tensor": place(y, zz, c)} for zz in ahead])

    load.wait()
    rows_in = mixed[...]

    def partial_of(k, cc):
        at = place(k % 2, k // 2, cc) * block
        return jnp.dot(rows_in, weight[:, pl.ds(pl.multiple_of(at, block), block)], preferred_element_type=jnp.float32)

    to_core = []
    for k in range(2 * Z):
        out_c[k] = partial_of(k, 1 - c).astype(jnp.bfloat16)
        to_core.append(remote(out_c.at[k], in_c.at[k], c_send.at[k], c_recv.at[k], tensor=other))
        to_core[-1].start()
    for k in range(2 * Z):
        kept[k // 2, k % 2] = partial_of(k, c)
    for k in range(2 * Z):
        to_core[k].wait_recv()
        total = kept[k // 2, k % 2] + in_c[k].astype(jnp.float32)
        kept[k // 2, k % 2] = total
        out_z[k // 2, k % 2] = total.astype(jnp.bfloat16)
    to_z = []
    for o in range(Z - 1):
        to_z.append(
            remote(out_z.at[ahead[o]], in_z.at[o], z_send.at[o], z_recv.at[o], tensor=place(y, ahead[o], c))
        )
        to_z[-1].start()
    total = kept[z]
    for o in range(Z - 1):
        to_z[o].wait_recv()
        total = total + in_z[o].astype(jnp.float32)
    slab[...] = total
    out_y[...] = slab[1 - y].astype(jnp.bfloat16)
    to_y = remote(out_y, in_y, y_send.at[0], y_recv.at[0], tensor=across)
    to_y.start()
    to_y.wait_recv()
    branch = slab[y] + in_y[...].astype(jnp.float32)
    mine = (emb[spot(t)].astype(jnp.float32) + branch).astype(jnp.bfloat16)
    stream[...] = mine.astype(jnp.float32).reshape(stream.shape).astype(jnp.bfloat16)
    whole[spot(t)] = mine
    spread = gather_blocks(whole, t, g_send, g_recv)
    normalize(whole, next_gain, normed)
    for copy in to_core + to_z + [to_y] + spread:
        copy.wait_send()


def project(mixed, weight, emb, next_gain, steps):
    holders, rows, block = emb.shape
    bf16, f32, dma = jnp.bfloat16, jnp.float32, pltpu.SemaphoreType.DMA
    vmem, anywhere = pl.BlockSpec(memory_space=pltpu.VMEM), pl.BlockSpec(memory_space=pl.ANY)
    return pl.pallas_call(
        project_kernel,
        out_shape=(
            jax.ShapeDtypeStruct((rows // steps, steps, block), bf16),
            jax.ShapeDtypeStruct((rows // steps, steps, holders * block), bf16),
        ),
        in_specs=[vmem, anywhere, vmem, vmem],
        out_specs=(vmem, vmem),
        scratch_shapes=[
            pltpu.VMEM((holders, rows, block), bf16),
            pltpu.VMEM(weight.shape, bf16),
            pltpu.VMEM((2 * Z, rows, block), bf16),
            pltpu.VMEM((2 * Z, rows, block), bf16),
            pltpu.VMEM((Z, 2, rows, block), f32),
            pltpu.VMEM((Z, 2, rows, block), bf16),
            pltpu.VMEM((Z - 1, 2, rows, block), bf16),
            pltpu.VMEM((2, rows, block), f32),
            pltpu.VMEM((rows, block), bf16),
            pltpu.VMEM((rows, block), bf16),
            dma((1,)),
            dma((2 * Z,)),
            dma((2 * Z,)),
            dma((Z - 1,)),
            dma((Z - 1,)),
            dma((1,)),
            dma((1,)),
            dma((holders - 1,)),
            dma((holders - 1,)),
        ],
        compiler_params=pltpu.CompilerParams(
            collective_id=2, has_side_effects=True, vmem_limit_bytes=40 * 2**20
        ),
        name="project",
    )(mixed, weight, emb, next_gain)


def readout(p, per, heads, steps, query, state, read):
    rows = read.shape[1]
    base = pl.multiple_of(p * (per * steps), per * steps)
    for h in range(heads):
        turned = pltpu.roll(query[h], lax.rem(rows - base, rows), 1)
        outs = []
        for i in range(per):
            old = state[p * per + i, h]
            for s in range(steps):
                lane = i * steps + s
                outs.append(jnp.sum(old * turned[:, lane : lane + 1], axis=0, keepdims=True))
        read[h, pl.ds(base, per * steps)] = jnp.concatenate(outs, axis=0)


def update(p, per, heads, steps, key, state, decay, xrow):
    rows = xrow.shape[1]
    base = pl.multiple_of(p * (per * steps), per * steps)
    for h in range(heads):
        turned = pltpu.roll(key[h], lax.rem(rows - base, rows), 1)
        for i in range(per):
            now = state[p * per + i, h]
            for s in range(steps):
                lane = i * steps + s
                now = decay[h, pl.ds(base + lane, 1)] * now + xrow[h, pl.ds(base + lane, 1)] * turned[:, lane : lane + 1]
            state[p * per + i, h] = now


def mix(h, proj, raw, bias, log_rate, columns, head_size, state_size, key, query, xin, xrow, decay):
    rows, at = proj.shape[0], h * columns
    value = raw[:, h : h + 1] + bias[h]
    size = jnp.maximum(value, 0.0) + jnp.log1p(jnp.exp(-jnp.abs(value)))
    rate = jnp.exp(-size * jnp.exp(jnp.full((rows, 1), log_rate[h], jnp.float32)))
    entry = proj[:, at : at + head_size]
    xin[h] = entry
    xrow[h] = size * entry
    decay[h] = jnp.broadcast_to(rate, (rows, head_size))
    at += 2 * head_size
    turned = proj[:, at : at + 2 * state_size].T
    key[h] = turned[:state_size]
    query[h] = turned[state_size:]


def close(h, steps, proj, skip, ngain, columns, head_size, state_size, xin, xrow, decay, read, mixed):
    at = h * columns
    rows = proj.shape[0]
    both = proj[:, at + 2 * head_size : at + 2 * head_size + 2 * state_size]
    queries = both[:, state_size:]
    step = lax.rem(lax.broadcasted_iota(jnp.int32, (rows, 1), 0), steps)
    rates, entry = decay[h], xrow[h]
    reach = rates
    out = jnp.sum(both[:, :state_size] * queries, axis=1, keepdims=True) * entry
    for back in range(1, steps):
        keys = pltpu.roll(both, back, 0)[:, :state_size]
        old = jnp.sum(keys * queries, axis=1, keepdims=True) * pltpu.roll(entry, back, 0)
        out = jnp.where(step >= back, out + reach * old, out)
        reach = jnp.where(step >= back, reach * pltpu.roll(rates, back, 0), reach)
    out = out + reach * read[h]
    out = out + skip[h] * xin[h]
    gate = proj[:, at + head_size : at + 2 * head_size]
    out = out * (gate / (1.0 + jnp.exp(-gate)))
    out = out * lax.rsqrt(jnp.mean(out * out, axis=1, keepdims=True) + epsilon)
    out = out * ngain[:, h * head_size : (h + 1) * head_size]
    mixed[:, h * head_size : (h + 1) * head_size] = out.astype(jnp.bfloat16)


def mixer_kernel(heads, emb, gain, weight_hbm, dtw, bias, log_rate, skip, ngain, state_hbm, new_hbm, mixed, weight, state, nrm, proj,
                 key, query, xin, xrow, decay, read, w_sem, s_sem, n_sem):
    holders, rows, block = emb.shape
    row_count, _, state_size, head_size = state.shape
    columns = weight.shape[1] // heads
    steps = rows // row_count
    parts = w_sem.shape[0]
    depth = weight.shape[0] // parts
    chunks = s_sem.shape[0]
    per = row_count // chunks
    loads = []
    for p in range(parts):
        at = pl.ds(p * depth, depth)
        loads.append(pltpu.make_async_copy(weight_hbm.at[at], weight.at[at], w_sem.at[p]))
        loads[-1].start()
    for p in range(chunks):
        at = pl.ds(p * per, per)
        pltpu.make_async_copy(state_hbm.at[at], state.at[at], s_sem.at[p]).start()

    squares = jnp.zeros((rows, block), jnp.float32)
    for k in range(holders):
        wide = emb[spot(k)].astype(jnp.float32)
        squares = squares + wide * wide
    scale = lax.rsqrt(jnp.sum(squares, axis=1, keepdims=True) / (holders * block) + epsilon)
    for k in range(holders):
        nrm[:, k * block : (k + 1) * block] = (emb[spot(k)].astype(jnp.float32) * scale * gain[:, k * block : (k + 1) * block]).astype(jnp.bfloat16)
    narrow = dtw[...].astype(jnp.float32)
    narrow = jnp.concatenate([narrow, jnp.zeros((16 - heads, narrow.shape[1]), jnp.float32)], axis=0).astype(jnp.bfloat16)
    steps_raw = lax.dot_general(nrm[...], narrow, (((1,), (1,)), ((), ())), preferred_element_type=jnp.float32)
    for p in range(parts):
        loads[p].wait()
        part = jnp.dot(nrm[:, p * depth : (p + 1) * depth], weight[p * depth : (p + 1) * depth],
                       preferred_element_type=jnp.float32)
        proj[...] = part if p == 0 else proj[...] + part

    sizes = (columns, head_size, state_size)
    for h in range(heads):
        mix(h, proj, steps_raw, bias, log_rate, *sizes, key, query, xin, xrow, decay)

    def chunk(p, carry):
        at = pl.ds(p * per, per)
        pltpu.make_async_copy(state_hbm.at[at], state.at[at], s_sem.at[p]).wait()
        readout(p, per, heads, steps, query, state, read)
        update(p, per, heads, steps, key, state, decay, xrow)
        pltpu.make_async_copy(state.at[at], new_hbm.at[at], n_sem.at[p]).start()
        return carry

    lax.fori_loop(0, chunks, chunk, 0)
    for h in range(heads):
        close(h, steps, proj, skip, ngain, *sizes, xin, xrow, decay, read, mixed)
    for p in range(chunks):
        at = pl.ds(p * per, per)
        pltpu.make_async_copy(state.at[at], new_hbm.at[at], n_sem.at[p]).wait()


def mixer(emb, gain, weight, dtw, bias, log_rate, skip, ngain, state):
    holders, rows, block = emb.shape
    row_count, heads, state_size, head_size = state.shape
    bf16, f32, dma = jnp.bfloat16, jnp.float32, pltpu.SemaphoreType.DMA
    vmem, anywhere = pl.BlockSpec(memory_space=pltpu.VMEM), pl.BlockSpec(memory_space=pl.ANY)
    smem = pl.BlockSpec(memory_space=pltpu.SMEM)
    return pl.pallas_call(
        functools.partial(mixer_kernel, heads),
        out_shape=(
            jax.ShapeDtypeStruct(state.shape, f32),
            jax.ShapeDtypeStruct((rows, heads * head_size), bf16),
        ),
        in_specs=[vmem, vmem, anywhere, vmem, smem, smem, smem, vmem, anywhere],
        out_specs=(anywhere, vmem),
        scratch_shapes=[
            pltpu.VMEM(weight.shape, bf16),
            pltpu.VMEM(state.shape, f32),
            pltpu.VMEM((rows, holders * block), bf16),
            pltpu.VMEM((rows, weight.shape[1]), f32),
            pltpu.VMEM((heads, state_size, rows), f32),
            pltpu.VMEM((heads, state_size, rows), f32),
            pltpu.VMEM((heads, rows, head_size), f32),
            pltpu.VMEM((heads, rows, head_size), f32),
            pltpu.VMEM((heads, rows, head_size), f32),
            pltpu.VMEM((heads, rows, head_size), f32),
            dma((4,)),
            dma((8,)),
            dma((8,)),
        ],
        compiler_params=pltpu.CompilerParams(vmem_limit_bytes=40 * 2**20),
        name="mixer",
    )(emb, gain, weight, dtw, bias, log_rate, skip, ngain, state)


def fused_kernel(heads, ids_in, table_hbm, trainer_hbm, gain, weight_hbm, dtw, bias, log_rate, skip, ngain,
                 state_hbm, oweight_hbm, next_gain, head_map, new_hbm, stream, normed, gathered_out, swap, need,
                 table, gathered, trainer, weight, state, oweight, all_ids, out_d, in_d, out_t, in_t, out_r, in_r,
                 emb, whole, swap_out, proj, narrow, raw, key, query, xin, xrow, decay, read, mixed, out_c, in_c,
                 kept, out_z, in_z, slab, slab_b, out_y, in_y, out_yb, in_yb, out_zb, in_zb, l_sem, w_sem, s_sem,
                 n_sem, m_sem, i_send, i_recv, d_send, d_recv, t_send, t_recv, r_send, r_recv, e_send, e_recv,
                 a_send, a_recv, x_send, x_recv, c_send, c_recv, z_send, z_recv, y_send, y_recv, g_send, g_recv):
    bf16, f32 = jnp.bfloat16, jnp.float32
    groups, holders = in_d.shape[0], in_t.shape[0]
    vocab, width = table.shape
    rows, block = emb.shape[1], emb.shape[2]
    half = width // 2
    row_count, _, state_size, head_size = state.shape
    steps = rows // row_count
    trows = trainer.shape[0]
    g, t = lax.axis_index("dp"), lax.axis_index("tensor")
    y, z, c, ahead, behind, place = tensor_near(t)
    other, across = place(y, z, 1 - c), place(1 - y, z, c)
    x, low = g // 2, lax.rem(g, 2)
    beside = x * 2 + 1 - low
    x_ahead = [lax.rem(x + o, X) * 2 + low for o in range(1, X)]
    x_behind = [lax.rem(x + X - o, X) * 2 + low for o in range(1, X)]

    load_table = pltpu.make_async_copy(table_hbm, table, l_sem.at[0])
    load_table.start()
    load_trainer = pltpu.make_async_copy(trainer_hbm, trainer, l_sem.at[1])
    load_trainer.start()
    ids2 = ids_in[...]
    row = jnp.concatenate([ids2[s : s + 1] for s in range(steps)], axis=1)
    all_ids[g] = jnp.broadcast_to(row, (8, rows))
    others_d = [xx * 2 + 1 - low for xx in (lax.rem(x + 2, X), lax.rem(x + 1, X), lax.rem(x + 3, X))]
    others_d += [x_ahead[1], x_ahead[0], x_ahead[2], beside]
    others_t = farthest_first(t)
    greet([{"dp": d} for d in others_d] + [{"tensor": d} for d in others_t])
    moves = []
    for o, d in enumerate(others_d):
        moves.append(remote(all_ids.at[g], all_ids.at[g], i_send.at[o], i_recv.at[o], dp=d))
        moves[-1].start()

    load_oweight = pltpu.make_async_copy(oweight_hbm, oweight, l_sem.at[2])
    loads_w = [
        pltpu.make_async_copy(weight_hbm.at[pl.ds(k * block, block)], weight.at[k], w_sem.at[k])
        for k in range(holders)
    ]
    chunks = s_sem.shape[0]
    per = row_count // chunks

    def old_state(p):
        at = pl.ds(p * per, per)
        return pltpu.make_async_copy(state_hbm.at[at], state.at[at], s_sem.at[p])

    def fresh_state(p):
        at = pl.ds(p * per, per)
        return pltpu.make_async_copy(state.at[at], new_hbm.at[at], n_sem.at[p])

    load_trainer.wait()
    for o in range(holders):
        swap_out[o] = trainer[:, o * block : (o + 1) * block].astype(bf16)
    swaps = []
    for o, d in enumerate(others_t):
        swaps.append(remote(swap_out.at[d], gathered.at[g, t], a_send.at[o], a_recv.at[o], tensor=d))
        swaps[-1].start()
    gathered[g, t] = swap_out[t]
    for copy in loads_w + [load_oweight]:
        copy.start()
    for p in range(chunks):
        old_state(p).start()

    at0 = lax.broadcasted_iota(jnp.int32, (rows, rows), 0)
    at1 = lax.broadcasted_iota(jnp.int32, (rows, rows), 1)

    def turn(column):
        return jnp.broadcast_to(column.astype(f32), (rows, rows)).T[0:1].astype(jnp.int32)

    def places(row, column):
        once, slot = order(row, column, at0, at1, vocab)
        fits = jnp.where(turn(slot) < SLOTS, once, 0.0)
        column_t, row_t = lax.rem(column // vocab, holders), lax.rem(row // vocab, holders)
        before = jnp.where((row_t == column_t) & (row < column), fits, 0.0)
        return once, slot, jnp.sum(before, axis=1, keepdims=True).astype(jnp.int32)

    column = jnp.broadcast_to(row, (8, rows)).astype(f32).T.astype(jnp.int32)[:, 0:1]
    once, slot, index = places(row, column)
    from_t, from_g = lax.rem(column // vocab, holders), column // (vocab * holders)
    comes = (slot < SLOTS) & (index < WIDE)
    want = jnp.where(comes, from_t * WIDE + index, -1)
    select = jnp.where(want == lax.broadcasted_iota(jnp.int32, (rows, holders * WIDE), 1), 1.0, 0.0).astype(bf16)
    permute = jnp.where(at1 == lax.rem(at0, steps) * row_count + at0 // steps, 1.0, 0.0).astype(bf16)
    select = jnp.dot(permute, select, preferred_element_type=f32).astype(bf16)
    index_row = turn(jnp.where((from_t == t) & comes, index, -1))
    lift = jnp.where(
        (lax.broadcasted_iota(jnp.int32, (WIDE, rows), 0) == index_row) & (once > 0.5), 1.0, 0.0
    ).astype(bf16)
    lie = jnp.where(slot < SLOTS, from_g * (2 * SLOTS) + slot, -2 * SLOTS * groups)
    take_low = jnp.dot(lift, jnp.where(lie == at1, 1.0, 0.0).astype(bf16), preferred_element_type=f32).astype(bf16)
    take_high = jnp.dot(
        lift, jnp.where(lie + SLOTS == at1, 1.0, 0.0).astype(bf16), preferred_element_type=f32
    ).astype(bf16)
    lower = jnp.where(
        lax.broadcasted_iota(jnp.int32, (vocab, vocab), 0) < lax.broadcasted_iota(jnp.int32, (vocab, vocab), 1),
        1.0,
        0.0,
    ).astype(bf16)

    for copy in moves:
        copy.wait_recv()
    owed = list(moves)
    ids_all = all_ids[0]
    at_g = lax.broadcasted_iota(jnp.int32, (8, rows), 0)
    for gg in range(1, groups):
        ids_all = jnp.where(at_g == gg, all_ids[gg], ids_all)
    columns = ids_all.astype(f32).T.astype(jnp.int32)
    base = (g * holders + t) * vocab
    at_v = lax.broadcasted_iota(jnp.int32, (rows, vocab), 1)
    pick_g = lax.broadcasted_iota(jnp.int32, (16, vocab), 0)
    held = jnp.zeros((16, vocab), f32)
    for gg in range(groups):
        asked = jnp.where(columns[:, gg : gg + 1] - base == at_v, 1.0, 0.0)
        held = jnp.where(pick_g == gg, jnp.max(asked, axis=0, keepdims=True), held)
    rank = jnp.dot(held.astype(bf16), lower, preferred_element_type=f32).astype(jnp.int32)
    at_c = lax.broadcasted_iota(jnp.int32, (SLOTS, vocab), 0)
    chosen = jnp.concatenate(
        [
            jnp.where((rank[gg : gg + 1] == at_c) & (held[gg : gg + 1] > 0.5), 1.0, 0.0)
            for gg in range(groups)
        ],
        axis=0,
    ).astype(bf16)
    load_table.wait()
    step = 512
    for at in range(0, half, step):
        left = jnp.dot(chosen, table[:, at : at + step], preferred_element_type=f32)
        right = jnp.dot(chosen, table[:, half + at : half + at + step], preferred_element_type=f32)
        both = jnp.concatenate(
            [left.reshape(groups, SLOTS, step), right.reshape(groups, SLOTS, step)], axis=1
        )
        out_d[:, :, at : at + step] = both.astype(bf16)
    sent = []
    for o, d in enumerate(others_d):
        sent.append(remote(out_d.at[d], in_d.at[g], d_send.at[o], d_recv.at[o], dp=d))
        sent[-1].start()
    in_d[g] = out_d[g]

    most = jnp.zeros((1, 1), jnp.int32)
    over = jnp.zeros((1, 1), jnp.int32)
    for gg in range(groups):
        _, slots, indices = places(all_ids[gg][0:1], columns[:, gg : gg + 1])
        most = jnp.maximum(most, jnp.max(slots, axis=0, keepdims=True))
        over = jnp.maximum(over, jnp.max(indices, axis=0, keepdims=True))
    todo = jnp.where((most >= SLOTS) | (over >= WIDE), most + 1, 0)
    need[0, 0] = todo[0, 0]
    units = heads * head_size
    maps = jnp.concatenate(
        [head_map[...].astype(f32), jnp.zeros((8 - heads, head_size), f32)], axis=0
    ).T.astype(jnp.int32)
    at_u = lax.broadcasted_iota(jnp.int32, (head_size, units), 1)
    for h in range(heads):
        swap[h * head_size : (h + 1) * head_size] = jnp.where(
            maps[:, h : h + 1] + h * head_size == at_u, 1.0, 0.0
        ).astype(bf16)
    for k in range(holders):
        thin = dtw[:, k * block : (k + 1) * block].astype(f32)
        narrow[k] = jnp.concatenate([thin, jnp.zeros((16 - heads, block), f32)], axis=0).astype(bf16)
    proj[...] = jnp.zeros_like(proj)
    raw[...] = jnp.zeros_like(raw)

    for copy in sent:
        copy.wait_recv()
    owed += sent
    arrived = in_d[...].reshape(groups * 2 * SLOTS, half)
    total = jnp.zeros((WIDE, block), f32)
    for part, take in enumerate((take_low, take_high)):
        for k in range(holders // 2):
            piece = jnp.dot(take, arrived[:, k * block : (k + 1) * block], preferred_element_type=f32)
            out_r[part * (holders // 2) + k] = piece.astype(bf16)
            total = total + piece * piece
    scale = lax.rsqrt(jnp.sum(total, axis=1, keepdims=True) / width + epsilon)
    for k in range(holders):
        scaled = out_r[k].astype(f32) * scale * gain[:, k * block : (k + 1) * block]
        out_t[k] = scaled.astype(bf16)
    sent = []
    for o, d in enumerate(others_t):
        sent.append(remote(out_t.at[d], in_t.at[t], t_send.at[o], t_recv.at[o], tensor=d))
        sent[-1].start()
    in_t[t] = out_t[t]

    shared = []

    def share(block_at, role, to):
        copy = remote(gathered.at[block_at], gathered.at[block_at], x_send.at[role], x_recv.at[role], dp=to)
        copy.start()
        shared.append(copy)
        return copy

    for copy in swaps:
        copy.wait_recv()
    owed += swaps
    to_x = [share(g, 1 + o, x_ahead[o]) for o in range(X - 1)]

    def relay(at):
        pass_on(at).start()

    def pass_on(at):
        return pltpu.make_async_copy(gathered.at[at], gathered_out.at[at], m_sem.at[at])


    for copy in sent:
        copy.wait_recv()
    owed += sent
    found = jnp.dot(select, in_t[...].reshape(holders * WIDE, block), preferred_element_type=f32)
    emb[spot(t)] = found.astype(bf16)

    def project_in(at, k):
        proj[...] += jnp.dot(emb[at], weight[k], preferred_element_type=f32)
        raw[...] += lax.dot_general(emb[at], narrow[k], (((1,), (1,)), ((), ())), preferred_element_type=f32)

    for copy in loads_w:
        copy.wait()
    residual = []

    def send_raw():
        for o, d in enumerate(others_t):
            residual.append(remote(out_r.at[d], in_r.at[t], r_send.at[o], r_recv.at[o], tensor=d))
            residual[-1].start()
        in_r[t] = out_r[t]

    owed += gather_blocks(emb, t, e_send, e_recv, project_in, send_raw)
    to_beside = share(g, 0, beside)
    sizes = (weight.shape[2] // heads, head_size, state_size)
    for h in range(heads):
        mix(h, proj, raw, bias, log_rate, *sizes, key, query, xin, xrow, decay)

    def look(p, carry):
        old_state(p).wait()
        readout(p, per, heads, steps, query, state, read)
        return carry

    lax.fori_loop(0, chunks, look, 0)
    for h in range(heads):
        close(h, steps, proj, skip, ngain, *sizes, xin, xrow, decay, read, mixed)

    load_oweight.wait()
    rows_in = mixed[...]

    def partial_of(yy, zz, cc):
        at = place(yy, zz, cc) * block
        return jnp.dot(rows_in, oweight[:, pl.ds(pl.multiple_of(at, block), block)], preferred_element_type=f32)

    to_core = []
    for n in range(2):
        for zz in range(Z // 2):
            for yy in range(2):
                out_c[n, zz, yy] = partial_of(yy, n * (Z // 2) + zz, 1 - c).astype(bf16)
        to_core.append(remote(out_c.at[n], in_c.at[n], c_send.at[n], c_recv.at[n], tensor=other))
        to_core[-1].start()
    for zz in range(Z):
        for yy in range(2):
            kept[zz, yy] = partial_of(yy, zz, c)
    cut = rows // 2
    for n in range(2):
        to_core[n].wait_recv()
        for zz in range(n * (Z // 2), (n + 1) * (Z // 2)):
            for yy in range(2):
                total = kept[zz, yy] + in_c[n, zz % (Z // 2), yy].astype(f32)
                kept[zz, yy] = total
                out_z[zz, yy] = total[:cut].astype(bf16)
                out_yb[yy, zz] = total[cut:].astype(bf16)
    to_yb = remote(out_yb.at[1 - y], in_yb, y_send.at[0], y_recv.at[0], tensor=across)
    to_yb.start()
    to_z = {}
    for o in (1, 0, 2):
        to_z[o] = remote(out_z.at[ahead[o]], in_z.at[o], z_send.at[o], z_recv.at[o], tensor=place(y, ahead[o], c))
        to_z[o].start()

    def move_on(p, carry):
        update(p, per, heads, steps, key, state, decay, xrow)
        fresh_state(p).start()
        return carry

    lax.fori_loop(0, chunks // 2, move_on, 0)
    to_beside.wait_recv()
    passed = [share(beside, X + o, x_ahead[o]) for o in range(X - 1)]
    relay(g)
    to_yb.wait_recv()
    for zz in range(Z):
        total = kept[zz, y, cut:] + in_yb[zz].astype(f32)
        slab_b[zz] = total
        out_zb[zz] = total.astype(bf16)
    to_zb = {}
    for o in (1, 0, 2):
        to_zb[o] = remote(
            out_zb.at[ahead[o]], in_zb.at[o], z_send.at[3 + o], z_recv.at[3 + o], tensor=place(y, ahead[o], c)
        )
        to_zb[o].start()
    total = kept[z, :, :cut]
    for o in (0, 2, 1):
        to_z[o].wait_recv()
        total = total + in_z[o].astype(f32)
    slab[...] = total
    out_y[...] = slab[1 - y].astype(bf16)
    to_y = remote(out_y, in_y, y_send.at[1], y_recv.at[1], tensor=across)
    to_y.start()
    lax.fori_loop(chunks // 2, chunks, move_on, 0)
    relay(beside)
    for o in range(X - 1):
        to_x[o].wait_recv()
        relay(x_behind[o])
    for copy in residual:
        copy.wait_recv()
    owed += residual
    embedded = jnp.dot(select, in_r[...].reshape(holders * WIDE, block), preferred_element_type=f32)
    total = slab_b[z]
    for o in (0, 2, 1):
        to_zb[o].wait_recv()
        total = total + in_zb[o].astype(f32)
    here = spot(t)
    whole[here, cut:] = (embedded[cut:] + total).astype(bf16)
    to_y.wait_recv()
    whole[here, :cut] = (embedded[:cut] + (slab[y] + in_y[...].astype(f32))).astype(bf16)
    stream[...] = whole[here].astype(f32).reshape(stream.shape).astype(bf16)
    owed += to_core + list(to_z.values()) + list(to_zb.values()) + [to_yb, to_y]

    def settle():
        for copy in owed:
            copy.wait_send()
        for p in range(chunks):
            fresh_state(p).wait()

    spread = gather_blocks(whole, t, g_send, g_recv, meanwhile=settle)
    for o in range(X - 1):
        passed[o].wait_recv()
        relay(x_behind[o] + 1 - 2 * low)
    normalize(whole, next_gain, normed)
    for copy in shared + spread:
        copy.wait_send()
    for at in range(groups):
        pass_on(at).wait()


def fused(ids, table, trainer, gain, weight, dtw, bias, log_rate, skip, ngain, state, oweight, next_gain, head_map,
          groups, holders):
    row_count, heads, state_size, head_size = state.shape
    steps = ids.shape[0]
    rows = steps * ids.shape[1]
    vocab, width = table.shape
    block = width // holders
    trows = trainer.shape[0]
    units = heads * head_size
    cut = rows // 2
    columns = weight.shape[1]
    bf16, f32, dma = jnp.bfloat16, jnp.float32, pltpu.SemaphoreType.DMA
    vmem, anywhere = pl.BlockSpec(memory_space=pltpu.VMEM), pl.BlockSpec(memory_space=pl.ANY)
    smem = pl.BlockSpec(memory_space=pltpu.SMEM)
    buffers = [
        ((vocab, width), bf16),
        ((groups, holders, trows, block), bf16),
        (trainer.shape, f32),
        ((holders, block, columns), bf16),
        (state.shape, f32),
        (oweight.shape, bf16),
        ((groups, 8, rows), jnp.int32),
        ((groups, 2 * SLOTS, width // 2), bf16),
        ((groups, 2 * SLOTS, width // 2), bf16),
        ((holders, WIDE, block), bf16),
        ((holders, WIDE, block), bf16),
        ((holders, WIDE, block), bf16),
        ((holders, WIDE, block), bf16),
        ((holders, rows, block), bf16),
        ((holders, rows, block), bf16),
        ((holders, trows, block), bf16),
        ((rows, columns), f32),
        ((holders, 16, block), bf16),
        ((rows, 16), f32),
        ((heads, state_size, rows), f32),
        ((heads, state_size, rows), f32),
        ((heads, rows, head_size), f32),
        ((heads, rows, head_size), f32),
        ((heads, rows, head_size), f32),
        ((heads, rows, head_size), f32),
        ((rows, units), bf16),
        ((2, Z // 2, 2, rows, block), bf16),
        ((2, Z // 2, 2, rows, block), bf16),
        ((Z, 2, rows, block), f32),
        ((Z, 2, cut, block), bf16),
        ((Z - 1, 2, cut, block), bf16),
        ((2, cut, block), f32),
        ((Z, cut, block), f32),
        ((cut, block), bf16),
        ((cut, block), bf16),
        ((2, Z, cut, block), bf16),
        ((Z, cut, block), bf16),
        ((Z, cut, block), bf16),
        ((Z - 1, cut, block), bf16),
    ]
    semaphores = [3, holders, 8, 8, groups]
    for count in (groups - 1, groups - 1, holders - 1, holders - 1, holders - 1, holders - 1, 2 * X - 1):
        semaphores += [count, count]
    for count in (2, 2 * (Z - 1), 2, holders - 1):
        semaphores += [count, count]
    return pl.pallas_call(
        functools.partial(fused_kernel, heads),
        out_shape=(
            jax.ShapeDtypeStruct(state.shape, f32),
            jax.ShapeDtypeStruct((row_count, steps, block), bf16),
            jax.ShapeDtypeStruct((row_count, steps, width), bf16),
            jax.ShapeDtypeStruct((groups, holders, trows, block), bf16),
            jax.ShapeDtypeStruct((units, units), bf16),
            jax.ShapeDtypeStruct((1, 1), jnp.int32),
        ),
        in_specs=[vmem, anywhere, anywhere, vmem, anywhere, vmem, smem, smem, smem, vmem, anywhere, anywhere, vmem, vmem],
        out_specs=(anywhere, vmem, vmem, anywhere, vmem, smem),
        scratch_shapes=[pltpu.VMEM(*buffer) for buffer in buffers] + [dma((count,)) for count in semaphores],
        compiler_params=pltpu.CompilerParams(
            collective_id=0, has_side_effects=True, vmem_limit_bytes=60 * 2**20
        ),
        name="fused",
    )(ids, table, trainer, gain, weight, dtw, bias, log_rate, skip, ngain, state, oweight, next_gain, head_map)


def per_device(
    token_ids,
    embed_table,
    in_gain,
    in_weight,
    dt_weight,
    dt_bias,
    a_log,
    d_skip,
    norm_gain,
    out_weight,
    next_gain,
    ssm_state,
    trainer_weight,
    head_map,
):
    row_count, step_count = token_ids.shape
    width = embed_table.shape[1]
    holders = lax.axis_size("tensor")
    groups = lax.axis_size("dp")
    rows = row_count * step_count
    state = ssm_state.swapaxes(2, 3)
    gain, ngain, ngain_next = in_gain.reshape(1, -1), norm_gain.reshape(1, -1), next_gain.reshape(1, -1)
    mix = (in_weight, dt_weight.T, dt_bias, a_log, d_skip, ngain, state)
    now, stream, normed, gathered, swap, need = fused(
        token_ids.T, embed_table, trainer_weight, gain, *mix, out_weight, ngain_next, head_map, groups, holders
    )

    def again(carry):
        todo = carry[0]

        def more(inner):
            done, held = inner
            return done + SLOTS, held + lookup(token_ids.T, embed_table, groups, holders, jnp.full((8, 128), done, jnp.int32))

        empty = jnp.zeros((holders, rows, width // holders), jnp.bfloat16)
        _, emb = lax.while_loop(lambda inner: inner[0] < todo, more, (jnp.int32(0), empty))
        now, mixed = mixer(emb, gain, *mix)
        stream, normed = project(mixed, out_weight, emb, ngain_next, step_count)
        return jnp.int32(0), now, stream, normed

    _, now, stream, normed = lax.while_loop(
        lambda carry: carry[0] > 0, again, (need.reshape(()), now, stream, normed)
    )
    relaid = lax.dot_general(
        swap, gathered.reshape(width, swap.shape[1]), (((1,), (1,)), ((), ())), preferred_element_type=jnp.float32
    )
    return (
        now.swapaxes(2, 3),
        stream,
        normed,
        relaid,
    )


def solution(mesh):
    placed = (
        P("dp", None),
        P(("dp", "tensor"), None),
        P(),
        P(None, "tensor"),
        P(None, "tensor"),
        P("tensor"),
        P("tensor"),
        P("tensor"),
        P("tensor"),
        P("tensor", None),
        P(),
        P("dp", "tensor", None, None),
        P(("dp", "tensor"), None),
        P("tensor", None),
    )
    return jax.shard_map(
        per_device,
        mesh=mesh,
        in_specs=placed,
        out_specs=(
            P("dp", "tensor", None, None),
            P("dp", None, "tensor"),
            P("dp", None, None),
            P("tensor", None),
        ),
        check_vma=False,
    )
```

```python
import functools
import jax
import jax.numpy as jnp
from jax import lax
from jax.experimental import pallas as pl
from jax.experimental.pallas import tpu as pltpu
from jax.sharding import PartitionSpec as P

epsilon = 1e-05
MESH = pl.DeviceIdType.MESH
SLOTS = 8
WIDE = 32
Z = 4
X = 4


def remote(src, dst, send_sem, recv_sem, **place):
    return pltpu.make_async_remote_copy(
        src_ref=src,
        dst_ref=dst,
        send_sem=send_sem,
        recv_sem=recv_sem,
        device_id=place,
        device_id_type=MESH,
    )


def greet(places):
    barrier = pltpu.get_barrier_semaphore()
    for place in places:
        pl.semaphore_signal(barrier, inc=1, device_id=place, device_id_type=MESH)
    pl.semaphore_wait(barrier, len(places))


def tensor_near(t):
    y, z, c = t // (2 * Z), lax.rem(t // 2, Z), lax.rem(t, 2)
    ahead = [lax.rem(z + o, Z) for o in range(1, Z)]
    behind = [lax.rem(z + Z - o, Z) for o in range(1, Z)]
    place = lambda yy, zz, cc: yy * (2 * Z) + zz * 2 + cc
    return y, z, c, ahead, behind, place


def spot(t):
    return lax.rem(t, 2) * (2 * Z) + t // 2 if not isinstance(t, int) else t % 2 * (2 * Z) + t // 2


def farthest_first(t):
    y, z, c, ahead, _, place = tensor_near(t)
    chips = [(1 - y, ahead[1]), (1 - y, ahead[0]), (1 - y, ahead[2]), (1 - y, z)]
    chips += [(y, ahead[1]), (y, ahead[0]), (y, ahead[2])]
    return [place(yy, zz, cc) for yy, zz in chips for cc in (c, 1 - c)] + [place(y, z, 1 - c)]


def gather_blocks(buf, t, send, recv, use=lambda at, position: None, meanwhile=lambda: None):
    y, z, c, ahead, behind, place = tensor_near(t)
    other = place(y, z, 1 - c)
    to = [(1 - y, ahead[1]), (1 - y, ahead[0]), (1 - y, ahead[2]), (1 - y, z), (y, ahead[1]), (y, ahead[0]), (y, ahead[2])]
    own = spot(t)
    sent = []
    for role, (yy, zz) in enumerate(to):
        sent.append(remote(buf.at[own], buf.at[own], send.at[role], recv.at[role], tensor=place(yy, zz, c)))
        sent[-1].start()

    def core(yy, role):
        at = pl.ds((c * 2 + yy) * Z, Z)
        copy = remote(buf.at[at], buf.at[at], send.at[role], recv.at[role], tensor=other)
        copy.start()
        return copy

    def used(yy, zz, cc):
        position = place(yy, zz, cc)
        use(spot(position), position)

    meanwhile()
    used(y, z, c)
    for role in (5, 6, 4):
        sent[role].wait_recv()
    near = core(y, 7)
    for zz in behind:
        used(y, zz, c)
    for role in (3, 1, 2, 0):
        sent[role].wait_recv()
    far = core(1 - y, 8)
    for zz in [z] + behind:
        used(1 - y, zz, c)
    near.wait_recv()
    for zz in [z] + behind:
        used(y, zz, 1 - c)
    far.wait_recv()
    for zz in [z] + behind:
        used(1 - y, zz, 1 - c)
    return sent + [near, far]


def order(row, column, at0, at1, vocab):
    again = jnp.where((column == row) & (at0 < at1), 1.0, 0.0)
    once = 1.0 - jnp.max(again, axis=0, keepdims=True)
    floor = column - lax.rem(column, vocab)
    before = jnp.where((row >= floor) & (row < column), once, 0.0)
    return once, jnp.sum(before, axis=1, keepdims=True).astype(jnp.int32)


def lookup_kernel(ids_ref, start_ref, table_hbm, emb, table, all_ids, out_d, in_d, out_t, in_t, local, ids_send, ids_recv,
                  d_send, d_recv, t_send, t_recv, g_send, g_recv):
    groups, holders = in_d.shape[0], in_t.shape[0]
    steps, row_count = ids_ref.shape
    rows, vocab, width = steps * row_count, table.shape[0], table.shape[1]
    block = width // holders
    half = width // 2
    g, t = lax.axis_index("dp"), lax.axis_index("tensor")
    load = pltpu.make_async_copy(table_hbm, table, local.at[0])
    load.start()
    row = jnp.concatenate([ids_ref[s : s + 1] for s in range(steps)], axis=1)
    all_ids[g] = jnp.broadcast_to(row, (8, rows))
    others_d = [lax.rem(g + o, groups) for o in range(1, groups)]
    others_t = [lax.rem(t + o, holders) for o in range(1, holders)]
    greet([{"dp": d} for d in others_d] + [{"tensor": d} for d in others_t])
    moves = []
    for o, d in enumerate(others_d):
        moves.append(remote(all_ids.at[g], all_ids.at[g], ids_send.at[o], ids_recv.at[o], dp=d))
        moves[-1].start()

    start = start_ref[0:1, 0:1]
    column = jnp.broadcast_to(row, (8, rows)).astype(jnp.float32).T.astype(jnp.int32)[:, 0:1]
    at0 = lax.broadcasted_iota(jnp.int32, (rows, rows), 0)
    at1 = lax.broadcasted_iota(jnp.int32, (rows, rows), 1)

    slot = order(row, column, at0, at1, vocab)[1] - start
    holder = column // vocab
    from_t, from_g = lax.rem(holder, holders), holder // holders
    want = jnp.where((slot >= 0) & (slot < SLOTS), (from_t * groups + from_g) * SLOTS + slot, -1)
    candidates = holders * groups * SLOTS

    for copy in moves:
        copy.wait()

    ids_all = all_ids[0]
    at_g = lax.broadcasted_iota(jnp.int32, (8, rows), 0)
    for gg in range(1, groups):
        ids_all = jnp.where(at_g == gg, all_ids[gg], ids_all)
    columns = ids_all.astype(jnp.float32).T.astype(jnp.int32)
    base = (g * holders + t) * vocab
    at_v = lax.broadcasted_iota(jnp.int32, (rows, vocab), 1)
    pick_g = lax.broadcasted_iota(jnp.int32, (16, vocab), 0)
    held = jnp.zeros((16, vocab), jnp.float32)
    for gg in range(groups):
        asked = jnp.where(columns[:, gg : gg + 1] - base == at_v, 1.0, 0.0)
        held = jnp.where(pick_g == gg, jnp.max(asked, axis=0, keepdims=True), held)
    lower = jnp.where(
        lax.broadcasted_iota(jnp.int32, (vocab, vocab), 0) < lax.broadcasted_iota(jnp.int32, (vocab, vocab), 1),
        1.0,
        0.0,
    ).astype(jnp.bfloat16)
    rank = jnp.dot(held.astype(jnp.bfloat16), lower, preferred_element_type=jnp.float32).astype(jnp.int32) - start
    at_c = lax.broadcasted_iota(jnp.int32, (SLOTS, vocab), 0)
    chosen = jnp.concatenate(
        [
            jnp.where((rank[gg : gg + 1] == at_c) & (held[gg : gg + 1] > 0.5), 1.0, 0.0)
            for gg in range(groups)
        ],
        axis=0,
    ).astype(jnp.bfloat16)
    load.wait()
    step = 512
    for at in range(0, half, step):
        low = jnp.dot(chosen, table[:, at : at + step], preferred_element_type=jnp.float32)
        high = jnp.dot(chosen, table[:, half + at : half + at + step], preferred_element_type=jnp.float32)
        both = jnp.concatenate(
            [low.reshape(groups, SLOTS, step), high.reshape(groups, SLOTS, step)], axis=1
        )
        out_d[:, :, at : at + step] = both.astype(jnp.bfloat16)
    sent = []
    for o, d in enumerate(others_d):
        sent.append(remote(out_d.at[d], in_d.at[g], d_send.at[o], d_recv.at[o], dp=d))
        sent[-1].start()
    in_d[g] = out_d[g]
    select = jnp.where(
        want == lax.broadcasted_iota(jnp.int32, (rows, candidates), 1), 1.0, 0.0
    ).astype(jnp.bfloat16)
    permute = jnp.where(at1 == lax.rem(at0, steps) * row_count + at0 // steps, 1.0, 0.0).astype(jnp.bfloat16)
    select = jnp.dot(permute, select, preferred_element_type=jnp.float32).astype(jnp.bfloat16)
    for copy in sent:
        copy.wait()
    for o in range(holders):
        part, at = o // (holders // 2), (o % (holders // 2)) * block
        piece = in_d[:, :, at : at + block].astype(jnp.float32)[:, part * SLOTS : (part + 1) * SLOTS]
        out_t[o] = piece.reshape(groups * SLOTS, block).astype(jnp.bfloat16)
    sent = []
    for o, d in enumerate(others_t):
        sent.append(remote(out_t.at[d], in_t.at[t], t_send.at[o], t_recv.at[o], tensor=d))
        sent[-1].start()
    in_t[t] = out_t[t]
    for copy in sent:
        copy.wait()
    found = jnp.dot(select, in_t[...].reshape(candidates, block), preferred_element_type=jnp.float32)
    emb[spot(t)] = found.astype(jnp.bfloat16)
    for copy in gather_blocks(emb, t, g_send, g_recv):
        copy.wait_send()


def lookup(ids, table, groups, holders, start):
    rows = ids.shape[0] * ids.shape[1]
    vocab, width = table.shape
    block = width // holders
    bf16, dma = jnp.bfloat16, pltpu.SemaphoreType.DMA
    vmem, anywhere = pl.BlockSpec(memory_space=pltpu.VMEM), pl.BlockSpec(memory_space=pl.ANY)
    return pl.pallas_call(
        lookup_kernel,
        out_shape=jax.ShapeDtypeStruct((holders, rows, block), bf16),
        in_specs=[vmem, vmem, anywhere],
        out_specs=vmem,
        scratch_shapes=[
            pltpu.VMEM((vocab, width), bf16),
            pltpu.VMEM((groups, 8, rows), jnp.int32),
            pltpu.VMEM((groups, 2 * SLOTS, width // 2), bf16),
            pltpu.VMEM((groups, 2 * SLOTS, width // 2), bf16),
            pltpu.VMEM((holders, groups * SLOTS, block), bf16),
            pltpu.VMEM((holders, groups * SLOTS, block), bf16),
            dma((1,)),
            dma((groups - 1,)),
            dma((groups - 1,)),
            dma((groups - 1,)),
            dma((groups - 1,)),
            dma((holders - 1,)),
            dma((holders - 1,)),
            dma((holders - 1,)),
            dma((holders - 1,)),
        ],
        compiler_params=pltpu.CompilerParams(collective_id=1, has_side_effects=True, vmem_limit_bytes=40 * 2**20),
        name="lookup_round",
    )(ids, start, table)


def normalize(whole, gain, out, squares=None):
    holders, rows, block = whole.shape
    if squares is None:
        squares = jnp.zeros((rows, block), jnp.float32)
        for k in range(holders):
            wide = whole[k].astype(jnp.float32)
            squares = squares + wide * wide
    scale = lax.rsqrt(jnp.sum(squares, axis=1, keepdims=True) / (holders * block) + epsilon)
    for k in range(holders):
        at = slice(k * block, (k + 1) * block)
        scaled = whole[spot(k)].astype(jnp.float32) * scale * gain[:, at]
        out[:, :, at] = scaled.reshape(out.shape[0], out.shape[1], block).astype(jnp.bfloat16)


def project_kernel(mixed, weight_hbm, emb, next_gain, stream, normed, whole, weight, out_c, in_c, kept, out_z, in_z, slab, out_y, in_y, local,
                   c_send, c_recv, z_send, z_recv, y_send, y_recv, g_send, g_recv):
    t = lax.axis_index("tensor")
    block = whole.shape[2]
    load = pltpu.make_async_copy(weight_hbm, weight, local.at[0])
    load.start()
    y, z, c, ahead, behind, place = tensor_near(t)
    other, across = place(y, z, 1 - c), place(1 - y, z, c)
    greet([{"tensor": other}, {"tensor": across}] + [{"tensor": place(y, zz, c)} for zz in ahead])

    load.wait()
    rows_in = mixed[...]

    def partial_of(k, cc):
        at = place(k % 2, k // 2, cc) * block
        return jnp.dot(rows_in, weight[:, pl.ds(pl.multiple_of(at, block), block)], preferred_element_type=jnp.float32)

    to_core = []
    for k in range(2 * Z):
        out_c[k] = partial_of(k, 1 - c).astype(jnp.bfloat16)
        to_core.append(remote(out_c.at[k], in_c.at[k], c_send.at[k], c_recv.at[k], tensor=other))
        to_core[-1].start()
    for k in range(2 * Z):
        kept[k // 2, k % 2] = partial_of(k, c)
    for k in range(2 * Z):
        to_core[k].wait_recv()
        total = kept[k // 2, k % 2] + in_c[k].astype(jnp.float32)
        kept[k // 2, k % 2] = total
        out_z[k // 2, k % 2] = total.astype(jnp.bfloat16)
    to_z = []
    for o in range(Z - 1):
        to_z.append(
            remote(out_z.at[ahead[o]], in_z.at[o], z_send.at[o], z_recv.at[o], tensor=place(y, ahead[o], c))
        )
        to_z[-1].start()
    total = kept[z]
    for o in range(Z - 1):
        to_z[o].wait_recv()
        total = total + in_z[o].astype(jnp.float32)
    slab[...] = total
    out_y[...] = slab[1 - y].astype(jnp.bfloat16)
    to_y = remote(out_y, in_y, y_send.at[0], y_recv.at[0], tensor=across)
    to_y.start()
    to_y.wait_recv()
    branch = slab[y] + in_y[...].astype(jnp.float32)
    mine = (emb[spot(t)].astype(jnp.float32) + branch).astype(jnp.bfloat16)
    stream[...] = mine.astype(jnp.float32).reshape(stream.shape).astype(jnp.bfloat16)
    whole[spot(t)] = mine
    spread = gather_blocks(whole, t, g_send, g_recv)
    normalize(whole, next_gain, normed)
    for copy in to_core + to_z + [to_y] + spread:
        copy.wait_send()


def project(mixed, weight, emb, next_gain, steps):
    holders, rows, block = emb.shape
    bf16, f32, dma = jnp.bfloat16, jnp.float32, pltpu.SemaphoreType.DMA
    vmem, anywhere = pl.BlockSpec(memory_space=pltpu.VMEM), pl.BlockSpec(memory_space=pl.ANY)
    return pl.pallas_call(
        project_kernel,
        out_shape=(
            jax.ShapeDtypeStruct((rows // steps, steps, block), bf16),
            jax.ShapeDtypeStruct((rows // steps, steps, holders * block), bf16),
        ),
        in_specs=[vmem, anywhere, vmem, vmem],
        out_specs=(vmem, vmem),
        scratch_shapes=[
            pltpu.VMEM((holders, rows, block), bf16),
            pltpu.VMEM(weight.shape, bf16),
            pltpu.VMEM((2 * Z, rows, block), bf16),
            pltpu.VMEM((2 * Z, rows, block), bf16),
            pltpu.VMEM((Z, 2, rows, block), f32),
            pltpu.VMEM((Z, 2, rows, block), bf16),
            pltpu.VMEM((Z - 1, 2, rows, block), bf16),
            pltpu.VMEM((2, rows, block), f32),
            pltpu.VMEM((rows, block), bf16),
            pltpu.VMEM((rows, block), bf16),
            dma((1,)),
            dma((2 * Z,)),
            dma((2 * Z,)),
            dma((Z - 1,)),
            dma((Z - 1,)),
            dma((1,)),
            dma((1,)),
            dma((holders - 1,)),
            dma((holders - 1,)),
        ],
        compiler_params=pltpu.CompilerParams(
            collective_id=2, has_side_effects=True, vmem_limit_bytes=40 * 2**20
        ),
        name="project",
    )(mixed, weight, emb, next_gain)


def readout(p, per, heads, steps, query, state, read):
    rows = read.shape[1]
    base = pl.multiple_of(p * (per * steps), per * steps)
    for h in range(heads):
        turned = pltpu.roll(query[h], lax.rem(rows - base, rows), 1)
        outs = []
        for i in range(per):
            old = state[p * per + i, h]
            for s in range(steps):
                lane = i * steps + s
                outs.append(jnp.sum(old * turned[:, lane : lane + 1], axis=0, keepdims=True))
        read[h, pl.ds(base, per * steps)] = jnp.concatenate(outs, axis=0)


def update(p, per, heads, steps, key, state, decay, xrow):
    rows = xrow.shape[1]
    base = pl.multiple_of(p * (per * steps), per * steps)
    for h in range(heads):
        turned = pltpu.roll(key[h], lax.rem(rows - base, rows), 1)
        for i in range(per):
            now = state[p * per + i, h]
            for s in range(steps):
                lane = i * steps + s
                now = decay[h, pl.ds(base + lane, 1)] * now + xrow[h, pl.ds(base + lane, 1)] * turned[:, lane : lane + 1]
            state[p * per + i, h] = now


def mix(h, proj, raw, bias, log_rate, columns, head_size, state_size, key, query, xin, xrow, decay):
    rows, at = proj.shape[0], h * columns
    value = raw[:, h : h + 1] + bias[h]
    size = jnp.maximum(value, 0.0) + jnp.log1p(jnp.exp(-jnp.abs(value)))
    rate = jnp.exp(-size * jnp.exp(jnp.full((rows, 1), log_rate[h], jnp.float32)))
    entry = proj[:, at : at + head_size]
    xin[h] = entry
    xrow[h] = size * entry
    decay[h] = jnp.broadcast_to(rate, (rows, head_size))
    at += 2 * head_size
    turned = proj[:, at : at + 2 * state_size].T
    key[h] = turned[:state_size]
    query[h] = turned[state_size:]


def close(h, steps, proj, skip, ngain, columns, head_size, state_size, xin, xrow, decay, read, mixed):
    at = h * columns
    rows = proj.shape[0]
    both = proj[:, at + 2 * head_size : at + 2 * head_size + 2 * state_size]
    queries = both[:, state_size:]
    step = lax.rem(lax.broadcasted_iota(jnp.int32, (rows, 1), 0), steps)
    rates, entry = decay[h], xrow[h]
    reach = rates
    out = jnp.sum(both[:, :state_size] * queries, axis=1, keepdims=True) * entry
    for back in range(1, steps):
        keys = pltpu.roll(both, back, 0)[:, :state_size]
        old = jnp.sum(keys * queries, axis=1, keepdims=True) * pltpu.roll(entry, back, 0)
        out = jnp.where(step >= back, out + reach * old, out)
        reach = jnp.where(step >= back, reach * pltpu.roll(rates, back, 0), reach)
    out = out + reach * read[h]
    out = out + skip[h] * xin[h]
    gate = proj[:, at + head_size : at + 2 * head_size]
    out = out * (gate / (1.0 + jnp.exp(-gate)))
    out = out * lax.rsqrt(jnp.mean(out * out, axis=1, keepdims=True) + epsilon)
    out = out * ngain[:, h * head_size : (h + 1) * head_size]
    mixed[:, h * head_size : (h + 1) * head_size] = out.astype(jnp.bfloat16)


def mixer_kernel(heads, emb, gain, weight_hbm, dtw, bias, log_rate, skip, ngain, state_hbm, new_hbm, mixed, weight, state, nrm, proj,
                 key, query, xin, xrow, decay, read, w_sem, s_sem, n_sem):
    holders, rows, block = emb.shape
    row_count, _, state_size, head_size = state.shape
    columns = weight.shape[1] // heads
    steps = rows // row_count
    parts = w_sem.shape[0]
    depth = weight.shape[0] // parts
    chunks = s_sem.shape[0]
    per = row_count // chunks
    loads = []
    for p in range(parts):
        at = pl.ds(p * depth, depth)
        loads.append(pltpu.make_async_copy(weight_hbm.at[at], weight.at[at], w_sem.at[p]))
        loads[-1].start()
    for p in range(chunks):
        at = pl.ds(p * per, per)
        pltpu.make_async_copy(state_hbm.at[at], state.at[at], s_sem.at[p]).start()

    squares = jnp.zeros((rows, block), jnp.float32)
    for k in range(holders):
        wide = emb[spot(k)].astype(jnp.float32)
        squares = squares + wide * wide
    scale = lax.rsqrt(jnp.sum(squares, axis=1, keepdims=True) / (holders * block) + epsilon)
    for k in range(holders):
        nrm[:, k * block : (k + 1) * block] = (emb[spot(k)].astype(jnp.float32) * scale * gain[:, k * block : (k + 1) * block]).astype(jnp.bfloat16)
    narrow = dtw[...].astype(jnp.float32)
    narrow = jnp.concatenate([narrow, jnp.zeros((16 - heads, narrow.shape[1]), jnp.float32)], axis=0).astype(jnp.bfloat16)
    steps_raw = lax.dot_general(nrm[...], narrow, (((1,), (1,)), ((), ())), preferred_element_type=jnp.float32)
    for p in range(parts):
        loads[p].wait()
        part = jnp.dot(nrm[:, p * depth : (p + 1) * depth], weight[p * depth : (p + 1) * depth],
                       preferred_element_type=jnp.float32)
        proj[...] = part if p == 0 else proj[...] + part

    sizes = (columns, head_size, state_size)
    for h in range(heads):
        mix(h, proj, steps_raw, bias, log_rate, *sizes, key, query, xin, xrow, decay)

    def chunk(p, carry):
        at = pl.ds(p * per, per)
        pltpu.make_async_copy(state_hbm.at[at], state.at[at], s_sem.at[p]).wait()
        readout(p, per, heads, steps, query, state, read)
        update(p, per, heads, steps, key, state, decay, xrow)
        pltpu.make_async_copy(state.at[at], new_hbm.at[at], n_sem.at[p]).start()
        return carry

    lax.fori_loop(0, chunks, chunk, 0)
    for h in range(heads):
        close(h, steps, proj, skip, ngain, *sizes, xin, xrow, decay, read, mixed)
    for p in range(chunks):
        at = pl.ds(p * per, per)
        pltpu.make_async_copy(state.at[at], new_hbm.at[at], n_sem.at[p]).wait()


def mixer(emb, gain, weight, dtw, bias, log_rate, skip, ngain, state):
    holders, rows, block = emb.shape
    row_count, heads, state_size, head_size = state.shape
    bf16, f32, dma = jnp.bfloat16, jnp.float32, pltpu.SemaphoreType.DMA
    vmem, anywhere = pl.BlockSpec(memory_space=pltpu.VMEM), pl.BlockSpec(memory_space=pl.ANY)
    smem = pl.BlockSpec(memory_space=pltpu.SMEM)
    return pl.pallas_call(
        functools.partial(mixer_kernel, heads),
        out_shape=(
            jax.ShapeDtypeStruct(state.shape, f32),
            jax.ShapeDtypeStruct((rows, heads * head_size), bf16),
        ),
        in_specs=[vmem, vmem, anywhere, vmem, smem, smem, smem, vmem, anywhere],
        out_specs=(anywhere, vmem),
        scratch_shapes=[
            pltpu.VMEM(weight.shape, bf16),
            pltpu.VMEM(state.shape, f32),
            pltpu.VMEM((rows, holders * block), bf16),
            pltpu.VMEM((rows, weight.shape[1]), f32),
            pltpu.VMEM((heads, state_size, rows), f32),
            pltpu.VMEM((heads, state_size, rows), f32),
            pltpu.VMEM((heads, rows, head_size), f32),
            pltpu.VMEM((heads, rows, head_size), f32),
            pltpu.VMEM((heads, rows, head_size), f32),
            pltpu.VMEM((heads, rows, head_size), f32),
            dma((4,)),
            dma((8,)),
            dma((8,)),
        ],
        compiler_params=pltpu.CompilerParams(vmem_limit_bytes=40 * 2**20),
        name="mixer",
    )(emb, gain, weight, dtw, bias, log_rate, skip, ngain, state)


def fused_kernel(heads, ids_in, table_hbm, trainer_hbm, gain, weight_hbm, dtw, bias, log_rate, skip, ngain,
                 state_hbm, oweight_hbm, next_gain, head_map, new_hbm, stream, normed, gathered_out, swap, need,
                 table, gathered, trainer, weight, state, oweight, all_ids, out_d, in_d, out_t, in_t, out_r, in_r,
                 emb, whole, swap_out, proj, narrow, raw, key, query, xin, xrow, decay, read, mixed, out_c, in_c,
                 kept, out_z, in_z, slab, slab_b, out_y, in_y, out_yb, in_yb, out_zb, in_zb, l_sem, w_sem, s_sem,
                 n_sem, m_sem, i_send, i_recv, d_send, d_recv, t_send, t_recv, r_send, r_recv, e_send, e_recv,
                 a_send, a_recv, x_send, x_recv, c_send, c_recv, z_send, z_recv, y_send, y_recv, g_send, g_recv):
    bf16, f32 = jnp.bfloat16, jnp.float32
    groups, holders = in_d.shape[0], in_t.shape[0]
    vocab, width = table.shape
    rows, block = emb.shape[1], emb.shape[2]
    half = width // 2
    row_count, _, state_size, head_size = state.shape
    steps = rows // row_count
    trows = trainer.shape[0]
    g, t = lax.axis_index("dp"), lax.axis_index("tensor")
    y, z, c, ahead, behind, place = tensor_near(t)
    other, across = place(y, z, 1 - c), place(1 - y, z, c)
    x, low = g // 2, lax.rem(g, 2)
    beside = x * 2 + 1 - low
    x_ahead = [lax.rem(x + o, X) * 2 + low for o in range(1, X)]
    x_behind = [lax.rem(x + X - o, X) * 2 + low for o in range(1, X)]

    load_table = pltpu.make_async_copy(table_hbm, table, l_sem.at[0])
    load_table.start()
    load_trainer = pltpu.make_async_copy(trainer_hbm, trainer, l_sem.at[1])
    load_trainer.start()
    ids2 = ids_in[...]
    row = jnp.concatenate([ids2[s : s + 1] for s in range(steps)], axis=1)
    all_ids[g] = jnp.broadcast_to(row, (8, rows))
    others_d = [xx * 2 + 1 - low for xx in (lax.rem(x + 2, X), lax.rem(x + 1, X), lax.rem(x + 3, X))]
    others_d += [x_ahead[1], x_ahead[0], x_ahead[2], beside]
    others_t = farthest_first(t)
    greet([{"dp": d} for d in others_d] + [{"tensor": d} for d in others_t])
    moves = []
    for o, d in enumerate(others_d):
        moves.append(remote(all_ids.at[g], all_ids.at[g], i_send.at[o], i_recv.at[o], dp=d))
        moves[-1].start()

    load_oweight = pltpu.make_async_copy(oweight_hbm, oweight, l_sem.at[2])
    loads_w = [
        pltpu.make_async_copy(weight_hbm.at[pl.ds(k * block, block)], weight.at[k], w_sem.at[k])
        for k in range(holders)
    ]
    chunks = s_sem.shape[0]
    per = row_count // chunks

    def old_state(p):
        at = pl.ds(p * per, per)
        return pltpu.make_async_copy(state_hbm.at[at], state.at[at], s_sem.at[p])

    def fresh_state(p):
        at = pl.ds(p * per, per)
        return pltpu.make_async_copy(state.at[at], new_hbm.at[at], n_sem.at[p])

    load_trainer.wait()
    for o in range(holders):
        swap_out[o] = trainer[:, o * block : (o + 1) * block].astype(bf16)
    swaps = []
    for o, d in enumerate(others_t):
        swaps.append(remote(swap_out.at[d], gathered.at[g, t], a_send.at[o], a_recv.at[o], tensor=d))
        swaps[-1].start()
    gathered[g, t] = swap_out[t]
    for copy in loads_w + [load_oweight]:
        copy.start()
    for p in range(chunks):
        old_state(p).start()

    at0 = lax.broadcasted_iota(jnp.int32, (rows, rows), 0)
    at1 = lax.broadcasted_iota(jnp.int32, (rows, rows), 1)

    def turn(column):
        return jnp.broadcast_to(column.astype(f32), (rows, rows)).T[0:1].astype(jnp.int32)

    def places(row, column):
        once, slot = order(row, column, at0, at1, vocab)
        fits = jnp.where(turn(slot) < SLOTS, once, 0.0)
        column_t, row_t = lax.rem(column // vocab, holders), lax.rem(row // vocab, holders)
        before = jnp.where((row_t == column_t) & (row < column), fits, 0.0)
        return once, slot, jnp.sum(before, axis=1, keepdims=True).astype(jnp.int32)

    lower = jnp.where(
        lax.broadcasted_iota(jnp.int32, (vocab, vocab), 0) < lax.broadcasted_iota(jnp.int32, (vocab, vocab), 1),
        1.0,
        0.0,
    ).astype(bf16)

    for copy in moves:
        copy.wait_recv()
    owed = list(moves)
    ids_all = all_ids[0]
    at_g = lax.broadcasted_iota(jnp.int32, (8, rows), 0)
    for gg in range(1, groups):
        ids_all = jnp.where(at_g == gg, all_ids[gg], ids_all)
    columns = ids_all.astype(f32).T.astype(jnp.int32)
    base = (g * holders + t) * vocab
    at_v = lax.broadcasted_iota(jnp.int32, (rows, vocab), 1)
    pick_g = lax.broadcasted_iota(jnp.int32, (16, vocab), 0)
    held = jnp.zeros((16, vocab), f32)
    for gg in range(groups):
        asked = jnp.where(columns[:, gg : gg + 1] - base == at_v, 1.0, 0.0)
        held = jnp.where(pick_g == gg, jnp.max(asked, axis=0, keepdims=True), held)
    rank = jnp.dot(held.astype(bf16), lower, preferred_element_type=f32).astype(jnp.int32)
    at_c = lax.broadcasted_iota(jnp.int32, (SLOTS, vocab), 0)
    chosen = jnp.concatenate(
        [
            jnp.where((rank[gg : gg + 1] == at_c) & (held[gg : gg + 1] > 0.5), 1.0, 0.0)
            for gg in range(groups)
        ],
        axis=0,
    ).astype(bf16)
    load_table.wait()
    step = 512
    for at in range(0, half, step):
        left = jnp.dot(chosen, table[:, at : at + step], preferred_element_type=f32)
        right = jnp.dot(chosen, table[:, half + at : half + at + step], preferred_element_type=f32)
        both = jnp.concatenate(
            [left.reshape(groups, SLOTS, step), right.reshape(groups, SLOTS, step)], axis=1
        )
        out_d[:, :, at : at + step] = both.astype(bf16)
    sent = []
    for o, d in enumerate(others_d):
        sent.append(remote(out_d.at[d], in_d.at[g], d_send.at[o], d_recv.at[o], dp=d))
        sent[-1].start()
    in_d[g] = out_d[g]

    column = jnp.broadcast_to(row, (8, rows)).astype(f32).T.astype(jnp.int32)[:, 0:1]
    once, slot, index = places(row, column)
    from_t, from_g = lax.rem(column // vocab, holders), column // (vocab * holders)
    comes = (slot < SLOTS) & (index < WIDE)
    want = jnp.where(comes, from_t * WIDE + index, -1)
    select = jnp.where(want == lax.broadcasted_iota(jnp.int32, (rows, holders * WIDE), 1), 1.0, 0.0).astype(bf16)
    permute = jnp.where(at1 == lax.rem(at0, steps) * row_count + at0 // steps, 1.0, 0.0).astype(bf16)
    select = jnp.dot(permute, select, preferred_element_type=f32).astype(bf16)
    index_row = turn(jnp.where((from_t == t) & comes, index, -1))
    lift = jnp.where(
        (lax.broadcasted_iota(jnp.int32, (WIDE, rows), 0) == index_row) & (once > 0.5), 1.0, 0.0
    ).astype(bf16)
    lie = jnp.where(slot < SLOTS, from_g * (2 * SLOTS) + slot, -2 * SLOTS * groups)
    take_low = jnp.dot(lift, jnp.where(lie == at1, 1.0, 0.0).astype(bf16), preferred_element_type=f32).astype(bf16)
    take_high = jnp.dot(
        lift, jnp.where(lie + SLOTS == at1, 1.0, 0.0).astype(bf16), preferred_element_type=f32
    ).astype(bf16)
    most = jnp.zeros((1, 1), jnp.int32)
    over = jnp.zeros((1, 1), jnp.int32)
    for gg in range(groups):
        _, slots, indices = places(all_ids[gg][0:1], columns[:, gg : gg + 1])
        most = jnp.maximum(most, jnp.max(slots, axis=0, keepdims=True))
        over = jnp.maximum(over, jnp.max(indices, axis=0, keepdims=True))
    todo = jnp.where((most >= SLOTS) | (over >= WIDE), most + 1, 0)
    need[0, 0] = todo[0, 0]
    units = heads * head_size
    maps = jnp.concatenate(
        [head_map[...].astype(f32), jnp.zeros((8 - heads, head_size), f32)], axis=0
    ).T.astype(jnp.int32)
    at_u = lax.broadcasted_iota(jnp.int32, (head_size, units), 1)
    for h in range(heads):
        swap[h * head_size : (h + 1) * head_size] = jnp.where(
            maps[:, h : h + 1] + h * head_size == at_u, 1.0, 0.0
        ).astype(bf16)
    for k in range(holders):
        thin = dtw[:, k * block : (k + 1) * block].astype(f32)
        narrow[k] = jnp.concatenate([thin, jnp.zeros((16 - heads, block), f32)], axis=0).astype(bf16)
    proj[...] = jnp.zeros_like(proj)
    raw[...] = jnp.zeros_like(raw)

    for copy in sent:
        copy.wait_recv()
    owed += sent
    arrived = in_d[...].reshape(groups * 2 * SLOTS, half)
    total = jnp.zeros((WIDE, block), f32)
    for part, take in enumerate((take_low, take_high)):
        for k in range(holders // 2):
            piece = jnp.dot(take, arrived[:, k * block : (k + 1) * block], preferred_element_type=f32)
            out_r[part * (holders // 2) + k] = piece.astype(bf16)
            total = total + piece * piece
    scale = lax.rsqrt(jnp.sum(total, axis=1, keepdims=True) / width + epsilon)
    for k in range(holders):
        scaled = out_r[k].astype(f32) * scale * gain[:, k * block : (k + 1) * block]
        out_t[k] = scaled.astype(bf16)
    sent = []
    for o, d in enumerate(others_t):
        sent.append(remote(out_t.at[d], in_t.at[t], t_send.at[o], t_recv.at[o], tensor=d))
        sent[-1].start()
    in_t[t] = out_t[t]

    shared = []

    def share(block_at, role, to):
        copy = remote(gathered.at[block_at], gathered.at[block_at], x_send.at[role], x_recv.at[role], dp=to)
        copy.start()
        shared.append(copy)
        return copy

    for copy in swaps:
        copy.wait_recv()
    owed += swaps
    to_x = [share(g, 1 + o, x_ahead[o]) for o in range(X - 1)]

    def relay(at):
        pass_on(at).start()

    def pass_on(at):
        return pltpu.make_async_copy(gathered.at[at], gathered_out.at[at], m_sem.at[at])


    for copy in loads_w:
        copy.wait()
    for copy in sent:
        copy.wait_recv()
    owed += sent
    found = jnp.dot(select, in_t[...].reshape(holders * WIDE, block), preferred_element_type=f32)
    emb[spot(t)] = found.astype(bf16)

    def project_in(at, k):
        proj[...] += jnp.dot(emb[at], weight[k], preferred_element_type=f32)
        raw[...] += lax.dot_general(emb[at], narrow[k], (((1,), (1,)), ((), ())), preferred_element_type=f32)

    residual = []

    def send_raw():
        for o, d in enumerate(others_t):
            residual.append(remote(out_r.at[d], in_r.at[t], r_send.at[o], r_recv.at[o], tensor=d))
            residual[-1].start()
        in_r[t] = out_r[t]

    owed += gather_blocks(emb, t, e_send, e_recv, project_in, send_raw)
    to_beside = share(g, 0, beside)
    sizes = (weight.shape[2] // heads, head_size, state_size)
    for h in range(heads):
        mix(h, proj, raw, bias, log_rate, *sizes, key, query, xin, xrow, decay)

    def look(p, carry):
        old_state(p).wait()
        readout(p, per, heads, steps, query, state, read)
        return carry

    lax.fori_loop(0, chunks, look, 0)
    for h in range(heads):
        close(h, steps, proj, skip, ngain, *sizes, xin, xrow, decay, read, mixed)

    load_oweight.wait()
    rows_in = mixed[...]

    def partial_of(yy, zz, cc):
        at = place(yy, zz, cc) * block
        return jnp.dot(rows_in, oweight[:, pl.ds(pl.multiple_of(at, block), block)], preferred_element_type=f32)

    to_core = []
    for n in range(2):
        for zz in range(Z // 2):
            for yy in range(2):
                out_c[n, zz, yy] = partial_of(yy, n * (Z // 2) + zz, 1 - c).astype(bf16)
        to_core.append(remote(out_c.at[n], in_c.at[n], c_send.at[n], c_recv.at[n], tensor=other))
        to_core[-1].start()
    for zz in range(Z):
        for yy in range(2):
            kept[zz, yy] = partial_of(yy, zz, c)
    cut = rows // 2
    for n in range(2):
        to_core[n].wait_recv()
        for zz in range(n * (Z // 2), (n + 1) * (Z // 2)):
            for yy in range(2):
                total = kept[zz, yy] + in_c[n, zz % (Z // 2), yy].astype(f32)
                kept[zz, yy] = total
                out_z[zz, yy] = total[:cut].astype(bf16)
                out_yb[yy, zz] = total[cut:].astype(bf16)
    to_yb = remote(out_yb.at[1 - y], in_yb, y_send.at[0], y_recv.at[0], tensor=across)
    to_yb.start()
    to_z = {}
    for o in (1, 0, 2):
        to_z[o] = remote(out_z.at[ahead[o]], in_z.at[o], z_send.at[o], z_recv.at[o], tensor=place(y, ahead[o], c))
        to_z[o].start()

    def move_on(p, carry):
        update(p, per, heads, steps, key, state, decay, xrow)
        fresh_state(p).start()
        return carry

    lax.fori_loop(0, chunks // 2, move_on, 0)
    to_beside.wait_recv()
    passed = [share(beside, X + o, x_ahead[o]) for o in range(X - 1)]
    relay(g)
    to_yb.wait_recv()
    for zz in range(Z):
        total = kept[zz, y, cut:] + in_yb[zz].astype(f32)
        slab_b[zz] = total
        out_zb[zz] = total.astype(bf16)
    to_zb = {}
    for o in (1, 0, 2):
        to_zb[o] = remote(
            out_zb.at[ahead[o]], in_zb.at[o], z_send.at[3 + o], z_recv.at[3 + o], tensor=place(y, ahead[o], c)
        )
        to_zb[o].start()
    total = kept[z, :, :cut]
    for o in (0, 2, 1):
        to_z[o].wait_recv()
        total = total + in_z[o].astype(f32)
    slab[...] = total
    out_y[...] = slab[1 - y].astype(bf16)
    to_y = remote(out_y, in_y, y_send.at[1], y_recv.at[1], tensor=across)
    to_y.start()
    lax.fori_loop(chunks // 2, chunks, move_on, 0)
    relay(beside)
    for o in range(X - 1):
        to_x[o].wait_recv()
        relay(x_behind[o])
    for copy in residual:
        copy.wait_recv()
    owed += residual
    embedded = jnp.dot(select, in_r[...].reshape(holders * WIDE, block), preferred_element_type=f32)
    total = slab_b[z]
    for o in (0, 2, 1):
        to_zb[o].wait_recv()
        total = total + in_zb[o].astype(f32)
    here = spot(t)
    whole[here, cut:] = (embedded[cut:] + total).astype(bf16)
    to_y.wait_recv()
    whole[here, :cut] = (embedded[:cut] + (slab[y] + in_y[...].astype(f32))).astype(bf16)
    stream[...] = whole[here].astype(f32).reshape(stream.shape).astype(bf16)
    owed += to_core + list(to_z.values()) + list(to_zb.values()) + [to_yb, to_y]

    def settle():
        for copy in owed:
            copy.wait_send()
        for p in range(chunks):
            fresh_state(p).wait()

    squares = [jnp.zeros((rows, block), f32)]

    def square(at, position):
        wide = whole[at].astype(f32)
        squares[0] = squares[0] + wide * wide

    spread = gather_blocks(whole, t, g_send, g_recv, square, settle)
    for o in range(X - 1):
        passed[o].wait_recv()
        relay(x_behind[o] + 1 - 2 * low)
    normalize(whole, next_gain, normed, squares[0])
    for copy in shared + spread:
        copy.wait_send()
    for at in range(groups):
        pass_on(at).wait()


def fused(ids, table, trainer, gain, weight, dtw, bias, log_rate, skip, ngain, state, oweight, next_gain, head_map,
          groups, holders):
    row_count, heads, state_size, head_size = state.shape
    steps = ids.shape[0]
    rows = steps * ids.shape[1]
    vocab, width = table.shape
    block = width // holders
    trows = trainer.shape[0]
    units = heads * head_size
    cut = rows // 2
    columns = weight.shape[1]
    bf16, f32, dma = jnp.bfloat16, jnp.float32, pltpu.SemaphoreType.DMA
    vmem, anywhere = pl.BlockSpec(memory_space=pltpu.VMEM), pl.BlockSpec(memory_space=pl.ANY)
    smem = pl.BlockSpec(memory_space=pltpu.SMEM)
    buffers = [
        ((vocab, width), bf16),
        ((groups, holders, trows, block), bf16),
        (trainer.shape, f32),
        ((holders, block, columns), bf16),
        (state.shape, f32),
        (oweight.shape, bf16),
        ((groups, 8, rows), jnp.int32),
        ((groups, 2 * SLOTS, width // 2), bf16),
        ((groups, 2 * SLOTS, width // 2), bf16),
        ((holders, WIDE, block), bf16),
        ((holders, WIDE, block), bf16),
        ((holders, WIDE, block), bf16),
        ((holders, WIDE, block), bf16),
        ((holders, rows, block), bf16),
        ((holders, rows, block), bf16),
        ((holders, trows, block), bf16),
        ((rows, columns), f32),
        ((holders, 16, block), bf16),
        ((rows, 16), f32),
        ((heads, state_size, rows), f32),
        ((heads, state_size, rows), f32),
        ((heads, rows, head_size), f32),
        ((heads, rows, head_size), f32),
        ((heads, rows, head_size), f32),
        ((heads, rows, head_size), f32),
        ((rows, units), bf16),
        ((2, Z // 2, 2, rows, block), bf16),
        ((2, Z // 2, 2, rows, block), bf16),
        ((Z, 2, rows, block), f32),
        ((Z, 2, cut, block), bf16),
        ((Z - 1, 2, cut, block), bf16),
        ((2, cut, block), f32),
        ((Z, cut, block), f32),
        ((cut, block), bf16),
        ((cut, block), bf16),
        ((2, Z, cut, block), bf16),
        ((Z, cut, block), bf16),
        ((Z, cut, block), bf16),
        ((Z - 1, cut, block), bf16),
    ]
    semaphores = [3, holders, 8, 8, groups]
    for count in (groups - 1, groups - 1, holders - 1, holders - 1, holders - 1, holders - 1, 2 * X - 1):
        semaphores += [count, count]
    for count in (2, 2 * (Z - 1), 2, holders - 1):
        semaphores += [count, count]
    return pl.pallas_call(
        functools.partial(fused_kernel, heads),
        out_shape=(
            jax.ShapeDtypeStruct(state.shape, f32),
            jax.ShapeDtypeStruct((row_count, steps, block), bf16),
            jax.ShapeDtypeStruct((row_count, steps, width), bf16),
            jax.ShapeDtypeStruct((groups, holders, trows, block), bf16),
            jax.ShapeDtypeStruct((units, units), bf16),
            jax.ShapeDtypeStruct((1, 1), jnp.int32),
        ),
        in_specs=[vmem, anywhere, anywhere, vmem, anywhere, vmem, smem, smem, smem, vmem, anywhere, anywhere, vmem, vmem],
        out_specs=(anywhere, vmem, vmem, anywhere, vmem, smem),
        scratch_shapes=[pltpu.VMEM(*buffer) for buffer in buffers] + [dma((count,)) for count in semaphores],
        compiler_params=pltpu.CompilerParams(
            collective_id=0, has_side_effects=True, vmem_limit_bytes=60 * 2**20
        ),
        name="fused",
    )(ids, table, trainer, gain, weight, dtw, bias, log_rate, skip, ngain, state, oweight, next_gain, head_map)


def per_device(
    token_ids,
    embed_table,
    in_gain,
    in_weight,
    dt_weight,
    dt_bias,
    a_log,
    d_skip,
    norm_gain,
    out_weight,
    next_gain,
    ssm_state,
    trainer_weight,
    head_map,
):
    row_count, step_count = token_ids.shape
    width = embed_table.shape[1]
    holders = lax.axis_size("tensor")
    groups = lax.axis_size("dp")
    rows = row_count * step_count
    state = ssm_state.swapaxes(2, 3)
    gain, ngain, ngain_next = in_gain.reshape(1, -1), norm_gain.reshape(1, -1), next_gain.reshape(1, -1)
    mix = (in_weight, dt_weight.T, dt_bias, a_log, d_skip, ngain, state)
    now, stream, normed, gathered, swap, need = fused(
        token_ids.T, embed_table, trainer_weight, gain, *mix, out_weight, ngain_next, head_map, groups, holders
    )

    def again(carry):
        todo = carry[0]

        def more(inner):
            done, held = inner
            return done + SLOTS, held + lookup(token_ids.T, embed_table, groups, holders, jnp.full((8, 128), done, jnp.int32))

        empty = jnp.zeros((holders, rows, width // holders), jnp.bfloat16)
        _, emb = lax.while_loop(lambda inner: inner[0] < todo, more, (jnp.int32(0), empty))
        now, mixed = mixer(emb, gain, *mix)
        stream, normed = project(mixed, out_weight, emb, ngain_next, step_count)
        return jnp.int32(0), now, stream, normed

    _, now, stream, normed = lax.while_loop(
        lambda carry: carry[0] > 0, again, (need.reshape(()), now, stream, normed)
    )
    relaid = lax.dot_general(
        swap, gathered.reshape(width, swap.shape[1]), (((1,), (1,)), ((), ())), preferred_element_type=jnp.float32
    )
    return (
        now.swapaxes(2, 3),
        stream,
        normed,
        relaid,
    )


def solution(mesh):
    placed = (
        P("dp", None),
        P(("dp", "tensor"), None),
        P(),
        P(None, "tensor"),
        P(None, "tensor"),
        P("tensor"),
        P("tensor"),
        P("tensor"),
        P("tensor"),
        P("tensor", None),
        P(),
        P("dp", "tensor", None, None),
        P(("dp", "tensor"), None),
        P("tensor", None),
    )
    return jax.shard_map(
        per_device,
        mesh=mesh,
        in_specs=placed,
        out_specs=(
            P("dp", "tensor", None, None),
            P("dp", None, "tensor"),
            P("dp", None, None),
            P("tensor", None),
        ),
        check_vma=False,
    )
```
